32 devices in a mesh: gx: 4 (over x, core), gy: 8 (over z, y).
Axes of the slice: x: 2, y: 2, z: 4, core: 2. Of those that a mesh axis runs over, the one named last changes fastest.
Arguments:
- fields_old: float32 [4, 8, 8, 5, 16, 256], P('gx', 'gy'), may hold values from -6 to 6
- coeff_old: float32 [4, 8, 8, 5], P('gx', 'gy'), may hold values from 0.1 to 4
- new_place: int32 [4, 8, 8], P('gx', 'gy'), may hold values from 0 to 255, as said below
- cf_mask: int32 [4, 8, 3, 8], P('gx', 'gy'), may hold values 0 or 1
Outputs:
- smoothed: float32 [4, 8, 8, 5, 16, 256], P('gx', 'gy')
- registers: float32 [4, 8, 5, 6, 256], P('gx', 'gy')
The draws below stay inside these ranges and needn't reach their ends.
Inputs may be any that keep to these rules, and one draw needn't show every extreme that they name: `new_place`: owners are ordered by row, then column. Each box's new owner is its old owner or the owner just before or after it in that order; at most 2 boxes go from one owner to each of these two neighbours, exactly 2 between the first two owners in every draw; every new slot receives exactly one box.
All inputs are finite; a program needn't handle non-finite values. No bound on the sum of `cf_mask` on one device may be relied on, other than what follows from the above.
Results may differ from the reference program's by a relative error of at most 0.00002.
Values sent between devices are 32-bit elements; how exact they have to be, the bound alone decides.
No kernel may reach another device: no remote copies, remote signals or barrier semaphores. Data moves between devices by JAX's collectives and lax.ppermute only.
A program may use at most 64 MiB of HBM per device.

```python
import math
import jax
import jax.numpy as jnp
from jax import lax

NC = 5
E = 16
BZ = 8
MOVE = 2
ROWS = 4
COLS = 8
NX = 64
NY = 128
NZ = 128
N_GX = 4
N_GY = 8


def draw_new_place(key, part):
    key = jax.random.fold_in(key, 11)
    owners = N_GX * N_GY
    key_cross, key_old, key_new = jax.random.split(key, 3)
    cross = jax.random.randint(key_cross, (owners,), 0, MOVE + 1).astype(jnp.int32)
    cross = cross.at[0].set(MOVE).at[owners - 1].set(0)
    left = jnp.concatenate([jnp.zeros((1,), jnp.int32), cross[:-1]])
    old_order = jax.vmap(lambda sub: jax.random.permutation(sub, BZ))(jax.random.split(key_old, owners)).astype(jnp.int32)
    new_order = jax.vmap(lambda sub: jax.random.permutation(sub, BZ))(jax.random.split(key_new, owners)).astype(jnp.int32)
    ranks = jnp.broadcast_to(jnp.arange(BZ, dtype=jnp.int32)[None, :], (owners, BZ))
    owner_ids = jnp.broadcast_to(jnp.arange(owners, dtype=jnp.int32)[:, None], (owners, BZ))
    go_left = ranks < left[:, None]
    go_right = ranks >= BZ - cross[:, None]
    previous = jnp.roll(new_order, 1, axis=0)
    following = jnp.roll(new_order, -1, axis=0)
    slot_left = jnp.take_along_axis(previous, jnp.clip(BZ - left[:, None] + ranks, 0, BZ - 1), axis=1)
    slot_right = jnp.take_along_axis(following, jnp.clip(ranks - (BZ - cross[:, None]), 0, BZ - 1), axis=1)
    dest_owner = jnp.where(go_left, owner_ids - 1, jnp.where(go_right, owner_ids + 1, owner_ids))
    dest_slot = jnp.where(go_left, slot_left, jnp.where(go_right, slot_right, new_order))
    values = dest_owner * BZ + dest_slot
    placed = jnp.zeros((owners, BZ), jnp.int32).at[owner_ids, old_order].set(values)
    return placed.reshape(N_GX, N_GY, BZ)


def with_ends(drawn, stream_key, least, largest):
    dims = drawn.shape
    place = [jax.random.randint(jax.random.fold_in(stream_key, axis), (), 0, dims[axis]) for axis in range(len(dims))]
    drawn = drawn.at[tuple(place)].set(least)
    longest = dims.index(max(dims))
    place[longest] = (place[longest] + 1) % dims[longest]
    return drawn.at[tuple(place)].set(largest)


def block_levels(own_key, dims, cuts, smallest, top_value):
    level, own = 1.0, jax.random.fold_in(own_key, 6)
    for dim, shards_of in cuts:
        draws = jnp.exp(jax.random.uniform(jax.random.fold_in(own, dim), (shards_of,), jnp.float32, smallest / len(cuts), top_value / len(cuts)))
        level = level * jnp.repeat(draws, dims[dim] // shards_of).reshape([-1 if axis == dim else 1 for axis in range(len(dims))])
    return level


def centred(stream_key, extent, spread, limit, cuts=(), kind=jnp.bfloat16):
    result = jax.random.normal(stream_key, extent, jnp.float32) * spread
    if len(cuts) > 0:
        result = block_levels(stream_key, extent, cuts, -0.22, 0.18) * result
    return jnp.clip(result, min=-limit, max=limit).astype(kind)


def setup_inputs(seed: int = 0) -> dict:
    arg_keys = jax.random.split(jax.random.key(seed), 5)
    return {
        "fields_old": centred(arg_keys[0], (ROWS, COLS, BZ, NC, E, E * E), 1.0, 6.0, ((0, 4), (1, 8)), jnp.float32),
        "coeff_old": jnp.clip(jnp.exp(math.log(4.0) - 3.6888794 * jax.random.uniform(arg_keys[1], (ROWS, COLS, BZ, NC), jnp.float32) ** block_levels(arg_keys[1], (ROWS, COLS, BZ, NC), ((0, 4), (1, 8)), -0.2, 0.2)), 0.1, 4.0),
        "new_place": draw_new_place(jax.random.fold_in(arg_keys[4], 71), 0),
        "cf_mask": with_ends((jax.random.randint(arg_keys[3], (ROWS, COLS, 3, BZ), 0, 2) < 1).astype(jnp.int32), jax.random.fold_in(arg_keys[3], 1), 0, 1),
    }


def nsum(field):
    padded = jnp.pad(field, 1)
    total = padded[:-2, 1:-1, 1:-1] + padded[2:, 1:-1, 1:-1]
    total = total + padded[1:-1, :-2, 1:-1] + padded[1:-1, 2:, 1:-1]
    total = total + padded[1:-1, 1:-1, :-2] + padded[1:-1, 1:-1, 2:]
    return total, padded


def reference(fields_old, coeff_old, new_place, cf_mask):
    count = N_GX * N_GY * BZ
    target = new_place.reshape(-1).astype(jnp.int32)
    parity_x = (jnp.arange(N_GX, dtype=jnp.int32) % 2)[:, None, None]
    parity_y = (jnp.arange(N_GY, dtype=jnp.int32) % 2)[None, :, None]
    flags = cf_mask.astype(jnp.float32)
    mask_x = jnp.repeat(jnp.repeat(flags[:, :, 0, :], E, 1), E, 2)
    mask_y = jnp.repeat(jnp.repeat(flags[:, :, 1, :], E, 0), E, 2)
    mask_low = jnp.repeat(jnp.repeat(flags[:, :, 2, 0::2], E, 0), E, 1)
    mask_high = jnp.repeat(jnp.repeat(flags[:, :, 2, 1::2], E, 0), E, 1)

    def component(index):
        boxes = lax.dynamic_index_in_dim(fields_old, index, 3, keepdims=False).reshape(count, E, E * E)
        moved = jnp.zeros_like(boxes).at[target].set(boxes)
        residual = moved.reshape(N_GX, N_GY, BZ, E, E, E).transpose(0, 3, 1, 4, 2, 5).reshape(NX, NY, NZ)
        rates = lax.dynamic_index_in_dim(coeff_old, index, 3, keepdims=False).reshape(count)
        rates = jnp.zeros_like(rates).at[target].set(rates).reshape(N_GX, N_GY, BZ)
        coeff = jnp.repeat(jnp.repeat(jnp.repeat(rates, E, 0), E, 1), E, 2)
        total, padded = nsum(residual)
        first = (residual + coeff * total) / (1.0 + 6.0 * coeff)
        total, padded = nsum(first)
        smoothed = (residual + coeff * total) / (1.0 + 6.0 * coeff)
        smoothed = smoothed.reshape(N_GX, E, N_GY, E, BZ, E).transpose(0, 2, 4, 1, 3, 5).reshape(N_GX, N_GY, BZ, E, E * E)

        low = (coeff * (padded[:-2, 1:-1, 1:-1] - first)).reshape(N_GX, E, NY, NZ)[:, 0]
        high = (coeff * (padded[2:, 1:-1, 1:-1] - first)).reshape(N_GX, E, NY, NZ)[:, E - 1]
        flux_x = jnp.where(parity_x == 0, low, high) * mask_x
        flux_x = flux_x.reshape(N_GX, NY // 2, 2, NZ // 2, 2).sum(axis=(2, 4)) * 0.25
        reg_x = flux_x.reshape(N_GX // 2, 2, N_GY // 2, E, BZ // 2, E).transpose(0, 2, 4, 1, 3, 5)

        low = (coeff * (padded[1:-1, :-2, 1:-1] - first)).reshape(NX, N_GY, E, NZ)[:, :, 0]
        high = (coeff * (padded[1:-1, 2:, 1:-1] - first)).reshape(NX, N_GY, E, NZ)[:, :, E - 1]
        flux_y = jnp.where(parity_y == 0, low, high) * mask_y
        flux_y = flux_y.reshape(NX // 2, 2, N_GY, NZ // 2, 2).sum(axis=(1, 4)) * 0.25
        reg_y = flux_y.reshape(N_GX // 2, E, N_GY // 2, 2, BZ // 2, E).transpose(0, 2, 4, 3, 1, 5)

        low = (coeff * (padded[1:-1, 1:-1, :-2] - first)).reshape(NX, NY, BZ // 2, 2 * E)[..., 0] * mask_low
        high = (coeff * (padded[1:-1, 1:-1, 2:] - first)).reshape(NX, NY, BZ // 2, 2 * E)[..., 2 * E - 1] * mask_high
        low = low.reshape(NX // 2, 2, NY // 2, 2, BZ // 2).sum(axis=(1, 3)) * 0.25
        high = high.reshape(NX // 2, 2, NY // 2, 2, BZ // 2).sum(axis=(1, 3)) * 0.25
        reg_low = low.reshape(N_GX // 2, E, N_GY // 2, E, BZ // 2).transpose(0, 2, 4, 1, 3)
        reg_high = high.reshape(N_GX // 2, E, N_GY // 2, E, BZ // 2).transpose(0, 2, 4, 1, 3)
        faces = jnp.stack([reg_x[:, :, :, 0], reg_x[:, :, :, 1], reg_y[:, :, :, 0], reg_y[:, :, :, 1], reg_low, reg_high], axis=3)
        return smoothed, faces

    smoothed, faces = lax.map(component, jnp.arange(NC, dtype=jnp.int32))
    smoothed = smoothed.transpose(1, 2, 3, 0, 4, 5)
    faces = faces.reshape(NC, N_GX // 2, N_GY // 2, 2, 2, 6, E * E).transpose(1, 3, 2, 4, 0, 5, 6)
    return smoothed, faces.reshape(N_GX, N_GY, NC, 6, E * E)
```

```python
import functools

import jax
import jax.numpy as jnp
from jax import lax
from jax.experimental import pallas as pl
from jax.experimental.pallas import tpu as pltpu
from jax.sharding import PartitionSpec as P

NC = 5
E = 16
BZ = 8
MOVE = 2
L = 128
F32 = jnp.float32
I32 = jnp.int32

PLANE = NC * BZ
FACE = 4 * PLANE
BOXROWS = NC * E
LABELS = MOVE * BOXROWS + MOVE * NC
PARCEL = 176

VM = pltpu.VMEM
SM = pltpu.SMEM


def call(kernel, ins, outs, scratch=(), aliases=None, flops=1000, **kw):
    given, in_specs = [], []
    for array, space in ins:
        if space == "vmem":
            given.append(pltpu.with_memory_space_constraint(array, VM))
            in_specs.append(pl.BlockSpec(memory_space=VM))
        elif space == "smem":
            given.append(array)
            in_specs.append(pl.BlockSpec(memory_space=SM))
        else:
            given.append(array)
            in_specs.append(pl.BlockSpec(memory_space=pl.ANY))
    shapes, out_specs = [], []
    for shape, space in outs:
        if space == "vmem":
            shapes.append(VM(shape, F32))
            out_specs.append(pl.BlockSpec(memory_space=VM))
        else:
            shapes.append(jax.ShapeDtypeStruct(shape, F32))
            out_specs.append(pl.BlockSpec(memory_space=VM))
    return pl.pallas_call(
        kernel,
        out_shape=shapes,
        in_specs=in_specs,
        out_specs=out_specs,
        scratch_shapes=list(scratch),
        input_output_aliases=aliases or {},
        cost_estimate=pl.CostEstimate(flops=flops, bytes_accessed=0, transcendentals=0),
        compiler_params=pltpu.CompilerParams(vmem_limit_bytes=24 * 1024 * 1024),
        **kw,
    )(*given)


def lanes():
    return lax.broadcasted_iota(I32, (BZ, L), 1)


def subs():
    return lax.broadcasted_iota(I32, (BZ, L), 0)


def rl(x, shift):
    shift %= L
    return x if shift == 0 else pltpu.roll(x, shift, 1)


def rs(x, shift):
    shift %= BZ
    return x if shift == 0 else pltpu.roll(x, shift, 0)


def pick_lanes(x, index):
    return jnp.take_along_axis(x, index, axis=1)


def place_of(mesh_shape):
    gx = lax.axis_index("gx")
    gy = lax.axis_index("gy")
    return gx, gy, gx * mesh_shape[1] + gy


def pack_kernel(shape, place_hbm, coeff_hbm, fields_hbm, boxes, even, odd, place, coeff, sem):
    big = pltpu.make_async_copy(fields_hbm.at[0, 0], boxes, sem.at[0])
    small = pltpu.make_async_copy(place_hbm, place, sem.at[1])
    other = pltpu.make_async_copy(coeff_hbm, coeff, sem.at[2])
    big.start()
    small.start()
    other.start()
    _, _, me = place_of(shape)
    ahead = 1 - 2 * (me % 2)
    small.wait()
    other.wait()
    chosen = []
    for out, owner in ((even, me + ahead), (odd, me - ahead)):
        count = jnp.int32(0)
        sources = [jnp.int32(0)] * MOVE
        labels = [jnp.int32(0)] * MOVE
        for s in range(BZ):
            value = place[0, 0, s]
            hit = value // BZ == owner
            for k in range(MOVE):
                taken = hit & (count == k)
                sources[k] = jnp.where(taken, s, sources[k])
                labels[k] = jnp.where(taken, value % BZ + 1, labels[k])
            count = count + hit.astype(I32)
        chosen.append(sources)
        out[LABELS + MOVE : PARCEL, :] = jnp.zeros((PARCEL - LABELS - MOVE, 2 * L), F32)
        for k in range(MOVE):
            out[LABELS + k : LABELS + k + 1, :] = jnp.full((1, 2 * L), labels[k].astype(F32), F32)
            for c in range(NC):
                row = MOVE * BOXROWS + k * NC + c
                out[row : row + 1, :] = jnp.full((1, 2 * L), coeff[0, 0, sources[k], c], F32)
    big.wait()
    for out, sources in zip((even, odd), chosen):
        for k in range(MOVE):
            for c in range(NC):
                row = (k * NC + c) * E
                out[row : row + E, :] = boxes[sources[k], c]


def stay_kernel(shape, place, coeff, mask, boxes, moved, rates, masks):
    _, _, me = place_of(shape)
    for s in range(BZ):
        value = place[0, 0, s]
        slot = value % BZ

        @pl.when(value // BZ == me)
        def _():
            for c in range(NC):
                for h in range(2):
                    moved[h, pl.ds(c * E * BZ + slot, E, stride=BZ), :] = boxes[s, c, :, h * L : h * L + L]
                rates[pl.ds(c * BZ + slot, 1), :] = jnp.full((1, L), coeff[0, 0, s, c], F32)

    for d in range(3):
        for s in range(BZ):
            masks[d * BZ + s : d * BZ + s + 1, :] = jnp.full((1, L), mask[0, 0, d, s].astype(F32), F32)


def arrivals(even, odd):
    sub = subs()
    found = []
    for parcel in (even, odd):
        for k in range(MOVE):
            label = parcel[LABELS + k : LABELS + k + 1, :L]
            found.append((parcel, k, label == (sub + 1).astype(F32)))
    return found


def merged(found, moved, c, x, h):
    row = (c * E + x) * BZ
    tile = moved[h, row : row + BZ, :]
    for parcel, k, hit in found:
        at = (k * NC + c) * E + x
        tile = jnp.where(hit, parcel[at : at + 1, h * L : h * L + L], tile)
    return tile


def plane_row(layer, h, c):
    return ((layer * 2 + h) * NC + c) * BZ


def xsend_kernel(shape, even, odd, moved, rates, core, link, all_rates):
    gx, _, _ = place_of(shape)
    first = gx % 2 == 0
    found = arrivals(even, odd)
    for c in range(NC):
        tile = rates[c * BZ : c * BZ + BZ, :]
        for parcel, k, hit in found:
            at = MOVE * BOXROWS + k * NC + c
            tile = jnp.where(hit, parcel[at : at + 1, :L], tile)
        all_rates[c * BZ : c * BZ + BZ, :] = tile
        core[FACE + c * BZ : FACE + c * BZ + BZ, :] = tile
        link[FACE + c * BZ : FACE + c * BZ + BZ, :] = tile
        for layer in range(2):
            for h in range(2):
                low = merged(found, moved, c, layer, h)
                high = merged(found, moved, c, E - 1 - layer, h)
                at = plane_row(layer, h, c)
                core[at : at + BZ, :] = jnp.where(first, high, low)
                link[at : at + BZ, :] = jnp.where(first, low, high)


def merge_kernel(shape, even, odd, moved, out, near, far):
    _, gy, _ = place_of(shape)
    first = gy % 2 == 0
    found = arrivals(even, odd)
    lane = lanes()
    for c in range(NC):
        low = [[None, None], [None, None]]
        high = [[None, None], [None, None]]
        for x in range(E):
            row = (c * E + x) * BZ
            at = L // 8 * (x % 8)
            here = lane // E == x % 8
            half = x // 8
            for h in range(2):
                tile = merged(found, moved, c, x, h)
                out[h, row : row + BZ, :] = tile
                for layer in range(2):
                    keep, start = ((low, E * layer) if h == 0 else (high, L - E - E * layer))
                    strip = rl(tile, at - start)
                    old = keep[layer][half]
                    keep[layer][half] = strip if old is None else jnp.where(here, strip, old)
        for layer in range(2):
            for h in range(2):
                at = plane_row(layer, h, c)
                near[at : at + BZ, :] = jnp.where(first, high[layer][h], low[layer][h])
                far[at : at + BZ, :] = jnp.where(first, low[layer][h], high[layer][h])


def ends(shape):
    gx, gy, _ = place_of(shape)
    x_first, y_first = gx % 2 == 0, gy % 2 == 0
    link_ok = jnp.where(x_first, gx > 0, gx < shape[0] - 1)
    far_ok = jnp.where(y_first, gy > 0, gy < shape[1] - 1)
    return x_first, y_first, link_ok, far_ok


def ysend_kernel(shape, core, link, rates, near, far, near_out, far_out):
    x_first, y_first, link_ok, _ = ends(shape)
    lane = lanes()
    near_out[:FACE, :] = near[...]
    far_out[:FACE, :] = far[...]
    for c in range(NC):
        lines = []
        for h in range(2):
            at = plane_row(0, h, c)
            a = core[at : at + BZ, :]
            b = jnp.where(link_ok, link[at : at + BZ, :], 0.0)
            lines.append((jnp.where(x_first, b, a), jnp.where(x_first, a, b)))
        rate = rates[c * BZ : c * BZ + BZ, :]
        bottom = jnp.where(lane < E, lines[0][0], rl(lines[0][1], E))
        top = jnp.where(lane < E, rl(lines[1][0], E), rl(lines[1][1], 2 * E))
        bottom = jnp.where(lane < 2 * E, bottom, rate)
        top = jnp.where(lane < 2 * E, top, rate)
        at = FACE + c * BZ
        near_out[at : at + BZ, :] = jnp.where(y_first, top, bottom)
        far_out[at : at + BZ, :] = jnp.where(y_first, bottom, top)


def z_parts(x, lane, sub, swap):
    z = lane % E
    down = jnp.where(sub == 0, 0.0, rs(x, 1))
    up = jnp.where(sub == BZ - 1, 0.0, rs(x, -1))
    ends_ = pick_lanes(jnp.where(z == E - 1, down, up), swap)
    return jnp.where(z == 0, ends_, rl(x, 1)) + jnp.where(z == E - 1, ends_, rl(x, -1))


def swap_index(lane):
    z = lane % E
    return jnp.where(z == 0, lane + E - 1, jnp.where(z == E - 1, lane - E + 1, lane))


def inner(pair, lane, sub, swap):
    a, b = pair
    a1, b1, a2, b2 = rl(a, E), rl(b, E), rl(a, -E), rl(b, -E)
    low, high = lane < E, lane >= L - E
    first = jnp.where(low, 0.0, a1) + jnp.where(high, b2, a2) + z_parts(a, lane, sub, swap)
    second = jnp.where(low, a1, b1) + jnp.where(high, 0.0, b2) + z_parts(b, lane, sub, swap)
    return first, second


def pair_at(ref, layer, c):
    return tuple(ref[plane_row(layer, h, c) : plane_row(layer, h, c) + BZ, :] for h in range(2))


def tile_at(ref, c, x):
    row = (c * E + x) * BZ
    return tuple(ref[h, row : row + BZ, :] for h in range(2))


def sweep_kernel(shape, moved, rates, core, link, core_sent, link_sent, out, core_first, link_first):
    x_first, _, link_ok, _ = ends(shape)
    lane, sub = lanes(), subs()
    swap = swap_index(lane)
    for c in range(NC):
        rate = rates[c * BZ : c * BZ + BZ, :]
        scale = 1.0 / (1.0 + 6.0 * rate)
        ghost = []
        for got, sent, kept, ok in ((core, core_sent, core_first, None), (link, link_sent, link_first, link_ok)):
            g0, g1, own = pair_at(got, 0, c), pair_at(got, 1, c), pair_at(sent, 0, c)
            g_rate = got[FACE + c * BZ : FACE + c * BZ + BZ, :]
            if ok is not None:
                g0, g1 = (tuple(jnp.where(ok, t, 0.0) for t in g) for g in (g0, g1))
                g_rate = jnp.where(ok, g_rate, 0.0)
            ghost.append(g0)
            g_scale = 1.0 / (1.0 + 6.0 * g_rate)
            sums = inner(g0, lane, sub, swap)
            for h in range(2):
                value = (g0[h] + g_rate * (sums[h] + g1[h] + own[h])) * g_scale
                if ok is not None:
                    value = jnp.where(ok, value, 0.0)
                row = (h * NC + c) * BZ
                kept[row : row + BZ, :] = value
        low = [jnp.where(x_first, b, a) for a, b in zip(*ghost)]
        high = [jnp.where(x_first, a, b) for a, b in zip(*ghost)]
        for x in range(E):
            here = tile_at(moved, c, x)
            before = low if x == 0 else tile_at(moved, c, x - 1)
            after = high if x == E - 1 else tile_at(moved, c, x + 1)
            sums = inner(here, lane, sub, swap)
            row = (c * E + x) * BZ
            for h in range(2):
                out[h, row : row + BZ, :] = (here[h] + rate * (sums[h] + before[h] + after[h])) * scale


def coarse_plane(pair, parity, lane, sub):
    sums = []
    for t in pair:
        t = t + rl(t, -1)
        sums.append(t + rl(t, -E))
    source = (lane // E % 4) * (2 * E) + 2 * (lane % 8)
    out = jnp.where(lane < L // 2, pick_lanes(sums[0], source), pick_lanes(sums[1], source))
    return jnp.where(lane % E // 8 == sub % 2, 0.25 * out, 0.0)


def flux_kernel(
    shape, partial, moved_rates, masks, core_first, link_first, near, far, near_sent, far_sent,
    first, x_core, x_link, y_near, y_far, kept, sent,
):
    x_first, y_first, link_ok, far_ok = ends(shape)
    gx, gy, _ = place_of(shape)
    par_x, par_y = gx % 2, gy % 2
    lane, sub = lanes(), subs()
    swap = swap_index(lane)
    upper = sub % 2 == 1
    z = lane % E
    low_lane, high_lane = lane < E, lane >= L - E
    for c in range(NC):
        rate = moved_rates[c * BZ : c * BZ + BZ, :]
        scale = 1.0 / (1.0 + 6.0 * rate)
        weight = rate * scale
        lines, ghost_r, ghost_f = [], [], []
        for got, sent_, kept_, ok in ((near, near_sent, y_near, None), (far, far_sent, y_far, far_ok)):
            g0, g1, own = pair_at(got, 0, c), pair_at(got, 1, c), pair_at(sent_, 0, c)
            extra = got[FACE + c * BZ : FACE + c * BZ + BZ, :]
            if ok is not None:
                g0, g1 = (tuple(jnp.where(ok, t, 0.0) for t in g) for g in (g0, g1))
                extra = jnp.where(ok, extra, 0.0)
            g_rate = jnp.where(lane < L // 2, rl(extra, L // 2), extra)
            g_scale = 1.0 / (1.0 + 6.0 * g_rate)
            sums = inner(g0, lane, sub, swap)
            line = (jnp.where(low_lane, extra, 0.0), jnp.where(high_lane, rl(extra, L - 2 * E), 0.0))
            first_g = []
            for h in range(2):
                value = (g0[h] + g_rate * (sums[h] + line[h] + g1[h] + own[h])) * g_scale
                if ok is not None:
                    value = jnp.where(ok, value, 0.0)
                row = (h * NC + c) * BZ
                kept_[row : row + BZ, :] = value
                first_g.append(value)
            lines.append(extra)
            ghost_r.append(g0)
            ghost_f.append(first_g)
        own, own1 = pair_at(far_sent, 0, c), pair_at(far_sent, 1, c)
        extra = far_sent[FACE + c * BZ : FACE + c * BZ + BZ, :]
        sums = inner(own, lane, sub, swap)
        line = (jnp.where(low_lane, extra, 0.0), jnp.where(high_lane, rl(extra, L - 2 * E), 0.0))
        flux_y = []
        for h in range(2):
            value = (own[h] + rate * (sums[h] + line[h] + own1[h] + ghost_r[1][h])) * scale
            flux_y.append(ghost_f[1][h] - value)
        low_r = [jnp.where(y_first, b, a) for a, b in zip(*ghost_r)]
        high_r = [jnp.where(y_first, a, b) for a, b in zip(*ghost_r)]
        low_line = jnp.where(y_first, lines[1], lines[0])
        high_line = jnp.where(y_first, lines[0], lines[1])
        for x in range(E):
            a, b = tile_at(partial, c, x)
            shift = E * (x % 8)
            a = a + weight * jnp.where(low_lane, rl(low_r[x // 8], -shift), 0.0)
            b = b + weight * jnp.where(high_lane, rl(high_r[x // 8], L - E - shift), 0.0)
            row = (c * E + x) * BZ
            first[0, row : row + BZ, :] = a
            first[1, row : row + BZ, :] = b
        planes = []
        for part, kept_, at_low, ok in ((core_first, x_core, ~x_first, None), (link_first, x_link, x_first, link_ok)):
            g_rate = kept_rate(part, c)
            g_weight = g_rate / (1.0 + 6.0 * g_rate)
            bottom = jnp.where(at_low, low_line, rl(low_line, -E))
            top = jnp.where(at_low, rl(high_line, L - E), rl(high_line, L - 2 * E))
            plane = []
            for h, (line_, there) in enumerate(((bottom, low_lane), (top, high_lane))):
                row = (h * NC + c) * BZ
                value = part[row : row + BZ, :] + g_weight * jnp.where(there, line_, 0.0)
                if ok is not None:
                    value = jnp.where(ok, value, 0.0)
                kept_[row : row + BZ, :] = value
                plane.append(value)
            planes.append(plane)
        flux_x = []
        for h in range(2):
            low = first[h, c * E * BZ : c * E * BZ + BZ, :]
            row = (c * E + E - 1) * BZ
            high = first[h, row : row + BZ, :]
            flux_x.append(planes[1][h] - jnp.where(x_first, low, high))
        faces_z = []
        for h in range(2):
            face = None
            for k in range(E // 2):
                row = (c * E + 2 * k) * BZ
                t = first[h, row : row + BZ, :] + first[h, row + BZ : row + 2 * BZ, :]
                down = jnp.where(sub == 0, 0.0, rs(t, 1))
                up = jnp.where(sub == BZ - 1, 0.0, rs(t, -1))
                high = rl(jnp.where(upper, t, down), 1 - E)
                d = high - jnp.where(upper, up, t)
                d = jnp.where(upper, -d, d)
                d = rl(d + rl(d, -E), k)
                face = d if face is None else jnp.where(z == k, d, face)
            faces_z.append(face)
        face_x = coarse_plane(flux_x, par_y, lane, sub) * (rate * masks[0:BZ, :])
        face_y = coarse_plane(flux_y, par_x, lane, sub) * (rate * masks[BZ : 2 * BZ, :])
        y8 = lane % 8
        source = (y8 % 4) * (2 * E) + lane // E
        face_z = jnp.where(y8 < 4, pick_lanes(faces_z[0], source), pick_lanes(faces_z[1], source))
        face_z = jnp.where(z // 8 == par_y, face_z, 0.0) * (0.25 * rate * masks[2 * BZ :, :])
        face_x = face_x + rs(face_x, -1)
        face_y = face_y + rs(face_y, 1)
        for h in range(2):
            sides = jnp.where(upper, jnp.where(par_x == h, face_y, 0.0), jnp.where(par_y == h, face_x, 0.0))
            tops = jnp.where(par_x == h, face_z, 0.0)
            left = sub % 4 < 2
            columns = (
                jnp.where(left, sides, rs(tops, 2)),
                jnp.where(left, rs(sides, -2), tops),
            )
            row = (h * NC + c) * BZ
            kept[row : row + BZ, :] = jnp.where(y_first, columns[0], columns[1])
            sent[row : row + BZ, :] = jnp.where(y_first, columns[1], columns[0])


def kept_rate(part, c):
    return part[2 * PLANE + c * BZ : 2 * PLANE + c * BZ + BZ, :]


def half_kernel(shape, kept, got, mine, sent):
    gx, _, _ = place_of(shape)
    first = gx % 2 == 0
    top = subs() < 4
    for i in range(2 * NC):
        a, b = kept[i * BZ : i * BZ + BZ, :], got[i * BZ : i * BZ + BZ, :]
        rows = (jnp.where(top, a, rs(b, 4)), jnp.where(top, rs(a, 4), b))
        mine[i * BZ : i * BZ + BZ, :] = jnp.where(first, rows[0], rows[1])
        sent[i * BZ : i * BZ + BZ, :] = jnp.where(first, rows[1], rows[0])


def register_kernel(shape, mine, got, out):
    x_first, y_first, _, _ = ends(shape)
    sub = subs()
    for h in range(2):
        for c in range(NC):
            row = (h * NC + c) * BZ
            m, g = mine[row : row + BZ, :], got[row : row + BZ, :]
            a, b = m + rs(m, 4), g + rs(g, 4)
            s = m + g
            ab = a + b
            x0, x1 = jnp.where(x_first, a, b), jnp.where(x_first, b, a)
            y0, y1 = jnp.where(y_first, rs(s, 1), rs(s, 5)), jnp.where(y_first, rs(s, 5), rs(s, 1))
            t = jnp.where(sub == 0, x0, jnp.where(sub == 1, rs(x1, 1), rs(ab, 2)))
            t = jnp.where(sub == 2, y0, jnp.where(sub == 3, rs(y1, 1), t))
            out[0, 0, c, :, h * L : h * L + L] = t[:6]


def smooth_kernel(shape, moved, rates, first, x_core, x_link, y_near, y_far, out, held):
    x_first, y_first, _, _ = ends(shape)
    lane, sub = lanes(), subs()
    swap = swap_index(lane)
    low_lane, high_lane = lane < E, lane >= L - E
    for c in range(NC):
        rate = rates[c * BZ : c * BZ + BZ, :]
        scale = 1.0 / (1.0 + 6.0 * rate)

        def ghosts(a_ref, b_ref, a_first):
            a, b = (tuple(ref[(h * NC + c) * BZ : (h * NC + c + 1) * BZ, :] for h in range(2)) for ref in (a_ref, b_ref))
            low = [jnp.where(a_first, q, p) for p, q in zip(a, b)]
            high = [jnp.where(a_first, p, q) for p, q in zip(a, b)]
            return low, high

        low, high = ghosts(x_core, x_link, x_first)
        low_y, high_y = ghosts(y_near, y_far, y_first)
        for x in range(E):
            here = tile_at(first, c, x)
            before = low if x == 0 else tile_at(first, c, x - 1)
            after = high if x == E - 1 else tile_at(first, c, x + 1)
            sums = inner(here, lane, sub, swap)
            shift = E * (x % 8)
            edge = (
                jnp.where(low_lane, rl(low_y[x // 8], -shift), 0.0),
                jnp.where(high_lane, rl(high_y[x // 8], L - E - shift), 0.0),
            )
            start = tile_at(moved, c, x)
            row = (c * E + x) * BZ
            for h in range(2):
                held[h, row : row + BZ, :] = (start[h] + rate * (sums[h] + before[h] + after[h] + edge[h])) * scale
        for s in range(BZ):
            for h in range(2):
                out[0, 0, s, c, :, h * L : h * L + L] = held[h, pl.ds(c * E * BZ + s, E, stride=BZ), :]


def body(shape, fields_old, coeff_old, new_place, cf_mask):
    rows, columns = shape
    count = rows * columns
    both = ("gx", "gy")

    def swap(array, pairs):
        return lax.ppermute(array, both, pairs)

    even_pairs = [(i, i ^ 1) for i in range(count)]
    odd_pairs = [(i, (i + 1) % count if i % 2 else (i - 1) % count) for i in range(count)]
    at = lambda a, b: a * columns + b
    core_pairs = [(at(a, b), at(a ^ 1, b)) for a in range(rows) for b in range(columns)]
    link_pairs = [
        (at(a, b), at((a + 1) % rows if a % 2 else (a - 1) % rows, b)) for a in range(rows) for b in range(columns)
    ]
    far_pairs = [
        (at(a, b), at(a ^ 1, b) if b in (0, columns - 1) else at(a, b + 1 if b % 2 else b - 1))
        for a in range(rows)
        for b in range(columns)
    ]
    k = lambda f: functools.partial(f, shape)
    big = (2, NC * E * BZ, L)

    boxes, even, odd = call(
        k(pack_kernel),
        [(new_place, "any"), (coeff_old, "any"), (fields_old, "any")],
        [((BZ, NC, E, 2 * L), "vmem"), ((PARCEL, 2 * L), "vmem"), ((PARCEL, 2 * L), "vmem")],
        [SM((1, 1, BZ), I32), SM((1, 1, BZ, NC), F32), pltpu.SemaphoreType.DMA((3,))],
    )
    odd_got = swap(odd, odd_pairs)
    even_got = swap(even, even_pairs)
    stayed, rates, masks = call(
        k(stay_kernel),
        [(new_place, "smem"), (coeff_old, "smem"), (cf_mask, "smem"), (boxes, "vmem")],
        [(big, "vmem"), ((PLANE, L), "vmem"), ((3 * BZ, L), "vmem")],
    )
    core, link, rates = call(
        k(xsend_kernel),
        [(even_got, "vmem"), (odd_got, "vmem"), (stayed, "vmem"), (rates, "vmem")],
        [((FACE + PLANE, L), "vmem"), ((FACE + PLANE, L), "vmem"), ((PLANE, L), "vmem")],
    )
    link_got = swap(link, link_pairs)
    core_got = swap(core, core_pairs)
    moved, near, far = call(
        k(merge_kernel),
        [(even_got, "vmem"), (odd_got, "vmem"), (stayed, "vmem")],
        [(big, "vmem"), ((FACE, L), "vmem"), ((FACE, L), "vmem")],
    )
    near, far = call(
        k(ysend_kernel),
        [(core_got, "vmem"), (link_got, "vmem"), (rates, "vmem"), (near, "vmem"), (far, "vmem")],
        [((FACE + PLANE, L), "vmem"), ((FACE + PLANE, L), "vmem")],
    )
    far_got = swap(far, far_pairs)
    near_got = swap(near, even_pairs)
    part, core_first, link_first = call(
        k(sweep_kernel_with_rates),
        [(a, "vmem") for a in (moved, rates, core_got, link_got, core, link)],
        [(big, "vmem"), ((3 * PLANE, L), "vmem"), ((3 * PLANE, L), "vmem")],
    )
    plane = ((2 * PLANE, L), "vmem")
    first, x_core, x_link, y_near, y_far, kept, sent = call(
        k(flux_kernel),
        [(a, "vmem") for a in (part, rates, masks, core_first, link_first, near_got, far_got, near, far)],
        [(big, "vmem"), plane, plane, plane, plane, plane, plane],
    )
    got = swap(sent, even_pairs)
    (smoothed,) = call(
        k(smooth_kernel),
        [(a, "vmem") for a in (moved, rates, first, x_core, x_link, y_near, y_far)],
        [((1, 1, BZ, NC, E, 2 * L), "out")],
        [VM(big, F32)],
    )
    mine, sent = call(k(half_kernel), [(kept, "vmem"), (got, "vmem")], [plane, plane])
    got = swap(sent, core_pairs)
    (registers,) = call(k(register_kernel), [(mine, "vmem"), (got, "vmem")], [((1, 1, NC, 6, 2 * L), "out")])
    return smoothed, registers


def sweep_kernel_with_rates(shape, moved, rates, core, link, core_sent, link_sent, out, core_first, link_first):
    sweep_kernel(shape, moved, rates, core, link, core_sent, link_sent, out, core_first, link_first)
    _, _, link_ok, _ = ends(shape)
    core_first[2 * PLANE :, :] = core[FACE:, :]
    link_first[2 * PLANE :, :] = jnp.where(link_ok, link[FACE:, :], 0.0)


def solution(mesh):
    shape = (mesh.shape["gx"], mesh.shape["gy"])
    return jax.shard_map(
        functools.partial(body, shape),
        mesh=mesh,
        in_specs=(
            P("gx", "gy", None, None, None, None),
            P("gx", "gy", None, None),
            P("gx", "gy", None),
            P("gx", "gy", None, None),
        ),
        out_specs=(P("gx", "gy", None, None, None, None), P("gx", "gy", None, None, None)),
        check_vma=False,
    )
```

```python
import functools

import jax
import jax.numpy as jnp
from jax import lax
from jax.experimental import pallas as pl
from jax.experimental.pallas import tpu as pltpu
from jax.sharding import PartitionSpec as P

NC = 5
E = 16
BZ = 8
MOVE = 2
L = 128
F32 = jnp.float32
I32 = jnp.int32

PLANE = NC * BZ
FACE = 4 * PLANE
BOXROWS = NC * E
LABELS = MOVE * BOXROWS + MOVE * NC
PARCEL = 176

VM = pltpu.VMEM
SM = pltpu.SMEM


def call(kernel, ins, outs, scratch=(), aliases=None, flops=1000, **kw):
    given, in_specs = [], []
    for array, space in ins:
        if space == "vmem":
            given.append(pltpu.with_memory_space_constraint(array, VM))
            in_specs.append(pl.BlockSpec(memory_space=VM))
        elif space == "smem":
            given.append(array)
            in_specs.append(pl.BlockSpec(memory_space=SM))
        else:
            given.append(pltpu.with_memory_space_constraint(array, pltpu.HBM))
            in_specs.append(pl.BlockSpec(memory_space=pltpu.HBM))
    shapes, out_specs = [], []
    for shape, space in outs:
        if space == "vmem":
            shapes.append(VM(shape, F32))
            out_specs.append(pl.BlockSpec(memory_space=VM))
        else:
            shapes.append(jax.ShapeDtypeStruct(shape, F32))
            out_specs.append(pl.BlockSpec(memory_space=VM))
    return pl.pallas_call(
        kernel,
        out_shape=shapes,
        in_specs=in_specs,
        out_specs=out_specs,
        scratch_shapes=list(scratch),
        input_output_aliases=aliases or {},
        cost_estimate=pl.CostEstimate(flops=flops, bytes_accessed=0, transcendentals=0),
        compiler_params=pltpu.CompilerParams(vmem_limit_bytes=24 * 1024 * 1024),
        **kw,
    )(*given)


def lanes():
    return lax.broadcasted_iota(I32, (BZ, L), 1)


def subs():
    return lax.broadcasted_iota(I32, (BZ, L), 0)


def rl(x, shift):
    shift %= L
    return x if shift == 0 else pltpu.roll(x, shift, 1)


def rs(x, shift):
    shift %= BZ
    return x if shift == 0 else pltpu.roll(x, shift, 0)


def pick_lanes(x, index):
    return jnp.take_along_axis(x, index, axis=1)


def place_of(mesh_shape):
    gx = lax.axis_index("gx")
    gy = lax.axis_index("gy")
    return gx, gy, gx * mesh_shape[1] + gy


def pack_kernel(shape, place_hbm, coeff_hbm, fields_hbm, boxes, even, odd, place, coeff, sem):
    big = pltpu.make_async_copy(fields_hbm.at[0, 0], boxes, sem.at[0])
    small = pltpu.make_async_copy(place_hbm, place, sem.at[1])
    other = pltpu.make_async_copy(coeff_hbm, coeff, sem.at[2])
    big.start()
    small.start()
    other.start()
    _, _, me = place_of(shape)
    ahead = 1 - 2 * (me % 2)
    small.wait()
    other.wait()
    chosen = []
    for out, owner in ((even, me + ahead), (odd, me - ahead)):
        count = jnp.int32(0)
        sources = [jnp.int32(0)] * MOVE
        labels = [jnp.int32(0)] * MOVE
        for s in range(BZ):
            value = place[0, 0, s]
            hit = value // BZ == owner
            for k in range(MOVE):
                taken = hit & (count == k)
                sources[k] = jnp.where(taken, s, sources[k])
                labels[k] = jnp.where(taken, value % BZ + 1, labels[k])
            count = count + hit.astype(I32)
        chosen.append(sources)
        out[LABELS + MOVE : PARCEL, :] = jnp.zeros((PARCEL - LABELS - MOVE, 2 * L), F32)
        for k in range(MOVE):
            out[LABELS + k : LABELS + k + 1, :] = jnp.full((1, 2 * L), labels[k].astype(F32), F32)
            for c in range(NC):
                row = MOVE * BOXROWS + k * NC + c
                out[row : row + 1, :] = jnp.full((1, 2 * L), coeff[0, c, 0, sources[k]], F32)
    big.wait()
    for out, sources in zip((even, odd), chosen):
        for k in range(MOVE):
            for c in range(NC):
                row = (k * NC + c) * E
                out[row : row + E, :] = boxes[sources[k], c]


def stay_kernel(shape, place, coeff, mask, boxes, moved, rates, masks):
    _, _, me = place_of(shape)
    for s in range(BZ):
        value = place[0, 0, s]
        slot = value % BZ

        @pl.when(value // BZ == me)
        def _():
            for c in range(NC):
                for h in range(2):
                    moved[h, pl.ds(c * E * BZ + slot, E, stride=BZ), :] = boxes[s, c, :, h * L : h * L + L]
                rates[pl.ds(c * BZ + slot, 1), :] = jnp.full((1, L), coeff[0, c, 0, s], F32)

    for d in range(3):
        for s in range(BZ):
            masks[d * BZ + s : d * BZ + s + 1, :] = jnp.full((1, L), mask[0, d, 0, s].astype(F32), F32)


def arrivals(even, odd):
    sub = subs()
    found = []
    for parcel in (even, odd):
        for k in range(MOVE):
            label = parcel[LABELS + k : LABELS + k + 1, :L]
            found.append((parcel, k, label == (sub + 1).astype(F32)))
    return found


def merged(found, moved, c, x, h):
    row = (c * E + x) * BZ
    tile = moved[h, row : row + BZ, :]
    for parcel, k, hit in found:
        at = (k * NC + c) * E + x
        tile = jnp.where(hit, parcel[at : at + 1, h * L : h * L + L], tile)
    return tile


def plane_row(layer, h, c):
    return ((layer * 2 + h) * NC + c) * BZ


def xsend_kernel(shape, even, odd, moved, rates, core, link, all_rates):
    gx, _, _ = place_of(shape)
    first = gx % 2 == 0
    found = arrivals(even, odd)
    for c in range(NC):
        tile = rates[c * BZ : c * BZ + BZ, :]
        for parcel, k, hit in found:
            at = MOVE * BOXROWS + k * NC + c
            tile = jnp.where(hit, parcel[at : at + 1, :L], tile)
        all_rates[c * BZ : c * BZ + BZ, :] = tile
        core[FACE + c * BZ : FACE + c * BZ + BZ, :] = tile
        link[FACE + c * BZ : FACE + c * BZ + BZ, :] = tile
        for layer in range(2):
            for h in range(2):
                low = merged(found, moved, c, layer, h)
                high = merged(found, moved, c, E - 1 - layer, h)
                at = plane_row(layer, h, c)
                core[at : at + BZ, :] = jnp.where(first, high, low)
                link[at : at + BZ, :] = jnp.where(first, low, high)


def merge_kernel(shape, even, odd, moved, out, near, far):
    _, gy, _ = place_of(shape)
    first = gy % 2 == 0
    found = arrivals(even, odd)
    lane = lanes()
    for c in range(NC):
        low = [[None, None], [None, None]]
        high = [[None, None], [None, None]]
        for x in range(E):
            row = (c * E + x) * BZ
            at = L // 8 * (x % 8)
            here = lane // E == x % 8
            half = x // 8
            for h in range(2):
                tile = merged(found, moved, c, x, h)
                out[h, row : row + BZ, :] = tile
                for layer in range(2):
                    keep, start = ((low, E * layer) if h == 0 else (high, L - E - E * layer))
                    strip = rl(tile, at - start)
                    old = keep[layer][half]
                    keep[layer][half] = strip if old is None else jnp.where(here, strip, old)
        for layer in range(2):
            for h in range(2):
                at = plane_row(layer, h, c)
                near[at : at + BZ, :] = jnp.where(first, high[layer][h], low[layer][h])
                far[at : at + BZ, :] = jnp.where(first, low[layer][h], high[layer][h])


def ends(shape):
    gx, gy, _ = place_of(shape)
    x_first, y_first = gx % 2 == 0, gy % 2 == 0
    link_ok = jnp.where(x_first, gx > 0, gx < shape[0] - 1)
    far_ok = jnp.where(y_first, gy > 0, gy < shape[1] - 1)
    return x_first, y_first, link_ok, far_ok


def ysend_kernel(shape, core, link, rates, near, far, near_out, far_out):
    x_first, y_first, link_ok, _ = ends(shape)
    lane = lanes()
    near_out[:FACE, :] = near[...]
    far_out[:FACE, :] = far[...]
    for c in range(NC):
        lines = []
        for h in range(2):
            at = plane_row(0, h, c)
            a = core[at : at + BZ, :]
            b = jnp.where(link_ok, link[at : at + BZ, :], 0.0)
            lines.append((jnp.where(x_first, b, a), jnp.where(x_first, a, b)))
        rate = rates[c * BZ : c * BZ + BZ, :]
        bottom = jnp.where(lane < E, lines[0][0], rl(lines[0][1], E))
        top = jnp.where(lane < E, rl(lines[1][0], E), rl(lines[1][1], 2 * E))
        bottom = jnp.where(lane < 2 * E, bottom, rate)
        top = jnp.where(lane < 2 * E, top, rate)
        at = FACE + c * BZ
        near_out[at : at + BZ, :] = jnp.where(y_first, top, bottom)
        far_out[at : at + BZ, :] = jnp.where(y_first, bottom, top)


def z_parts(x, lane, sub, swap):
    z = lane % E
    down = jnp.where(sub == 0, 0.0, rs(x, 1))
    up = jnp.where(sub == BZ - 1, 0.0, rs(x, -1))
    ends_ = pick_lanes(jnp.where(z == E - 1, down, up), swap)
    return jnp.where(z == 0, ends_, rl(x, 1)) + jnp.where(z == E - 1, ends_, rl(x, -1))


def swap_index(lane):
    z = lane % E
    return jnp.where(z == 0, lane + E - 1, jnp.where(z == E - 1, lane - E + 1, lane))


def inner(pair, lane, sub, swap):
    a, b = pair
    a1, b1, a2, b2 = rl(a, E), rl(b, E), rl(a, -E), rl(b, -E)
    low, high = lane < E, lane >= L - E
    first = jnp.where(low, 0.0, a1) + jnp.where(high, b2, a2) + z_parts(a, lane, sub, swap)
    second = jnp.where(low, a1, b1) + jnp.where(high, 0.0, b2) + z_parts(b, lane, sub, swap)
    return first, second


def pair_at(ref, layer, c):
    return tuple(ref[plane_row(layer, h, c) : plane_row(layer, h, c) + BZ, :] for h in range(2))


def tile_at(ref, c, x):
    row = (c * E + x) * BZ
    return tuple(ref[h, row : row + BZ, :] for h in range(2))


def z_differences(tiles, sub, upper):
    down = [jnp.where(sub == 0, 0.0, t) for t in [rs(t, 1) for t in tiles]]
    up = [jnp.where(sub == BZ - 1, 0.0, t) for t in [rs(t, -1) for t in tiles]]
    high = [rl(t, 1 - E) for t in [jnp.where(upper, t, d) for t, d in zip(tiles, down)]]
    return [jnp.where(upper, u - g, g - t) for g, u, t in zip(high, up, tiles)]


def sweep_kernel(shape, moved, rates, core, link, core_sent, link_sent, out, core_first, link_first, tops):
    x_first, _, link_ok, _ = ends(shape)
    _, gy, _ = place_of(shape)
    lane, sub = lanes(), subs()
    swap = swap_index(lane)
    upper = sub % 2 == 1
    z = lane % E
    core_first[2 * PLANE :, :] = core[FACE:, :]
    link_first[2 * PLANE :, :] = jnp.where(link_ok, link[FACE:, :], 0.0)
    for c in range(NC):
        rate = rates[c * BZ : c * BZ + BZ, :]
        scale = 1.0 / (1.0 + 6.0 * rate)
        ghost = []
        for got, sent, kept, ok in ((core, core_sent, core_first, None), (link, link_sent, link_first, link_ok)):
            g0, g1, own = pair_at(got, 0, c), pair_at(got, 1, c), pair_at(sent, 0, c)
            g_rate = got[FACE + c * BZ : FACE + c * BZ + BZ, :]
            if ok is not None:
                g0, g1 = (tuple(jnp.where(ok, t, 0.0) for t in g) for g in (g0, g1))
                g_rate = jnp.where(ok, g_rate, 0.0)
            ghost.append(g0)
            g_scale = 1.0 / (1.0 + 6.0 * g_rate)
            sums = inner(g0, lane, sub, swap)
            for h in range(2):
                value = (g0[h] + g_rate * (sums[h] + g1[h] + own[h])) * g_scale
                if ok is not None:
                    value = jnp.where(ok, value, 0.0)
                row = (h * NC + c) * BZ
                kept[row : row + BZ, :] = value
        low = [jnp.where(x_first, b, a) for a, b in zip(*ghost)]
        high = [jnp.where(x_first, a, b) for a, b in zip(*ghost)]
        for x in range(E):
            here = tile_at(moved, c, x)
            before = low if x == 0 else tile_at(moved, c, x - 1)
            after = high if x == E - 1 else tile_at(moved, c, x + 1)
            sums = inner(here, lane, sub, swap)
            row = (c * E + x) * BZ
            for h in range(2):
                out[h, row : row + BZ, :] = (here[h] + rate * (sums[h] + before[h] + after[h])) * scale
    every = [(h, c, k) for c in range(NC) for h in range(2) for k in range(E // 2)]
    d = []
    for h, c, k in every:
        row = (c * E + 2 * k) * BZ
        d.append(out[h, row : row + BZ, :] + out[h, row + BZ : row + 2 * BZ, :])
    d = z_differences(d, sub, upper)
    d = [t + r for t, r in zip(d, [rl(t, -E) for t in d])]
    d = [rl(t, k) for t, (_, _, k) in zip(d, every)]
    faces = {}
    for t, (h, c, k) in zip(d, every):
        faces[h, c] = t if k == 0 else jnp.where(z == k, t, faces[h, c])
    y8 = lane % 8
    source = (y8 % 4) * (2 * E) + lane // E
    picked = {key: pick_lanes(t, source) for key, t in faces.items()}
    for c in range(NC):
        top = jnp.where(y8 < 4, picked[0, c], picked[1, c])
        tops[c * BZ : c * BZ + BZ, :] = jnp.where(z // 8 == gy % 2, top, 0.0)


def coarse_plane(pair, parity, lane, sub):
    sums = []
    for t in pair:
        t = t + rl(t, -1)
        sums.append(t + rl(t, -E))
    source = (lane // E % 4) * (2 * E) + 2 * (lane % 8)
    out = jnp.where(lane < L // 2, pick_lanes(sums[0], source), pick_lanes(sums[1], source))
    return jnp.where(lane % E // 8 == sub % 2, 0.25 * out, 0.0)


def strips(low, high, x, low_lane, high_lane):
    shift = E * (x % 8)
    return (
        jnp.where(low_lane, rl(low[x // 8], -shift), 0.0),
        jnp.where(high_lane, rl(high[x // 8], L - E - shift), 0.0),
    )


def flux_kernel(
    shape, partial, moved_rates, masks, tops, core_first, link_first, near, far, near_sent, far_sent,
    x_core, x_link, y_near, y_far, kept, sent,
):
    x_first, y_first, link_ok, far_ok = ends(shape)
    gx, gy, _ = place_of(shape)
    par_x, par_y = gx % 2, gy % 2
    lane, sub = lanes(), subs()
    swap = swap_index(lane)
    upper = sub % 2 == 1
    z = lane % E
    low_lane, high_lane = lane < E, lane >= L - E
    each = range(NC)
    rate = [moved_rates[c * BZ : c * BZ + BZ, :] for c in each]
    scale = [1.0 / (1.0 + 6.0 * r) for r in rate]
    weight = [r * q for r, q in zip(rate, scale)]

    def extra_at(ref, c):
        return ref[FACE + c * BZ : FACE + c * BZ + BZ, :]

    def corner(extra):
        return jnp.where(low_lane, extra, 0.0), jnp.where(high_lane, rl(extra, L - 2 * E), 0.0)

    sides = []
    for got, sent_, kept_, ok in ((near, near_sent, y_near, None), (far, far_sent, y_far, far_ok)):
        planes, extras, firsts = [], [], []
        for c in each:
            g0, g1, own = pair_at(got, 0, c), pair_at(got, 1, c), pair_at(sent_, 0, c)
            extra = extra_at(got, c)
            if ok is not None:
                g0, g1 = (tuple(jnp.where(ok, t, 0.0) for t in g) for g in (g0, g1))
                extra = jnp.where(ok, extra, 0.0)
            g_rate = jnp.where(lane < L // 2, rl(extra, L // 2), extra)
            g_scale = 1.0 / (1.0 + 6.0 * g_rate)
            sums, line = inner(g0, lane, sub, swap), corner(extra)
            first = []
            for h in range(2):
                value = (g0[h] + g_rate * (sums[h] + line[h] + g1[h] + own[h])) * g_scale
                if ok is not None:
                    value = jnp.where(ok, value, 0.0)
                row = (h * NC + c) * BZ
                kept_[row : row + BZ, :] = value
                first.append(value)
            planes.append(g0)
            extras.append(extra)
            firsts.append(first)
        sides.append((planes, extras, firsts))
    far_r, far_f = sides[1][0], sides[1][2]

    def by_side(which, c):
        a, b = sides[0][which][c], sides[1][which][c]
        if which == 1:
            return jnp.where(y_first, b, a), jnp.where(y_first, a, b)
        return [jnp.where(y_first, q, p) for p, q in zip(a, b)], [jnp.where(y_first, p, q) for p, q in zip(a, b)]

    faces_y = []
    for c in each:
        own, own1 = pair_at(far_sent, 0, c), pair_at(far_sent, 1, c)
        sums, line = inner(own, lane, sub, swap), corner(extra_at(far_sent, c))
        flux = [
            far_f[c][h] - (own[h] + rate[c] * (sums[h] + line[h] + own1[h] + far_r[c][h])) * scale[c] for h in range(2)
        ]
        face = coarse_plane(flux, par_x, lane, sub) * (rate[c] * masks[BZ : 2 * BZ, :])
        faces_y.append(face + rs(face, 1))
    faces_x = []
    for c in each:
        low_line, high_line = by_side(1, c)
        planes = []
        for part, kept_, at_low, ok in ((core_first, x_core, ~x_first, None), (link_first, x_link, x_first, link_ok)):
            g_rate = kept_rate(part, c)
            g_weight = g_rate / (1.0 + 6.0 * g_rate)
            bottom = jnp.where(at_low, low_line, rl(low_line, -E))
            top = jnp.where(at_low, rl(high_line, L - E), rl(high_line, L - 2 * E))
            plane = []
            for h, (line, there) in enumerate(((bottom, low_lane), (top, high_lane))):
                row = (h * NC + c) * BZ
                value = part[row : row + BZ, :] + g_weight * jnp.where(there, line, 0.0)
                if ok is not None:
                    value = jnp.where(ok, value, 0.0)
                kept_[row : row + BZ, :] = value
                plane.append(value)
            planes.append(plane)
        low_r, high_r = by_side(0, c)
        at_0, at_15 = (strips(low_r, high_r, x, low_lane, high_lane) for x in (0, E - 1))
        cells_0, cells_15 = tile_at(partial, c, 0), tile_at(partial, c, E - 1)
        flux = []
        for h in range(2):
            cell = jnp.where(x_first, cells_0[h], cells_15[h])
            cell = cell + weight[c] * jnp.where(x_first, at_0[h], at_15[h])
            flux.append(planes[1][h] - cell)
        face = coarse_plane(flux, par_y, lane, sub) * (rate[c] * masks[0:BZ, :])
        faces_x.append(face + rs(face, -1))
    faces_z = []
    source = (lane // E % 4) * (2 * E) + jnp.where(lane % 8 == 7, 7, 0)
    d = []
    for c in each:
        for side in by_side(0, c):
            d += [weight[c] * t for t in side]
    d = [t + r for t, r in zip(d, [rl(t, -E) for t in d])]
    d = z_differences(d, sub, upper)
    halves = []
    for c in each:
        for h in range(2):
            halves.append(jnp.where(z == 7, rl(d[4 * c + 2 + h], 7), d[4 * c + h]))
    halves = [pick_lanes(t, source) for t in halves]
    for c in each:
        add = jnp.where(lane < L // 2, halves[2 * c], halves[2 * c + 1])
        add = jnp.where((z == 8 * par_y) | (z == 8 * par_y + 7), add, 0.0)
        faces_z.append((tops[c * BZ : c * BZ + BZ, :] + add) * (0.25 * rate[c] * masks[2 * BZ :, :]))
    left = sub % 4 < 2
    for c in each:
        for h in range(2):
            outer = jnp.where(
                upper, jnp.where(par_x == h, faces_y[c], 0.0), jnp.where(par_y == h, faces_x[c], 0.0)
            )
            top = jnp.where(par_x == h, faces_z[c], 0.0)
            columns = (jnp.where(left, outer, rs(top, 2)), jnp.where(left, rs(outer, -2), top))
            row = (h * NC + c) * BZ
            kept[row : row + BZ, :] = jnp.where(y_first, columns[0], columns[1])
            sent[row : row + BZ, :] = jnp.where(y_first, columns[1], columns[0])


def kept_rate(part, c):
    return part[2 * PLANE + c * BZ : 2 * PLANE + c * BZ + BZ, :]


def half_kernel(shape, kept, got, mine, sent):
    gx, _, _ = place_of(shape)
    first = gx % 2 == 0
    top = subs() < 4
    for i in range(2 * NC):
        a, b = kept[i * BZ : i * BZ + BZ, :], got[i * BZ : i * BZ + BZ, :]
        rows = (jnp.where(top, a, rs(b, 4)), jnp.where(top, rs(a, 4), b))
        mine[i * BZ : i * BZ + BZ, :] = jnp.where(first, rows[0], rows[1])
        sent[i * BZ : i * BZ + BZ, :] = jnp.where(first, rows[1], rows[0])


def register_kernel(shape, mine, got, out):
    x_first, y_first, _, _ = ends(shape)
    sub = subs()
    for h in range(2):
        for c in range(NC):
            row = (h * NC + c) * BZ
            m, g = mine[row : row + BZ, :], got[row : row + BZ, :]
            a, b = m + rs(m, 4), g + rs(g, 4)
            s = m + g
            ab = a + b
            x0, x1 = jnp.where(x_first, a, b), jnp.where(x_first, b, a)
            y0, y1 = jnp.where(y_first, rs(s, 1), rs(s, 5)), jnp.where(y_first, rs(s, 5), rs(s, 1))
            t = jnp.where(sub == 0, x0, jnp.where(sub == 1, rs(x1, 1), rs(ab, 2)))
            t = jnp.where(sub == 2, y0, jnp.where(sub == 3, rs(y1, 1), t))
            out[0, 0, c, :, h * L : h * L + L] = t[:6]


def smooth_kernel(shape, moved, rates, partial, near, far, x_core, x_link, y_near, y_far, out, first, held):
    x_first, y_first, _, far_ok = ends(shape)
    lane, sub = lanes(), subs()
    swap = swap_index(lane)
    low_lane, high_lane = lane < E, lane >= L - E
    for c in range(NC):
        rate = rates[c * BZ : c * BZ + BZ, :]
        scale = 1.0 / (1.0 + 6.0 * rate)
        weight = rate * scale

        def ghosts(a, b, a_first):
            low = [jnp.where(a_first, q, p) for p, q in zip(a, b)]
            high = [jnp.where(a_first, p, q) for p, q in zip(a, b)]
            return low, high

        low, high = ghosts(pair_at(x_core, 0, c), pair_at(x_link, 0, c), x_first)
        low_y, high_y = ghosts(pair_at(y_near, 0, c), pair_at(y_far, 0, c), y_first)
        far_r = [jnp.where(far_ok, t, 0.0) for t in pair_at(far, 0, c)]
        low_r, high_r = ghosts(pair_at(near, 0, c), far_r, y_first)

        for x in range(E):
            edge = strips(low_r, high_r, x, low_lane, high_lane)
            row = (c * E + x) * BZ
            for h in range(2):
                first[h, row : row + BZ, :] = partial[h, row : row + BZ, :] + weight * edge[h]
        for x in range(E):
            here = tile_at(first, c, x)
            before = low if x == 0 else tile_at(first, c, x - 1)
            after = high if x == E - 1 else tile_at(first, c, x + 1)
            sums = inner(here, lane, sub, swap)
            edge = strips(low_y, high_y, x, low_lane, high_lane)
            start = tile_at(moved, c, x)
            row = (c * E + x) * BZ
            for h in range(2):
                held[h, row : row + BZ, :] = (start[h] + rate * (sums[h] + before[h] + after[h] + edge[h])) * scale
        for s in range(BZ):
            for h in range(2):
                out[0, 0, s, c, :, h * L : h * L + L] = held[h, pl.ds(c * E * BZ + s, E, stride=BZ), :]


def body(shape, fields_old, coeff_old, new_place, cf_mask):
    rows, columns = shape
    count = rows * columns
    both = ("gx", "gy")

    def swap(array, pairs):
        return lax.ppermute(array, both, pairs)

    even_pairs = [(i, i ^ 1) for i in range(count)]
    odd_pairs = [(i, (i + 1) % count if i % 2 else (i - 1) % count) for i in range(count)]
    at = lambda a, b: a * columns + b
    core_pairs = [(at(a, b), at(a ^ 1, b)) for a in range(rows) for b in range(columns)]
    link_pairs = [
        (at(a, b), at((a + 1) % rows if a % 2 else (a - 1) % rows, b)) for a in range(rows) for b in range(columns)
    ]
    far_pairs = [
        (at(a, b), at(a ^ 1, b) if b in (0, columns - 1) else at(a, b + 1 if b % 2 else b - 1))
        for a in range(rows)
        for b in range(columns)
    ]
    k = lambda f: functools.partial(f, shape)
    coeff_old = coeff_old.transpose(0, 3, 1, 2)
    cf_mask = cf_mask.transpose(0, 2, 1, 3)
    big = (2, NC * E * BZ, L)

    boxes, even, odd = call(
        k(pack_kernel),
        [(new_place, "any"), (coeff_old, "any"), (fields_old, "any")],
        [((BZ, NC, E, 2 * L), "vmem"), ((PARCEL, 2 * L), "vmem"), ((PARCEL, 2 * L), "vmem")],
        [SM((1, 1, BZ), I32), SM((1, NC, 1, BZ), F32), pltpu.SemaphoreType.DMA((3,))],
    )
    odd_got = swap(odd, odd_pairs)
    even_got = swap(even, even_pairs)
    stayed, rates, masks = call(
        k(stay_kernel),
        [(new_place, "smem"), (coeff_old, "smem"), (cf_mask, "smem"), (boxes, "vmem")],
        [(big, "vmem"), ((PLANE, L), "vmem"), ((3 * BZ, L), "vmem")],
    )
    core, link, rates = call(
        k(xsend_kernel),
        [(even_got, "vmem"), (odd_got, "vmem"), (stayed, "vmem"), (rates, "vmem")],
        [((FACE + PLANE, L), "vmem"), ((FACE + PLANE, L), "vmem"), ((PLANE, L), "vmem")],
    )
    link_got = swap(link, link_pairs)
    core_got = swap(core, core_pairs)
    moved, near, far = call(
        k(merge_kernel),
        [(even_got, "vmem"), (odd_got, "vmem"), (stayed, "vmem")],
        [(big, "vmem"), ((FACE, L), "vmem"), ((FACE, L), "vmem")],
    )
    near, far = call(
        k(ysend_kernel),
        [(core_got, "vmem"), (link_got, "vmem"), (rates, "vmem"), (near, "vmem"), (far, "vmem")],
        [((FACE + PLANE, L), "vmem"), ((FACE + PLANE, L), "vmem")],
    )
    far_got = swap(far, far_pairs)
    near_got = swap(near, even_pairs)
    part, core_first, link_first, tops = call(
        k(sweep_kernel),
        [(a, "vmem") for a in (moved, rates, core_got, link_got, core, link)],
        [(big, "vmem"), ((3 * PLANE, L), "vmem"), ((3 * PLANE, L), "vmem"), ((PLANE, L), "vmem")],
    )
    plane = ((2 * PLANE, L), "vmem")
    x_core, x_link, y_near, y_far, kept, sent = call(
        k(flux_kernel),
        [(a, "vmem") for a in (part, rates, masks, tops, core_first, link_first, near_got, far_got, near, far)],
        [plane] * 6,
    )
    got = swap(sent, even_pairs)
    (smoothed,) = call(
        k(smooth_kernel),
        [(a, "vmem") for a in (moved, rates, part, near_got, far_got, x_core, x_link, y_near, y_far)],
        [((1, 1, BZ, NC, E, 2 * L), "out")],
        [VM(big, F32), VM(big, F32)],
    )
    mine, sent = call(k(half_kernel), [(kept, "vmem"), (got, "vmem")], [plane, plane])
    got = swap(sent, core_pairs)
    (registers,) = call(k(register_kernel), [(mine, "vmem"), (got, "vmem")], [((1, 1, NC, 6, 2 * L), "out")])
    return smoothed, registers


def solution(mesh):
    shape = (mesh.shape["gx"], mesh.shape["gy"])
    return jax.shard_map(
        functools.partial(body, shape),
        mesh=mesh,
        in_specs=(
            P("gx", "gy", None, None, None, None),
            P("gx", "gy", None, None),
            P("gx", "gy", None),
            P("gx", "gy", None, None),
        ),
        out_specs=(P("gx", "gy", None, None, None, None), P("gx", "gy", None, None, None)),
        check_vma=False,
    )
```

```python
import functools

import jax
import jax.numpy as jnp
from jax import lax
from jax.experimental import pallas as pl
from jax.experimental.pallas import tpu as pltpu
from jax.sharding import PartitionSpec as P

NC = 5
E = 16
BZ = 8
MOVE = 2
L = 128
F32 = jnp.float32
I32 = jnp.int32

PLANE = NC * BZ
FACE = 4 * PLANE
EDGES = (0, 1, E - 2, E - 1)
AHEAD = MOVE * NC * 4
LABELS = AHEAD + MOVE * NC
PARCEL = 56
REST = MOVE * NC * 12
XFACE = FACE + BZ
YFACE = FACE + 2 * BZ

VM = pltpu.VMEM
SM = pltpu.SMEM


def call(kernel, ins, outs, scratch=(), aliases=None, flops=1000, **kw):
    given, in_specs = [], []
    for array, space in ins:
        if space == "vmem":
            given.append(pltpu.with_memory_space_constraint(array, VM))
            in_specs.append(pl.BlockSpec(memory_space=VM))
        elif space == "smem":
            given.append(array)
            in_specs.append(pl.BlockSpec(memory_space=SM))
        else:
            given.append(pltpu.with_memory_space_constraint(array, pltpu.HBM))
            in_specs.append(pl.BlockSpec(memory_space=pltpu.HBM))
    shapes, out_specs = [], []
    for shape, space in outs:
        if space == "vmem":
            shapes.append(VM(shape, F32))
            out_specs.append(pl.BlockSpec(memory_space=VM))
        else:
            shapes.append(jax.ShapeDtypeStruct(shape, F32))
            out_specs.append(pl.BlockSpec(memory_space=pltpu.HBM if space == "hbm" else VM))
    return pl.pallas_call(
        kernel,
        out_shape=shapes,
        in_specs=in_specs,
        out_specs=out_specs,
        scratch_shapes=list(scratch),
        input_output_aliases=aliases or {},
        cost_estimate=pl.CostEstimate(flops=flops, bytes_accessed=0, transcendentals=0),
        compiler_params=pltpu.CompilerParams(vmem_limit_bytes=24 * 1024 * 1024),
        **kw,
    )(*given)


def lanes():
    return lax.broadcasted_iota(I32, (BZ, L), 1)


def subs():
    return lax.broadcasted_iota(I32, (BZ, L), 0)


def rl(x, shift):
    shift %= L
    return x if shift == 0 else pltpu.roll(x, shift, 1)


def rs(x, shift):
    shift %= BZ
    return x if shift == 0 else pltpu.roll(x, shift, 0)


def pick_lanes(x, index):
    return jnp.take_along_axis(x, index, axis=1)


def place_of(mesh_shape):
    gx = lax.axis_index("gx")
    gy = lax.axis_index("gy")
    return gx, gy, gx * mesh_shape[1] + gy


def pack_kernel(
    shape, place_hbm, coeff_hbm, mask_hbm, fields_hbm, even, odd, even_rest, odd_rest, boxes, slots, rates, masks,
    place, coeff, mask, sem,
):
    pairs = ((fields_hbm.at[0, 0], boxes), (place_hbm, place), (coeff_hbm, coeff), (mask_hbm, mask))
    copies = [pltpu.make_async_copy(a, b, sem.at[i]) for i, (a, b) in enumerate(pairs)]
    for copy in copies:
        copy.start()
    _, _, me = place_of(shape)
    ahead = 1 - 2 * (me % 2)
    for copy in copies[1:]:
        copy.wait()
    chosen = []
    for out, owner in ((even, me + ahead), (odd, me - ahead)):
        count = jnp.int32(0)
        sources = [jnp.int32(0)] * MOVE
        labels = [jnp.int32(0)] * MOVE
        for s in range(BZ):
            value = place[0, 0, s]
            hit = value // BZ == owner
            for k in range(MOVE):
                taken = hit & (count == k)
                sources[k] = jnp.where(taken, s, sources[k])
                labels[k] = jnp.where(taken, value % BZ + 1, labels[k])
            count = count + hit.astype(I32)
        chosen.append(sources)
        out[LABELS + MOVE : PARCEL, :] = jnp.zeros((PARCEL - LABELS - MOVE, 2 * L), F32)
        for k in range(MOVE):
            out[LABELS + k : LABELS + k + 1, :] = jnp.full((1, 2 * L), labels[k].astype(F32), F32)
            for c in range(NC):
                row = AHEAD + k * NC + c
                out[row : row + 1, :] = jnp.full((1, 2 * L), coeff[0, c, 0, sources[k]], F32)
    for s in range(BZ):
        value = place[0, 0, s]
        label = jnp.where(value // BZ == me, value % BZ + 1, 0)
        slots[s : s + 1, :] = jnp.full((1, L), label.astype(F32), F32)
        for c in range(NC):
            rates[s * NC + c : s * NC + c + 1, :] = jnp.full((1, L), coeff[0, c, 0, s], F32)
        for d in range(3):
            masks[d * BZ + s : d * BZ + s + 1, :] = jnp.full((1, L), mask[0, d, 0, s].astype(F32), F32)
    copies[0].wait()
    for out, rest, sources in ((even, even_rest, chosen[0]), (odd, odd_rest, chosen[1])):
        for k in range(MOVE):
            for c in range(NC):
                box = k * NC + c
                out[4 * box : 4 * box + 2, :] = boxes[sources[k], c, :2]
                out[4 * box + 2 : 4 * box + 4, :] = boxes[sources[k], c, E - 2 :]
                rest[12 * box : 12 * box + 12, :] = boxes[sources[k], c, 2 : E - 2]


def stay_kernel(shape, boxes, slots, old_rates, moved, rates):
    label = (subs() + 1).astype(F32)
    found = [slots[s : s + 1, :] == label for s in range(BZ)]
    for c in range(NC):
        tile = jnp.zeros((BZ, L), F32)
        for s in range(BZ):
            tile = jnp.where(found[s], old_rates[s * NC + c : s * NC + c + 1, :], tile)
        rates[c * BZ : c * BZ + BZ, :] = tile
        for x in range(E):
            row = (c * E + x) * BZ
            for h in range(2):
                tile = jnp.zeros((BZ, L), F32)
                for s in range(BZ):
                    tile = jnp.where(found[s], boxes[s, c, x : x + 1, h * L : h * L + L], tile)
                moved[h, row : row + BZ, :] = tile


def arrivals(even, odd):
    sub = subs()
    found = []
    for parcel in (even, odd):
        for k in range(MOVE):
            label = parcel[LABELS + k : LABELS + k + 1, :L]
            found.append((parcel, k, label == (sub + 1).astype(F32)))
    return found


def merged(found, moved, c, x, h, rests=None):
    row = (c * E + x) * BZ
    tile = moved[h, row : row + BZ, :]
    for i, (parcel, k, hit) in enumerate(found):
        if x in EDGES:
            source, at = parcel, (k * NC + c) * 4 + EDGES.index(x)
        else:
            source, at = rests[i // MOVE], (k * NC + c) * 12 + x - 2
        tile = jnp.where(hit, source[at : at + 1, h * L : h * L + L], tile)
    return tile


def spread(tile, lane):
    return pick_lanes(tile, jnp.full((BZ, L), lane, I32))


def plane_row(layer, h, c):
    return ((layer * 2 + h) * NC + c) * BZ


def xsend_kernel(shape, even, odd, moved, rates, core, link, all_rates):
    gx, _, _ = place_of(shape)
    first = gx % 2 == 0
    found = arrivals(even, odd)
    lane = lanes()
    together = jnp.zeros((BZ, L), F32)
    for c in range(NC):
        tile = rates[c * BZ : c * BZ + BZ, :]
        for parcel, k, hit in found:
            at = AHEAD + k * NC + c
            tile = jnp.where(hit, parcel[at : at + 1, :L], tile)
        all_rates[c * BZ : c * BZ + BZ, :] = tile
        together = jnp.where(lane % L == c, tile, together)
        for layer in range(2):
            for h in range(2):
                low = merged(found, moved, c, layer, h)
                high = merged(found, moved, c, E - 1 - layer, h)
                at = plane_row(layer, h, c)
                core[at : at + BZ, :] = jnp.where(first, high, low)
                link[at : at + BZ, :] = jnp.where(first, low, high)
    core[FACE:, :] = together
    link[FACE:, :] = together


def merge_kernel(shape, odd, even, odd_rest, even_rest, moved, out, near, far):
    _, gy, _ = place_of(shape)
    first = gy % 2 == 0
    found = arrivals(even, odd)
    lane = lanes()
    for c in range(NC):
        low = [[None, None], [None, None]]
        high = [[None, None], [None, None]]
        for x in range(E):
            row = (c * E + x) * BZ
            at = L // 8 * (x % 8)
            here = lane // E == x % 8
            half = x // 8
            for h in range(2):
                tile = merged(found, moved, c, x, h, (even_rest, odd_rest))
                out[h, row : row + BZ, :] = tile
                for layer in range(2):
                    keep, start = ((low, E * layer) if h == 0 else (high, L - E - E * layer))
                    strip = rl(tile, at - start)
                    old = keep[layer][half]
                    keep[layer][half] = strip if old is None else jnp.where(here, strip, old)
        for layer in range(2):
            for h in range(2):
                at = plane_row(layer, h, c)
                near[at : at + BZ, :] = jnp.where(first, high[layer][h], low[layer][h])
                far[at : at + BZ, :] = jnp.where(first, low[layer][h], high[layer][h])


def ends(shape):
    gx, gy, _ = place_of(shape)
    x_first, y_first = gx % 2 == 0, gy % 2 == 0
    link_ok = jnp.where(x_first, gx > 0, gx < shape[0] - 1)
    far_ok = jnp.where(y_first, gy > 0, gy < shape[1] - 1)
    return x_first, y_first, link_ok, far_ok


def ysend_kernel(shape, link, core, rates, near, far, near_out, far_out):
    x_first, y_first, link_ok, _ = ends(shape)
    lane = lanes()
    near_out[:FACE, :] = near[...]
    far_out[:FACE, :] = far[...]
    bottoms = [jnp.zeros((BZ, L), F32)] * 2
    tops = [jnp.zeros((BZ, L), F32)] * 2
    for c in range(NC):
        lines = []
        for h in range(2):
            at = plane_row(0, h, c)
            a = core[at : at + BZ, :]
            b = jnp.where(link_ok, link[at : at + BZ, :], 0.0)
            lines.append((jnp.where(x_first, b, a), jnp.where(x_first, a, b)))
        i, at = divmod(c, 4)
        at *= 2 * E
        low = (lane >= at) & (lane < at + E)
        high = (lane >= at + E) & (lane < at + 2 * E)
        bottoms[i] = jnp.where(low, rl(lines[0][0], at), jnp.where(high, rl(lines[0][1], at + E), bottoms[i]))
        tops[i] = jnp.where(low, rl(lines[1][0], at + E), jnp.where(high, rl(lines[1][1], at + 2 * E), tops[i]))
        rate = rates[c * BZ : c * BZ + BZ, :]
        bottoms[1] = jnp.where(lane == L // 2 + c, rate, bottoms[1])
        tops[1] = jnp.where(lane == L // 2 + c, rate, tops[1])
    for i in range(2):
        at = FACE + i * BZ
        near_out[at : at + BZ, :] = jnp.where(y_first, tops[i], bottoms[i])
        far_out[at : at + BZ, :] = jnp.where(y_first, bottoms[i], tops[i])


def extra_at(ref, c):
    i, at = divmod(c, 4)
    return rl(ref[FACE + i * BZ : FACE + i * BZ + BZ, :], -2 * E * at)


def y_rate(ref, c):
    return spread(ref[FACE + BZ : FACE + 2 * BZ, :], L // 2 + c)


def z_parts(x, lane, sub, swap):
    z = lane % E
    down = jnp.where(sub == 0, 0.0, rs(x, 1))
    up = jnp.where(sub == BZ - 1, 0.0, rs(x, -1))
    ends_ = pick_lanes(jnp.where(z == E - 1, down, up), swap)
    return jnp.where(z == 0, ends_, rl(x, 1)) + jnp.where(z == E - 1, ends_, rl(x, -1))


def swap_index(lane):
    z = lane % E
    return jnp.where(z == 0, lane + E - 1, jnp.where(z == E - 1, lane - E + 1, lane))


def inner(pair, lane, sub, swap):
    a, b = pair
    a1, b1, a2, b2 = rl(a, E), rl(b, E), rl(a, -E), rl(b, -E)
    low, high = lane < E, lane >= L - E
    first = jnp.where(low, 0.0, a1) + jnp.where(high, b2, a2) + z_parts(a, lane, sub, swap)
    second = jnp.where(low, a1, b1) + jnp.where(high, 0.0, b2) + z_parts(b, lane, sub, swap)
    return first, second


def pair_at(ref, layer, c):
    return tuple(ref[plane_row(layer, h, c) : plane_row(layer, h, c) + BZ, :] for h in range(2))


def tile_at(ref, c, x):
    row = (c * E + x) * BZ
    return tuple(ref[h, row : row + BZ, :] for h in range(2))


def z_differences(tiles, sub, upper):
    down = [jnp.where(sub == 0, 0.0, t) for t in [rs(t, 1) for t in tiles]]
    up = [jnp.where(sub == BZ - 1, 0.0, t) for t in [rs(t, -1) for t in tiles]]
    high = [rl(t, 1 - E) for t in [jnp.where(upper, t, d) for t, d in zip(tiles, down)]]
    return [jnp.where(upper, u - g, g - t) for g, u, t in zip(high, up, tiles)]


def sweep_kernel(shape, moved, rates, link, core, core_sent, link_sent, out, core_first, link_first, tops):
    x_first, _, link_ok, _ = ends(shape)
    _, gy, _ = place_of(shape)
    lane, sub = lanes(), subs()
    swap = swap_index(lane)
    upper = sub % 2 == 1
    z = lane % E
    for c in range(NC):
        rate = rates[c * BZ : c * BZ + BZ, :]
        scale = 1.0 / (1.0 + 6.0 * rate)
        ghost = []
        for got, sent, kept, ok in ((core, core_sent, core_first, None), (link, link_sent, link_first, link_ok)):
            g0, g1, own = pair_at(got, 0, c), pair_at(got, 1, c), pair_at(sent, 0, c)
            g_rate = spread(got[FACE:, :], c)
            if ok is not None:
                g0, g1 = (tuple(jnp.where(ok, t, 0.0) for t in g) for g in (g0, g1))
                g_rate = jnp.where(ok, g_rate, 0.0)
            kept[2 * PLANE + c * BZ : 2 * PLANE + c * BZ + BZ, :] = g_rate
            ghost.append(g0)
            g_scale = 1.0 / (1.0 + 6.0 * g_rate)
            sums = inner(g0, lane, sub, swap)
            for h in range(2):
                value = (g0[h] + g_rate * (sums[h] + g1[h] + own[h])) * g_scale
                if ok is not None:
                    value = jnp.where(ok, value, 0.0)
                row = (h * NC + c) * BZ
                kept[row : row + BZ, :] = value
        low = [jnp.where(x_first, b, a) for a, b in zip(*ghost)]
        high = [jnp.where(x_first, a, b) for a, b in zip(*ghost)]
        for x in range(E):
            here = tile_at(moved, c, x)
            before = low if x == 0 else tile_at(moved, c, x - 1)
            after = high if x == E - 1 else tile_at(moved, c, x + 1)
            sums = inner(here, lane, sub, swap)
            row = (c * E + x) * BZ
            for h in range(2):
                out[h, row : row + BZ, :] = (here[h] + rate * (sums[h] + before[h] + after[h])) * scale
    every = [(h, c, k) for c in range(NC) for h in range(2) for k in range(E // 2)]
    d = []
    for h, c, k in every:
        row = (c * E + 2 * k) * BZ
        d.append(out[h, row : row + BZ, :] + out[h, row + BZ : row + 2 * BZ, :])
    d = z_differences(d, sub, upper)
    d = [t + r for t, r in zip(d, [rl(t, -E) for t in d])]
    d = [rl(t, k) for t, (_, _, k) in zip(d, every)]
    faces = {}
    for t, (h, c, k) in zip(d, every):
        faces[h, c] = t if k == 0 else jnp.where(z == k, t, faces[h, c])
    y8 = lane % 8
    source = (y8 % 4) * (2 * E) + lane // E
    picked = {key: pick_lanes(t, source) for key, t in faces.items()}
    for c in range(NC):
        top = jnp.where(y8 < 4, picked[0, c], picked[1, c])
        tops[c * BZ : c * BZ + BZ, :] = jnp.where(z // 8 == gy % 2, top, 0.0)


def coarse_plane(pair, parity, lane, sub):
    sums = []
    for t in pair:
        t = t + rl(t, -1)
        sums.append(t + rl(t, -E))
    source = (lane // E % 4) * (2 * E) + 2 * (lane % 8)
    out = jnp.where(lane < L // 2, pick_lanes(sums[0], source), pick_lanes(sums[1], source))
    return jnp.where(lane % E // 8 == sub % 2, 0.25 * out, 0.0)


def strips(low, high, x, low_lane, high_lane):
    shift = E * (x % 8)
    return (
        jnp.where(low_lane, rl(low[x // 8], -shift), 0.0),
        jnp.where(high_lane, rl(high[x // 8], L - E - shift), 0.0),
    )


def corner(extra, low_lane, high_lane):
    return jnp.where(low_lane, extra, 0.0), jnp.where(high_lane, rl(extra, L - 2 * E), 0.0)


def y_ghosts(got, ok, c):
    g0, g1, extra = pair_at(got, 0, c), pair_at(got, 1, c), extra_at(got, c)
    if ok is not None:
        g0, g1 = (tuple(jnp.where(ok, t, 0.0) for t in g) for g in (g0, g1))
        extra = jnp.where(ok, extra, 0.0)
    return g0, g1, extra


def y_first_sweep(got, sent, ok, ghost, c, lane, sub, swap):
    g0, g1, extra = ghost
    own = pair_at(sent, 0, c)
    g_rate = y_rate(got, c)
    if ok is not None:
        g_rate = jnp.where(ok, g_rate, 0.0)
    g_scale = 1.0 / (1.0 + 6.0 * g_rate)
    sums, line = inner(g0, lane, sub, swap), corner(extra, lane < E, lane >= L - E)
    values = [(g0[h] + g_rate * (sums[h] + line[h] + g1[h] + own[h])) * g_scale for h in range(2)]
    return values if ok is None else [jnp.where(ok, t, 0.0) for t in values]


def x_first_sweep(part, ok, at_low, low_line, high_line, c, low_lane, high_lane):
    g_rate = part[2 * PLANE + c * BZ : 2 * PLANE + c * BZ + BZ, :]
    g_weight = g_rate / (1.0 + 6.0 * g_rate)
    bottom = jnp.where(at_low, low_line, rl(low_line, -E))
    top = jnp.where(at_low, rl(high_line, L - E), rl(high_line, L - 2 * E))
    values = []
    for h, (line, there) in enumerate(((bottom, low_lane), (top, high_lane))):
        row = (h * NC + c) * BZ
        values.append(part[row : row + BZ, :] + g_weight * jnp.where(there, line, 0.0))
    return values if ok is None else [jnp.where(ok, t, 0.0) for t in values]


def flux_kernel(
    shape, partial, moved_rates, masks, tops, link_first, near, far, far_sent, x_link, y_far, kept, sent
):
    x_first, y_first, link_ok, far_ok = ends(shape)
    gx, gy, _ = place_of(shape)
    par_x, par_y = gx % 2, gy % 2
    lane, sub = lanes(), subs()
    swap = swap_index(lane)
    upper = sub % 2 == 1
    z = lane % E
    low_lane, high_lane = lane < E, lane >= L - E
    each = range(NC)
    rate = [moved_rates[c * BZ : c * BZ + BZ, :] for c in each]
    scale = [1.0 / (1.0 + 6.0 * r) for r in rate]
    weight = [r * q for r, q in zip(rate, scale)]
    near_g = [y_ghosts(near, None, c) for c in each]
    far_g = [y_ghosts(far, far_ok, c) for c in each]
    far_f = []
    for c in each:
        values = y_first_sweep(far, far_sent, far_ok, far_g[c], c, lane, sub, swap)
        for h in range(2):
            row = (h * NC + c) * BZ
            y_far[row : row + BZ, :] = values[h]
        far_f.append(values)
    far_r = [g[0] for g in far_g]

    def by_side(which, c):
        a, b = near_g[c][which], far_g[c][which]
        if which == 2:
            return jnp.where(y_first, b, a), jnp.where(y_first, a, b)
        return [jnp.where(y_first, q, p) for p, q in zip(a, b)], [jnp.where(y_first, p, q) for p, q in zip(a, b)]

    faces_y = []
    for c in each:
        own, own1 = pair_at(far_sent, 0, c), pair_at(far_sent, 1, c)
        sums, line = inner(own, lane, sub, swap), corner(extra_at(far_sent, c), low_lane, high_lane)
        flux = [
            far_f[c][h] - (own[h] + rate[c] * (sums[h] + line[h] + own1[h] + far_r[c][h])) * scale[c] for h in range(2)
        ]
        face = coarse_plane(flux, par_x, lane, sub) * (rate[c] * masks[BZ : 2 * BZ, :])
        faces_y.append(face + rs(face, 1))
    faces_x = []
    for c in each:
        ghost = x_first_sweep(link_first, link_ok, x_first, *by_side(2, c), c, low_lane, high_lane)
        for h in range(2):
            row = (h * NC + c) * BZ
            x_link[row : row + BZ, :] = ghost[h]
        low_r, high_r = by_side(0, c)
        at_0, at_15 = (strips(low_r, high_r, x, low_lane, high_lane) for x in (0, E - 1))
        cells_0, cells_15 = tile_at(partial, c, 0), tile_at(partial, c, E - 1)
        flux = []
        for h in range(2):
            cell = jnp.where(x_first, cells_0[h], cells_15[h])
            cell = cell + weight[c] * jnp.where(x_first, at_0[h], at_15[h])
            flux.append(ghost[h] - cell)
        face = coarse_plane(flux, par_y, lane, sub) * (rate[c] * masks[0:BZ, :])
        faces_x.append(face + rs(face, -1))
    faces_z = []
    source = (lane // E % 4) * (2 * E) + jnp.where(lane % 8 == 7, 7, 0)
    d = []
    for c in each:
        for side in by_side(0, c):
            d += [weight[c] * t for t in side]
    d = [t + r for t, r in zip(d, [rl(t, -E) for t in d])]
    d = z_differences(d, sub, upper)
    halves = []
    for c in each:
        for h in range(2):
            halves.append(jnp.where(z == 7, rl(d[4 * c + 2 + h], 7), d[4 * c + h]))
    halves = [pick_lanes(t, source) for t in halves]
    for c in each:
        add = jnp.where(lane < L // 2, halves[2 * c], halves[2 * c + 1])
        add = jnp.where((z == 8 * par_y) | (z == 8 * par_y + 7), add, 0.0)
        faces_z.append((tops[c * BZ : c * BZ + BZ, :] + add) * (0.25 * rate[c] * masks[2 * BZ :, :]))
    left = sub % 4 < 2
    for c in each:
        for h in range(2):
            outer = jnp.where(
                upper, jnp.where(par_x == h, faces_y[c], 0.0), jnp.where(par_y == h, faces_x[c], 0.0)
            )
            top = jnp.where(par_x == h, faces_z[c], 0.0)
            columns = (jnp.where(left, outer, rs(top, 2)), jnp.where(left, rs(outer, -2), top))
            row = (h * NC + c) * BZ
            kept[row : row + BZ, :] = jnp.where(y_first, columns[0], columns[1])
            sent[row : row + BZ, :] = jnp.where(y_first, columns[1], columns[0])


def half_kernel(shape, kept, got, _, mine, sent):
    gx, _, _ = place_of(shape)
    first = gx % 2 == 0
    top = subs() < 4
    for i in range(2 * NC):
        a, b = kept[i * BZ : i * BZ + BZ, :], got[i * BZ : i * BZ + BZ, :]
        rows = (jnp.where(top, a, rs(b, 4)), jnp.where(top, rs(a, 4), b))
        mine[i * BZ : i * BZ + BZ, :] = jnp.where(first, rows[0], rows[1])
        sent[i * BZ : i * BZ + BZ, :] = jnp.where(first, rows[1], rows[0])


def register_kernel(shape, mine, got, _, out):
    x_first, y_first, _, _ = ends(shape)
    sub = subs()
    for h in range(2):
        for c in range(NC):
            row = (h * NC + c) * BZ
            m, g = mine[row : row + BZ, :], got[row : row + BZ, :]
            a, b = m + rs(m, 4), g + rs(g, 4)
            s = m + g
            ab = a + b
            x0, x1 = jnp.where(x_first, a, b), jnp.where(x_first, b, a)
            y0, y1 = jnp.where(y_first, rs(s, 1), rs(s, 5)), jnp.where(y_first, rs(s, 5), rs(s, 1))
            t = jnp.where(sub == 0, x0, jnp.where(sub == 1, rs(x1, 1), rs(ab, 2)))
            t = jnp.where(sub == 2, y0, jnp.where(sub == 3, rs(y1, 1), t))
            out[0, 0, c, :, h * L : h * L + L] = t[:6]


def smooth_kernel(
    comps, shape, moved, rates, partial, core_first, near, far, near_sent, x_link, y_far, _, out, done,
    first, held, boxes, sem,
):
    done[...] = jnp.zeros((BZ, L), F32)
    x_first, y_first, _, far_ok = ends(shape)
    lane, sub = lanes(), subs()
    swap = swap_index(lane)
    low_lane, high_lane = lane < E, lane >= L - E
    copies = []
    for c in comps:
        rate = rates[c * BZ : c * BZ + BZ, :]
        scale = 1.0 / (1.0 + 6.0 * rate)
        weight = rate * scale

        def by_side(a, b, a_first):
            low = [jnp.where(a_first, q, p) for p, q in zip(a, b)]
            high = [jnp.where(a_first, p, q) for p, q in zip(a, b)]
            return low, high

        near_g, far_g = y_ghosts(near, None, c), y_ghosts(far, far_ok, c)
        (low_line,), (high_line,) = by_side(near_g[2:], far_g[2:], y_first)
        core = x_first_sweep(core_first, None, ~x_first, low_line, high_line, c, low_lane, high_lane)
        low, high = by_side(core, pair_at(x_link, 0, c), x_first)
        near_f = y_first_sweep(near, near_sent, None, near_g, c, lane, sub, swap)
        low_y, high_y = by_side(near_f, pair_at(y_far, 0, c), y_first)
        low_r, high_r = by_side(near_g[0], far_g[0], y_first)
        for x in range(E):
            edge = strips(low_r, high_r, x, low_lane, high_lane)
            row = (c * E + x) * BZ
            for h in range(2):
                first[h, row : row + BZ, :] = partial[h, row : row + BZ, :] + weight * edge[h]
        for x in range(E):
            here = tile_at(first, c, x)
            before = low if x == 0 else tile_at(first, c, x - 1)
            after = high if x == E - 1 else tile_at(first, c, x + 1)
            sums = inner(here, lane, sub, swap)
            edge = strips(low_y, high_y, x, low_lane, high_lane)
            start = tile_at(moved, c, x)
            row = (c * E + x) * BZ
            for h in range(2):
                held[h, row : row + BZ, :] = (start[h] + rate * (sums[h] + before[h] + after[h] + edge[h])) * scale
        for s in range(BZ):
            for h in range(2):
                boxes[c, s, :, h * L : h * L + L] = held[h, pl.ds(c * E * BZ + s, E, stride=BZ), :]
        copies.append(pltpu.make_async_copy(boxes.at[c], out.at[0, 0, :, c], sem.at[c]))
        copies[-1].start()
    for copy in copies:
        copy.wait()


def body(shape, fields_old, coeff_old, new_place, cf_mask):
    rows, columns = shape
    count = rows * columns
    both = ("gx", "gy")

    def swap(array, pairs):
        return lax.ppermute(array, both, pairs)

    even_pairs = [(i, i ^ 1) for i in range(count)]
    odd_pairs = [(i, (i + 1) % count if i % 2 else (i - 1) % count) for i in range(count)]
    at = lambda a, b: a * columns + b
    core_pairs = [(at(a, b), at(a ^ 1, b)) for a in range(rows) for b in range(columns)]
    link_pairs = [
        (at(a, b), at((a + 1) % rows if a % 2 else (a - 1) % rows, b)) for a in range(rows) for b in range(columns)
    ]
    far_pairs = [
        (at(a, b), at(a ^ 1, b) if b in (0, columns - 1) else at(a, b + 1 if b % 2 else b - 1))
        for a in range(rows)
        for b in range(columns)
    ]
    k = lambda f: functools.partial(f, shape)
    coeff_old = coeff_old.transpose(0, 3, 1, 2)
    cf_mask = cf_mask.transpose(0, 2, 1, 3)
    big = (2, NC * E * BZ, L)

    plane = ((2 * PLANE, L), "vmem")
    even, odd, even_rest, odd_rest, boxes, slots, rates, masks = call(
        k(pack_kernel),
        [(a, "hbm") for a in (new_place, coeff_old, cf_mask, fields_old)],
        [
            ((PARCEL, 2 * L), "vmem"),
            ((PARCEL, 2 * L), "vmem"),
            ((REST, 2 * L), "vmem"),
            ((REST, 2 * L), "vmem"),
            ((BZ, NC, E, 2 * L), "vmem"),
            ((BZ, L), "vmem"),
            ((PLANE, L), "vmem"),
            ((3 * BZ, L), "vmem"),
        ],
        [
            SM((1, 1, BZ), I32),
            SM((1, NC, 1, BZ), F32),
            SM((1, 3, 1, BZ), I32),
            pltpu.SemaphoreType.DMA((4,)),
        ],
    )
    even_got = swap(even, even_pairs)
    odd_got = swap(odd, odd_pairs)
    even_rest_got = swap(even_rest, even_pairs)
    odd_rest_got = swap(odd_rest, odd_pairs)
    stayed, rates = call(
        k(stay_kernel),
        [(a, "vmem") for a in (boxes, slots, rates)],
        [(big, "vmem"), ((PLANE, L), "vmem")],
    )
    core, link, rates = call(
        k(xsend_kernel),
        [(a, "vmem") for a in (even_got, odd_got, stayed, rates)],
        [((XFACE, L), "vmem"), ((XFACE, L), "vmem"), ((PLANE, L), "vmem")],
    )
    core_got = swap(core, core_pairs)
    link_got = swap(link, link_pairs)
    moved, near, far = call(
        k(merge_kernel),
        [(a, "vmem") for a in (odd_got, even_got, odd_rest_got, even_rest_got, stayed)],
        [(big, "vmem"), ((FACE, L), "vmem"), ((FACE, L), "vmem")],
    )
    near, far = call(
        k(ysend_kernel),
        [(a, "vmem") for a in (link_got, core_got, rates, near, far)],
        [((YFACE, L), "vmem"), ((YFACE, L), "vmem")],
    )
    near_got = swap(near, even_pairs)
    far_got = swap(far, far_pairs)
    part, core_first, link_first, tops = call(
        k(sweep_kernel),
        [(a, "vmem") for a in (moved, rates, link_got, core_got, core, link)],
        [(big, "vmem"), ((3 * PLANE, L), "vmem"), ((3 * PLANE, L), "vmem"), ((PLANE, L), "vmem")],
    )
    x_link, y_far, kept, sent = call(
        k(flux_kernel),
        [(a, "vmem") for a in (part, rates, masks, tops, link_first, near_got, far_got, far)],
        [plane] * 4,
    )
    got = swap(sent, even_pairs)

    def smooth(comps, before, aliases):
        ins = (moved, rates, part, core_first, near_got, far_got, near, x_link, y_far)
        return call(
            functools.partial(smooth_kernel, comps, shape),
            [(a, "vmem") for a in ins] + [before],
            [((1, 1, BZ, NC, E, 2 * L), "hbm"), ((BZ, L), "vmem")],
            [VM(big, F32), VM(big, F32), VM((NC, BZ, E, 2 * L), F32), pltpu.SemaphoreType.DMA((NC,))],
            aliases,
        )

    smoothed, done = smooth((0, 1, 2), (masks, "vmem"), None)
    mine, sent = call(k(half_kernel), [(kept, "vmem"), (got, "vmem"), (done, "vmem")], [plane, plane])
    got = swap(sent, core_pairs)
    smoothed, done = smooth((3, 4), (smoothed, "hbm"), {9: 0})
    (registers,) = call(
        k(register_kernel), [(mine, "vmem"), (got, "vmem"), (done, "vmem")], [((1, 1, NC, 6, 2 * L), "out")]
    )
    return smoothed, registers


def solution(mesh):
    shape = (mesh.shape["gx"], mesh.shape["gy"])
    return jax.shard_map(
        functools.partial(body, shape),
        mesh=mesh,
        in_specs=(
            P("gx", "gy", None, None, None, None),
            P("gx", "gy", None, None),
            P("gx", "gy", None),
            P("gx", "gy", None, None),
        ),
        out_specs=(P("gx", "gy", None, None, None, None), P("gx", "gy", None, None, None)),
        check_vma=False,
    )
```

```python
import functools

import jax
import jax.numpy as jnp
from jax import lax
from jax.experimental import pallas as pl
from jax.experimental.pallas import tpu as pltpu
from jax.sharding import PartitionSpec as P

NC = 5
E = 16
BZ = 8
MOVE = 2
L = 128
F32 = jnp.float32
I32 = jnp.int32

PLANE = NC * BZ
FACE = 4 * PLANE
EDGES = (0, 1, E - 2, E - 1)
AHEAD = MOVE * NC * 4
PARCEL = 48
REST = MOVE * NC * 12
XFACE = FACE + BZ
YFACE = FACE + 2 * BZ

VM = pltpu.VMEM
SM = pltpu.SMEM


def call(kernel, ins, outs, scratch=(), aliases=None, flops=1000, **kw):
    given, in_specs = [], []
    for array, space in ins:
        if space == "vmem":
            given.append(pltpu.with_memory_space_constraint(array, VM))
            in_specs.append(pl.BlockSpec(memory_space=VM))
        else:
            given.append(pltpu.with_memory_space_constraint(array, pltpu.HBM))
            in_specs.append(pl.BlockSpec(memory_space=pltpu.HBM))
    shapes, out_specs = [], []
    for shape, space in outs:
        if space == "vmem":
            shapes.append(VM(shape, F32))
            out_specs.append(pl.BlockSpec(memory_space=VM))
        else:
            shapes.append(jax.ShapeDtypeStruct(shape, F32))
            out_specs.append(pl.BlockSpec(memory_space=pltpu.HBM if space == "hbm" else VM))
    return pl.pallas_call(
        kernel,
        out_shape=shapes,
        in_specs=in_specs,
        out_specs=out_specs,
        scratch_shapes=list(scratch),
        input_output_aliases=aliases or {},
        cost_estimate=pl.CostEstimate(flops=flops, bytes_accessed=0, transcendentals=0),
        compiler_params=pltpu.CompilerParams(vmem_limit_bytes=24 * 1024 * 1024),
        **kw,
    )(*given)


def lanes():
    return lax.broadcasted_iota(I32, (BZ, L), 1)


def subs():
    return lax.broadcasted_iota(I32, (BZ, L), 0)


def rl(x, shift):
    shift %= L
    return x if shift == 0 else pltpu.roll(x, shift, 1)


def rs(x, shift):
    shift %= BZ
    return x if shift == 0 else pltpu.roll(x, shift, 0)


def pick_lanes(x, index):
    return jnp.take_along_axis(x, index, axis=1)


def place_of(mesh_shape):
    gx = lax.axis_index("gx")
    gy = lax.axis_index("gy")
    return gx, gy, gx * mesh_shape[1] + gy


def sources_of(place, owner):
    count = jnp.int32(0)
    sources = [jnp.int32(0)] * MOVE
    labels = [jnp.int32(0)] * MOVE
    for s in range(BZ):
        value = place[s]
        hit = value // BZ == owner
        for k in range(MOVE):
            taken = hit & (count == k)
            sources[k] = jnp.where(taken, s, sources[k])
            labels[k] = jnp.where(taken, value % BZ + 1, labels[k])
        count = count + hit.astype(I32)
    return sources, labels


def fill_rest(rest, boxes, sources):
    for k in range(MOVE):
        for c in range(NC):
            box = k * NC + c
            rest[12 * box : 12 * box + 12, :] = boxes[sources[k], c, 2 : E - 2]


def pack_kernel(
    shape, place_hbm, coeff_hbm, mask_hbm, fields_hbm, even, odd, even_rest, odd_rest, boxes, slots, rates, masks,
    place_s, coeff, mask, sem,
):
    pairs = ((fields_hbm.at[0, 0], boxes), (place_hbm, place_s), (coeff_hbm, coeff), (mask_hbm, mask))
    copies = [pltpu.make_async_copy(a, b, sem.at[i]) for i, (a, b) in enumerate(pairs)]
    for copy in copies:
        copy.start()
    _, _, me = place_of(shape)
    ahead = 1 - 2 * (me % 2)
    lane = lax.broadcasted_iota(I32, (1, L), 1)
    for copy in copies[1:]:
        copy.wait()
    place = [place_s[0, 0, s] for s in range(BZ)]
    chosen = [sources_of(place, me + ahead), sources_of(place, me - ahead)]
    for out, (sources, labels) in zip((even, odd), chosen):
        out[AHEAD:PARCEL, :] = jnp.zeros((PARCEL - AHEAD, 2 * L), F32)
        for k in range(MOVE):
            out[AHEAD + k : AHEAD + k + 1, L:] = jnp.full((1, L), labels[k].astype(F32), F32)
            line = jnp.zeros((1, L), F32)
            for c in range(NC):
                line = jnp.where(lane == c, coeff[0, c, 0, sources[k]], line)
            out[AHEAD + k : AHEAD + k + 1, :L] = line
    for s in range(BZ):
        label = jnp.where(place[s] // BZ == me, place[s] % BZ + 1, 0)
        slots[s : s + 1, :] = jnp.full((1, L), label.astype(F32), F32)
        for c in range(NC):
            rates[s * NC + c : s * NC + c + 1, :] = jnp.full((1, L), coeff[0, c, 0, s], F32)
        for d in range(3):
            masks[d * BZ + s : d * BZ + s + 1, :] = jnp.full((1, L), mask[0, d, 0, s].astype(F32), F32)
    copies[0].wait()
    for out, rest, (sources, _) in zip((even, odd), (even_rest, odd_rest), chosen):
        for k in range(MOVE):
            for c in range(NC):
                box = k * NC + c
                out[4 * box : 4 * box + 2, :] = boxes[sources[k], c, :2]
                out[4 * box + 2 : 4 * box + 4, :] = boxes[sources[k], c, E - 2 :]
                rest[12 * box : 12 * box + 12, :] = boxes[sources[k], c, 2 : E - 2]


def stay_kernel(shape, boxes, slots, old_rates, moved, rates):
    label = (subs() + 1).astype(F32)
    found = [slots[s : s + 1, :] == label for s in range(BZ)]
    for c in range(NC):
        tile = jnp.zeros((BZ, L), F32)
        for s in range(BZ):
            tile = jnp.where(found[s], old_rates[s * NC + c : s * NC + c + 1, :], tile)
        rates[c * BZ : c * BZ + BZ, :] = tile
        for x in range(E):
            row = (c * E + x) * BZ
            for h in range(2):
                tile = jnp.zeros((BZ, L), F32)
                for s in range(BZ):
                    tile = jnp.where(found[s], boxes[s, c, x : x + 1, h * L : h * L + L], tile)
                moved[h, row : row + BZ, :] = tile


def arrivals(even, odd):
    sub = subs()
    found = []
    for parcel in (even, odd):
        for k in range(MOVE):
            label = parcel[AHEAD + k : AHEAD + k + 1, L:]
            found.append((parcel, k, label == (sub + 1).astype(F32)))
    return found


def merged(found, moved, c, x, h, rests=None):
    row = (c * E + x) * BZ
    tile = moved[h, row : row + BZ, :]
    for i, (parcel, k, hit) in enumerate(found):
        if x in EDGES:
            source, at = parcel, (k * NC + c) * 4 + EDGES.index(x)
        else:
            source, at = rests[i // MOVE], (k * NC + c) * 12 + x - 2
        tile = jnp.where(hit, source[at : at + 1, h * L : h * L + L], tile)
    return tile


def spread(tile, lane):
    return pick_lanes(tile, jnp.full((BZ, L), lane, I32))


def plane_row(layer, h, c):
    return ((layer * 2 + h) * NC + c) * BZ


def xsend_kernel(shape, even, odd, moved, rates, core, link, all_rates):
    gx, _, _ = place_of(shape)
    first = gx % 2 == 0
    found = arrivals(even, odd)
    lane = lanes()
    together = jnp.zeros((BZ, L), F32)
    for c in range(NC):
        tile = rates[c * BZ : c * BZ + BZ, :]
        for parcel, k, hit in found:
            line = jnp.broadcast_to(parcel[AHEAD + k : AHEAD + k + 1, :L], (BZ, L))
            tile = jnp.where(hit, spread(line, c), tile)
        all_rates[c * BZ : c * BZ + BZ, :] = tile
        together = jnp.where(lane % L == c, tile, together)
        for layer in range(2):
            for h in range(2):
                low = merged(found, moved, c, layer, h)
                high = merged(found, moved, c, E - 1 - layer, h)
                at = plane_row(layer, h, c)
                core[at : at + BZ, :] = jnp.where(first, high, low)
                link[at : at + BZ, :] = jnp.where(first, low, high)
    core[FACE:, :] = together
    link[FACE:, :] = together


def merge_kernel(shape, even, odd, even_rest, odd_rest, moved, out, near, far):
    _, gy, _ = place_of(shape)
    first = gy % 2 == 0
    found = arrivals(even, odd)
    lane = lanes()
    for c in range(NC):
        low = [[None, None], [None, None]]
        high = [[None, None], [None, None]]
        for x in range(E):
            row = (c * E + x) * BZ
            at = L // 8 * (x % 8)
            here = lane // E == x % 8
            half = x // 8
            for h in range(2):
                tile = merged(found, moved, c, x, h, (even_rest, odd_rest))
                out[h, row : row + BZ, :] = tile
                for layer in range(2):
                    keep, start = ((low, E * layer) if h == 0 else (high, L - E - E * layer))
                    strip = rl(tile, at - start)
                    old = keep[layer][half]
                    keep[layer][half] = strip if old is None else jnp.where(here, strip, old)
        for layer in range(2):
            for h in range(2):
                at = plane_row(layer, h, c)
                near[at : at + BZ, :] = jnp.where(first, high[layer][h], low[layer][h])
                far[at : at + BZ, :] = jnp.where(first, low[layer][h], high[layer][h])


def ends(shape):
    gx, gy, _ = place_of(shape)
    x_first, y_first = gx % 2 == 0, gy % 2 == 0
    link_ok = jnp.where(x_first, gx > 0, gx < shape[0] - 1)
    far_ok = jnp.where(y_first, gy > 0, gy < shape[1] - 1)
    return x_first, y_first, link_ok, far_ok


def ysend_kernel(shape, link, core, rates, near, far, near_out, far_out):
    x_first, y_first, link_ok, _ = ends(shape)
    lane = lanes()
    near_out[:FACE, :] = near[...]
    far_out[:FACE, :] = far[...]
    bottoms = [jnp.zeros((BZ, L), F32)] * 2
    tops = [jnp.zeros((BZ, L), F32)] * 2
    for c in range(NC):
        lines = []
        for h in range(2):
            at = plane_row(0, h, c)
            a = core[at : at + BZ, :]
            b = jnp.where(link_ok, link[at : at + BZ, :], 0.0)
            lines.append((jnp.where(x_first, b, a), jnp.where(x_first, a, b)))
        i, at = divmod(c, 4)
        at *= 2 * E
        low = (lane >= at) & (lane < at + E)
        high = (lane >= at + E) & (lane < at + 2 * E)
        bottoms[i] = jnp.where(low, rl(lines[0][0], at), jnp.where(high, rl(lines[0][1], at + E), bottoms[i]))
        tops[i] = jnp.where(low, rl(lines[1][0], at + E), jnp.where(high, rl(lines[1][1], at + 2 * E), tops[i]))
        rate = rates[c * BZ : c * BZ + BZ, :]
        bottoms[1] = jnp.where(lane == L // 2 + c, rate, bottoms[1])
        tops[1] = jnp.where(lane == L // 2 + c, rate, tops[1])
    for i in range(2):
        at = FACE + i * BZ
        near_out[at : at + BZ, :] = jnp.where(y_first, tops[i], bottoms[i])
        far_out[at : at + BZ, :] = jnp.where(y_first, bottoms[i], tops[i])


def extra_at(ref, c):
    i, at = divmod(c, 4)
    return rl(ref[FACE + i * BZ : FACE + i * BZ + BZ, :], -2 * E * at)


def y_rate(ref, c):
    return spread(ref[FACE + BZ : FACE + 2 * BZ, :], L // 2 + c)


def z_parts(x, lane, sub, swap):
    z = lane % E
    down = jnp.where(sub == 0, 0.0, rs(x, 1))
    up = jnp.where(sub == BZ - 1, 0.0, rs(x, -1))
    ends_ = pick_lanes(jnp.where(z == E - 1, down, up), swap)
    return jnp.where(z == 0, ends_, rl(x, 1)) + jnp.where(z == E - 1, ends_, rl(x, -1))


def swap_index(lane):
    z = lane % E
    return jnp.where(z == 0, lane + E - 1, jnp.where(z == E - 1, lane - E + 1, lane))


def inner(pair, lane, sub, swap):
    a, b = pair
    a1, b1, a2, b2 = rl(a, E), rl(b, E), rl(a, -E), rl(b, -E)
    low, high = lane < E, lane >= L - E
    first = jnp.where(low, 0.0, a1) + jnp.where(high, b2, a2) + z_parts(a, lane, sub, swap)
    second = jnp.where(low, a1, b1) + jnp.where(high, 0.0, b2) + z_parts(b, lane, sub, swap)
    return first, second


def pair_at(ref, layer, c):
    return tuple(ref[plane_row(layer, h, c) : plane_row(layer, h, c) + BZ, :] for h in range(2))


def tile_at(ref, c, x):
    row = (c * E + x) * BZ
    return tuple(ref[h, row : row + BZ, :] for h in range(2))


def z_differences(tiles, sub, upper):
    down = [jnp.where(sub == 0, 0.0, t) for t in [rs(t, 1) for t in tiles]]
    up = [jnp.where(sub == BZ - 1, 0.0, t) for t in [rs(t, -1) for t in tiles]]
    high = [rl(t, 1 - E) for t in [jnp.where(upper, t, d) for t, d in zip(tiles, down)]]
    return [jnp.where(upper, u - g, g - t) for g, u, t in zip(high, up, tiles)]


def sweep_kernel(shape, moved, rates, link, core, core_sent, link_sent, out, core_first, link_first, tops):
    x_first, _, link_ok, _ = ends(shape)
    _, gy, _ = place_of(shape)
    lane, sub = lanes(), subs()
    swap = swap_index(lane)
    upper = sub % 2 == 1
    z = lane % E
    for c in range(NC):
        rate = rates[c * BZ : c * BZ + BZ, :]
        scale = 1.0 / (1.0 + 6.0 * rate)
        ghost = []
        for got, sent, kept, ok in ((core, core_sent, core_first, None), (link, link_sent, link_first, link_ok)):
            g0, g1, own = pair_at(got, 0, c), pair_at(got, 1, c), pair_at(sent, 0, c)
            g_rate = spread(got[FACE:, :], c)
            if ok is not None:
                g0, g1 = (tuple(jnp.where(ok, t, 0.0) for t in g) for g in (g0, g1))
                g_rate = jnp.where(ok, g_rate, 0.0)
            kept[2 * PLANE + c * BZ : 2 * PLANE + c * BZ + BZ, :] = g_rate
            ghost.append(g0)
            g_scale = 1.0 / (1.0 + 6.0 * g_rate)
            sums = inner(g0, lane, sub, swap)
            for h in range(2):
                value = (g0[h] + g_rate * (sums[h] + g1[h] + own[h])) * g_scale
                if ok is not None:
                    value = jnp.where(ok, value, 0.0)
                row = (h * NC + c) * BZ
                kept[row : row + BZ, :] = value
        low = [jnp.where(x_first, b, a) for a, b in zip(*ghost)]
        high = [jnp.where(x_first, a, b) for a, b in zip(*ghost)]
        for x in range(E):
            here = tile_at(moved, c, x)
            before = low if x == 0 else tile_at(moved, c, x - 1)
            after = high if x == E - 1 else tile_at(moved, c, x + 1)
            sums = inner(here, lane, sub, swap)
            row = (c * E + x) * BZ
            for h in range(2):
                out[h, row : row + BZ, :] = (here[h] + rate * (sums[h] + before[h] + after[h])) * scale
    every = [(h, c, k) for c in range(NC) for h in range(2) for k in range(E // 2)]
    d = []
    for h, c, k in every:
        row = (c * E + 2 * k) * BZ
        d.append(out[h, row : row + BZ, :] + out[h, row + BZ : row + 2 * BZ, :])
    d = z_differences(d, sub, upper)
    d = [t + r for t, r in zip(d, [rl(t, -E) for t in d])]
    d = [rl(t, k) for t, (_, _, k) in zip(d, every)]
    faces = {}
    for t, (h, c, k) in zip(d, every):
        faces[h, c] = t if k == 0 else jnp.where(z == k, t, faces[h, c])
    y8 = lane % 8
    source = (y8 % 4) * (2 * E) + lane // E
    picked = {key: pick_lanes(t, source) for key, t in faces.items()}
    for c in range(NC):
        top = jnp.where(y8 < 4, picked[0, c], picked[1, c])
        tops[c * BZ : c * BZ + BZ, :] = jnp.where(z // 8 == gy % 2, top, 0.0)


def coarse_plane(pair, parity, lane, sub):
    sums = []
    for t in pair:
        t = t + rl(t, -1)
        sums.append(t + rl(t, -E))
    source = (lane // E % 4) * (2 * E) + 2 * (lane % 8)
    out = jnp.where(lane < L // 2, pick_lanes(sums[0], source), pick_lanes(sums[1], source))
    return jnp.where(lane % E // 8 == sub % 2, 0.25 * out, 0.0)


def strips(low, high, x, low_lane, high_lane):
    shift = E * (x % 8)
    return (
        jnp.where(low_lane, rl(low[x // 8], -shift), 0.0),
        jnp.where(high_lane, rl(high[x // 8], L - E - shift), 0.0),
    )


def corner(extra, low_lane, high_lane):
    return jnp.where(low_lane, extra, 0.0), jnp.where(high_lane, rl(extra, L - 2 * E), 0.0)


def y_ghosts(got, ok, c):
    g0, g1, extra = pair_at(got, 0, c), pair_at(got, 1, c), extra_at(got, c)
    if ok is not None:
        g0, g1 = (tuple(jnp.where(ok, t, 0.0) for t in g) for g in (g0, g1))
        extra = jnp.where(ok, extra, 0.0)
    return g0, g1, extra


def y_first_sweep(got, sent, ok, ghost, c, lane, sub, swap):
    g0, g1, extra = ghost
    own = pair_at(sent, 0, c)
    g_rate = y_rate(got, c)
    if ok is not None:
        g_rate = jnp.where(ok, g_rate, 0.0)
    g_scale = 1.0 / (1.0 + 6.0 * g_rate)
    sums, line = inner(g0, lane, sub, swap), corner(extra, lane < E, lane >= L - E)
    values = [(g0[h] + g_rate * (sums[h] + line[h] + g1[h] + own[h])) * g_scale for h in range(2)]
    return values if ok is None else [jnp.where(ok, t, 0.0) for t in values]


def x_first_sweep(part, ok, at_low, low_line, high_line, c, low_lane, high_lane):
    g_rate = part[2 * PLANE + c * BZ : 2 * PLANE + c * BZ + BZ, :]
    g_weight = g_rate / (1.0 + 6.0 * g_rate)
    bottom = jnp.where(at_low, low_line, rl(low_line, -E))
    top = jnp.where(at_low, rl(high_line, L - E), rl(high_line, L - 2 * E))
    values = []
    for h, (line, there) in enumerate(((bottom, low_lane), (top, high_lane))):
        row = (h * NC + c) * BZ
        values.append(part[row : row + BZ, :] + g_weight * jnp.where(there, line, 0.0))
    return values if ok is None else [jnp.where(ok, t, 0.0) for t in values]


def flux_kernel(
    shape, partial, moved_rates, masks, tops, link_first, far, near, far_sent, _, y_far, kept, sent
):
    x_first, y_first, link_ok, far_ok = ends(shape)
    gx, gy, _ = place_of(shape)
    par_x, par_y = gx % 2, gy % 2
    lane, sub = lanes(), subs()
    swap = swap_index(lane)
    upper = sub % 2 == 1
    z = lane % E
    low_lane, high_lane = lane < E, lane >= L - E
    each = range(NC)
    rate = [moved_rates[c * BZ : c * BZ + BZ, :] for c in each]
    scale = [1.0 / (1.0 + 6.0 * r) for r in rate]
    weight = [r * q for r, q in zip(rate, scale)]
    near_g = [y_ghosts(near, None, c) for c in each]
    far_g = [y_ghosts(far, far_ok, c) for c in each]
    far_f = []
    for c in each:
        values = y_first_sweep(far, far_sent, far_ok, far_g[c], c, lane, sub, swap)
        for h in range(2):
            row = (h * NC + c) * BZ
            y_far[row : row + BZ, :] = values[h]
        far_f.append(values)
    far_r = [g[0] for g in far_g]

    def by_side(which, c):
        a, b = near_g[c][which], far_g[c][which]
        if which == 2:
            return jnp.where(y_first, b, a), jnp.where(y_first, a, b)
        return [jnp.where(y_first, q, p) for p, q in zip(a, b)], [jnp.where(y_first, p, q) for p, q in zip(a, b)]

    faces_y = []
    for c in each:
        own, own1 = pair_at(far_sent, 0, c), pair_at(far_sent, 1, c)
        sums, line = inner(own, lane, sub, swap), corner(extra_at(far_sent, c), low_lane, high_lane)
        flux = [
            far_f[c][h] - (own[h] + rate[c] * (sums[h] + line[h] + own1[h] + far_r[c][h])) * scale[c] for h in range(2)
        ]
        face = coarse_plane(flux, par_x, lane, sub) * (rate[c] * masks[BZ : 2 * BZ, :])
        faces_y.append(face + rs(face, 1))
    faces_x = []
    for c in each:
        ghost = x_first_sweep(link_first, link_ok, x_first, *by_side(2, c), c, low_lane, high_lane)
        low_r, high_r = by_side(0, c)
        at_0, at_15 = (strips(low_r, high_r, x, low_lane, high_lane) for x in (0, E - 1))
        cells_0, cells_15 = tile_at(partial, c, 0), tile_at(partial, c, E - 1)
        flux = []
        for h in range(2):
            cell = jnp.where(x_first, cells_0[h], cells_15[h])
            cell = cell + weight[c] * jnp.where(x_first, at_0[h], at_15[h])
            flux.append(ghost[h] - cell)
        face = coarse_plane(flux, par_y, lane, sub) * (rate[c] * masks[0:BZ, :])
        faces_x.append(face + rs(face, -1))
    faces_z = []
    source = (lane // E % 4) * (2 * E) + jnp.where(lane % 8 == 7, 7, 0)
    d = []
    for c in each:
        for side in by_side(0, c):
            d += [weight[c] * t for t in side]
    d = [t + r for t, r in zip(d, [rl(t, -E) for t in d])]
    d = z_differences(d, sub, upper)
    halves = []
    for c in each:
        for h in range(2):
            halves.append(jnp.where(z == 7, rl(d[4 * c + 2 + h], 7), d[4 * c + h]))
    halves = [pick_lanes(t, source) for t in halves]
    for c in each:
        add = jnp.where(lane < L // 2, halves[2 * c], halves[2 * c + 1])
        add = jnp.where((z == 8 * par_y) | (z == 8 * par_y + 7), add, 0.0)
        faces_z.append((tops[c * BZ : c * BZ + BZ, :] + add) * (0.25 * rate[c] * masks[2 * BZ :, :]))
    left = sub % 4 < 2
    for c in each:
        for h in range(2):
            outer = jnp.where(
                upper, jnp.where(par_x == h, faces_y[c], 0.0), jnp.where(par_y == h, faces_x[c], 0.0)
            )
            top = jnp.where(par_x == h, faces_z[c], 0.0)
            columns = (jnp.where(left, outer, rs(top, 2)), jnp.where(left, rs(outer, -2), top))
            row = (h * NC + c) * BZ
            kept[row : row + BZ, :] = jnp.where(y_first, columns[0], columns[1])
            sent[row : row + BZ, :] = jnp.where(y_first, columns[1], columns[0])


def half_kernel(shape, kept, got, _, mine, sent):
    gx, _, _ = place_of(shape)
    first = gx % 2 == 0
    top = subs() < 4
    for i in range(2 * NC):
        a, b = kept[i * BZ : i * BZ + BZ, :], got[i * BZ : i * BZ + BZ, :]
        rows = (jnp.where(top, a, rs(b, 4)), jnp.where(top, rs(a, 4), b))
        mine[i * BZ : i * BZ + BZ, :] = jnp.where(first, rows[0], rows[1])
        sent[i * BZ : i * BZ + BZ, :] = jnp.where(first, rows[1], rows[0])


def register_kernel(shape, mine, got, out):
    x_first, y_first, _, _ = ends(shape)
    sub = subs()
    for h in range(2):
        for c in range(NC):
            row = (h * NC + c) * BZ
            m, g = mine[row : row + BZ, :], got[row : row + BZ, :]
            a, b = m + rs(m, 4), g + rs(g, 4)
            s = m + g
            ab = a + b
            x0, x1 = jnp.where(x_first, a, b), jnp.where(x_first, b, a)
            y0, y1 = jnp.where(y_first, rs(s, 1), rs(s, 5)), jnp.where(y_first, rs(s, 5), rs(s, 1))
            t = jnp.where(sub == 0, x0, jnp.where(sub == 1, rs(x1, 1), rs(ab, 2)))
            t = jnp.where(sub == 2, y0, jnp.where(sub == 3, rs(y1, 1), t))
            out[0, 0, c, :, h * L : h * L + L] = t[:6]


def second_kernel(shape, moved, rates, partial, core_first, link_first, out):
    x_first, _, _, _ = ends(shape)
    lane, sub = lanes(), subs()
    swap = swap_index(lane)
    for c in range(NC):
        rate = rates[c * BZ : c * BZ + BZ, :]
        core, link = pair_at(core_first, 0, c), pair_at(link_first, 0, c)
        low = [jnp.where(x_first, b, a) for a, b in zip(core, link)]
        high = [jnp.where(x_first, a, b) for a, b in zip(core, link)]
        for x in range(E):
            here = tile_at(partial, c, x)
            before = low if x == 0 else tile_at(partial, c, x - 1)
            after = high if x == E - 1 else tile_at(partial, c, x + 1)
            sums = inner(here, lane, sub, swap)
            start = tile_at(moved, c, x)
            row = (c * E + x) * BZ
            for h in range(2):
                out[h, row : row + BZ, :] = start[h] + rate * (sums[h] + before[h] + after[h])


def smooth_kernel(
    shape, rates, partial, core_first, link_first, far, near, near_sent, y_far, out, done, planes, held, boxes, sem
):
    done[...] = jnp.zeros((BZ, L), F32)
    x_first, y_first, _, far_ok = ends(shape)
    lane, sub = lanes(), subs()
    swap = swap_index(lane)
    low_lane, high_lane = lane < E, lane >= L - E

    def by_side(a, b, a_first):
        low = [jnp.where(a_first, q, p) for p, q in zip(a, b)]
        high = [jnp.where(a_first, p, q) for p, q in zip(a, b)]
        return low, high

    for c in range(NC):
        rate = rates[c * BZ : c * BZ + BZ, :]
        weight = rate / (1.0 + 6.0 * rate)
        near_g, far_g = y_ghosts(near, None, c), y_ghosts(far, far_ok, c)
        near_f = y_first_sweep(near, near_sent, None, near_g, c, lane, sub, swap)
        ghosts_f = by_side(near_f, pair_at(y_far, 0, c), y_first)
        ghosts_r = by_side(near_g[0], far_g[0], y_first)
        lines = by_side(near_g[2:], far_g[2:], y_first)
        x_rates = [ref[2 * PLANE + c * BZ : 2 * PLANE + c * BZ + BZ, :] for ref in (core_first, link_first)]
        x_weights = [t / (1.0 + 6.0 * t) for t in x_rates]
        (low_w,), (high_w,) = by_side(x_weights[:1], x_weights[1:], x_first)
        for side in range(2):
            added = [weight * t for t in ghosts_r[side]]
            (line,) = lines[side]
            sums = inner(added, lane, sub, swap)
            ends_ = (jnp.where(low_lane, low_w * line, 0.0), jnp.where(high_lane, high_w * rl(line, L - 2 * E), 0.0))
            for h in range(2):
                row = ((side * 2 + h) * NC + c) * BZ
                planes[0, row : row + BZ, :] = rate * (sums[h] + ends_[h] + ghosts_f[side][h])
                planes[1, row : row + BZ, :] = rate * added[h]
    next_low = (lane >= E) & (lane < 2 * E)
    next_high = (lane >= L - 2 * E) & (lane < L - E)
    copies = []
    for c in range(NC):
        rate = rates[c * BZ : c * BZ + BZ, :]
        scale = 1.0 / (1.0 + 6.0 * rate)
        for x in range(E):
            row = (c * E + x) * BZ
            shift = E * (x % 8)
            for h, (here, there, at) in enumerate(((low_lane, next_low, 0), (high_lane, next_high, L - E))):
                plane = ((h * 2 + x // 8) * NC + c) * BZ
                first = rl(planes[0, plane : plane + BZ, :], at - shift)
                second = rl(planes[1, plane : plane + BZ, :], (at - E if h else E) - shift)
                add = jnp.where(here, first, jnp.where(there, second, 0.0))
                held[h, row : row + BZ, :] = (partial[h, row : row + BZ, :] + add) * scale
        for s in range(BZ):
            for h in range(2):
                boxes[c, s, :, h * L : h * L + L] = held[h, pl.ds(c * E * BZ + s, E, stride=BZ), :]
        copies.append(pltpu.make_async_copy(boxes.at[c], out.at[0, 0, :, c], sem.at[c]))
        copies[-1].start()
    for copy in copies:
        copy.wait()


def body(shape, fields_old, coeff_old, new_place, cf_mask):
    rows, columns = shape
    count = rows * columns
    both = ("gx", "gy")

    def swap(array, pairs):
        return lax.ppermute(array, both, pairs)

    even_pairs = [(i, i ^ 1) for i in range(count)]
    odd_pairs = [(i, (i + 1) % count if i % 2 else (i - 1) % count) for i in range(count)]
    at = lambda a, b: a * columns + b
    core_pairs = [(at(a, b), at(a ^ 1, b)) for a in range(rows) for b in range(columns)]
    link_pairs = [
        (at(a, b), at((a + 1) % rows if a % 2 else (a - 1) % rows, b)) for a in range(rows) for b in range(columns)
    ]
    far_pairs = [
        (at(a, b), at(a ^ 1, b) if b in (0, columns - 1) else at(a, b + 1 if b % 2 else b - 1))
        for a in range(rows)
        for b in range(columns)
    ]
    k = lambda f: functools.partial(f, shape)
    coeff_old = coeff_old.transpose(0, 3, 1, 2)
    cf_mask = cf_mask.transpose(0, 2, 1, 3)
    big = (2, NC * E * BZ, L)

    plane = ((2 * PLANE, L), "vmem")
    even, odd, even_rest, odd_rest, boxes, slots, rates, masks = call(
        k(pack_kernel),
        [(a, "hbm") for a in (new_place, coeff_old, cf_mask, fields_old)],
        [
            ((PARCEL, 2 * L), "vmem"),
            ((PARCEL, 2 * L), "vmem"),
            ((REST, 2 * L), "vmem"),
            ((REST, 2 * L), "vmem"),
            ((BZ, NC, E, 2 * L), "vmem"),
            ((BZ, L), "vmem"),
            ((PLANE, L), "vmem"),
            ((3 * BZ, L), "vmem"),
        ],
        [
            SM((1, 1, BZ), I32),
            SM((1, NC, 1, BZ), F32),
            SM((1, 3, 1, BZ), I32),
            pltpu.SemaphoreType.DMA((4,)),
        ],
    )
    even_got = swap(even, even_pairs)
    odd_got = swap(odd, odd_pairs)
    even_rest_got = swap(even_rest, even_pairs)
    odd_rest_got = swap(odd_rest, odd_pairs)
    stayed, rates = call(
        k(stay_kernel),
        [(a, "vmem") for a in (boxes, slots, rates)],
        [(big, "vmem"), ((PLANE, L), "vmem")],
    )
    core, link, rates = call(
        k(xsend_kernel),
        [(a, "vmem") for a in (even_got, odd_got, stayed, rates)],
        [((XFACE, L), "vmem"), ((XFACE, L), "vmem"), ((PLANE, L), "vmem")],
    )
    core_got = swap(core, core_pairs)
    link_got = swap(link, link_pairs)
    moved, near, far = call(
        k(merge_kernel),
        [(a, "vmem") for a in (even_got, odd_got, even_rest_got, odd_rest_got, stayed)],
        [(big, "vmem"), ((FACE, L), "vmem"), ((FACE, L), "vmem")],
    )
    near, far = call(
        k(ysend_kernel),
        [(a, "vmem") for a in (link_got, core_got, rates, near, far)],
        [((YFACE, L), "vmem"), ((YFACE, L), "vmem")],
    )
    near_got = swap(near, even_pairs)
    far_got = swap(far, far_pairs)
    part, core_first, link_first, tops = call(
        k(sweep_kernel),
        [(a, "vmem") for a in (moved, rates, link_got, core_got, core, link)],
        [(big, "vmem"), ((3 * PLANE, L), "vmem"), ((3 * PLANE, L), "vmem"), ((PLANE, L), "vmem")],
    )
    (second,) = call(
        k(second_kernel),
        [(a, "vmem") for a in (moved, rates, part, core_first, link_first)],
        [(big, "vmem")],
    )
    y_far, kept, sent = call(
        k(flux_kernel),
        [(a, "vmem") for a in (part, rates, masks, tops, link_first, far_got, near_got, far, second)],
        [plane] * 3,
    )
    got = swap(sent, even_pairs)

    smoothed, done = call(
        k(smooth_kernel),
        [(a, "vmem") for a in (rates, second, core_first, link_first, far_got, near_got, near, y_far)],
        [((1, 1, BZ, NC, E, 2 * L), "hbm"), ((BZ, L), "vmem")],
        [
            VM((2, 4 * PLANE, L), F32),
            VM(big, F32),
            VM((NC, BZ, E, 2 * L), F32),
            pltpu.SemaphoreType.DMA((NC,)),
        ],
    )
    mine, sent = call(k(half_kernel), [(kept, "vmem"), (got, "vmem"), (done, "vmem")], [plane, plane])
    got = swap(sent, core_pairs)
    (registers,) = call(
        k(register_kernel), [(mine, "vmem"), (got, "vmem")], [((1, 1, NC, 6, 2 * L), "out")]
    )
    return smoothed, registers


def solution(mesh):
    shape = (mesh.shape["gx"], mesh.shape["gy"])
    return jax.shard_map(
        functools.partial(body, shape),
        mesh=mesh,
        in_specs=(
            P("gx", "gy", None, None, None, None),
            P("gx", "gy", None, None),
            P("gx", "gy", None),
            P("gx", "gy", None, None),
        ),
        out_specs=(P("gx", "gy", None, None, None, None), P("gx", "gy", None, None, None)),
        check_vma=False,
    )
```

```python
import functools

import jax
import jax.numpy as jnp
from jax import lax
from jax.experimental import pallas as pl
from jax.experimental.pallas import tpu as pltpu
from jax.sharding import PartitionSpec as P

NC = 5
E = 16
BZ = 8
MOVE = 2
L = 128
F32 = jnp.float32
I32 = jnp.int32

PLANE = NC * BZ
FACE = 4 * PLANE
EDGES = (0, 1, E - 2, E - 1)
AHEAD = MOVE * NC * 4
PARCEL = 48
REST = MOVE * NC * 12
XFACE = FACE + BZ
YFACE = FACE + 2 * BZ

VM = pltpu.VMEM
SM = pltpu.SMEM


def call(kernel, ins, outs, scratch=(), aliases=None, flops=1000, **kw):
    given, in_specs = [], []
    for array, space in ins:
        if space == "vmem":
            given.append(pltpu.with_memory_space_constraint(array, VM))
            in_specs.append(pl.BlockSpec(memory_space=VM))
        else:
            given.append(pltpu.with_memory_space_constraint(array, pltpu.HBM))
            in_specs.append(pl.BlockSpec(memory_space=pltpu.HBM))
    shapes, out_specs = [], []
    for shape, space in outs:
        if space == "vmem":
            shapes.append(VM(shape, F32))
            out_specs.append(pl.BlockSpec(memory_space=VM))
        else:
            shapes.append(jax.ShapeDtypeStruct(shape, F32))
            out_specs.append(pl.BlockSpec(memory_space=pltpu.HBM if space == "hbm" else VM))
    return pl.pallas_call(
        kernel,
        out_shape=shapes,
        in_specs=in_specs,
        out_specs=out_specs,
        scratch_shapes=list(scratch),
        input_output_aliases=aliases or {},
        cost_estimate=pl.CostEstimate(flops=flops, bytes_accessed=0, transcendentals=0),
        compiler_params=pltpu.CompilerParams(vmem_limit_bytes=24 * 1024 * 1024),
        **kw,
    )(*given)


def lanes():
    return lax.broadcasted_iota(I32, (BZ, L), 1)


def subs():
    return lax.broadcasted_iota(I32, (BZ, L), 0)


def rl(x, shift):
    shift %= L
    return x if shift == 0 else pltpu.roll(x, shift, 1)


def rs(x, shift):
    shift %= BZ
    return x if shift == 0 else pltpu.roll(x, shift, 0)


def pick_lanes(x, index):
    return jnp.take_along_axis(x, index, axis=1)


def place_of(mesh_shape):
    gx = lax.axis_index("gx")
    gy = lax.axis_index("gy")
    return gx, gy, gx * mesh_shape[1] + gy


def sources_of(place, owner):
    count = jnp.int32(0)
    sources = [jnp.int32(0)] * MOVE
    labels = [jnp.int32(0)] * MOVE
    for s in range(BZ):
        value = place[s]
        hit = value // BZ == owner
        for k in range(MOVE):
            taken = hit & (count == k)
            sources[k] = jnp.where(taken, s, sources[k])
            labels[k] = jnp.where(taken, value % BZ + 1, labels[k])
        count = count + hit.astype(I32)
    return sources, labels


def fill_rest(rest, boxes, sources):
    for k in range(MOVE):
        for c in range(NC):
            box = k * NC + c
            rest[12 * box : 12 * box + 12, :] = boxes[sources[k], c, 2 : E - 2]


def pack_kernel(
    shape, place_hbm, coeff_hbm, mask_hbm, fields_hbm, even, odd, even_rest, odd_rest, boxes, slots, rates, masks,
    place_s, coeff, mask, sem,
):
    pairs = ((fields_hbm.at[0, 0], boxes), (place_hbm, place_s), (coeff_hbm, coeff), (mask_hbm, mask))
    copies = [pltpu.make_async_copy(a, b, sem.at[i]) for i, (a, b) in enumerate(pairs)]
    for copy in copies:
        copy.start()
    _, _, me = place_of(shape)
    ahead = 1 - 2 * (me % 2)
    lane = lax.broadcasted_iota(I32, (1, L), 1)
    for copy in copies[1:]:
        copy.wait()
    place = [place_s[0, 0, s] for s in range(BZ)]
    chosen = [sources_of(place, me + ahead), sources_of(place, me - ahead)]
    for out, (sources, labels) in zip((even, odd), chosen):
        out[AHEAD:PARCEL, :] = jnp.zeros((PARCEL - AHEAD, 2 * L), F32)
        for k in range(MOVE):
            out[AHEAD + k : AHEAD + k + 1, L:] = jnp.full((1, L), labels[k].astype(F32), F32)
            line = jnp.zeros((1, L), F32)
            for c in range(NC):
                line = jnp.where(lane == c, coeff[0, c, 0, sources[k]], line)
            out[AHEAD + k : AHEAD + k + 1, :L] = line
    for s in range(BZ):
        label = jnp.where(place[s] // BZ == me, place[s] % BZ + 1, 0)
        slots[s : s + 1, :] = jnp.full((1, L), label.astype(F32), F32)
        for c in range(NC):
            rates[s * NC + c : s * NC + c + 1, :] = jnp.full((1, L), coeff[0, c, 0, s], F32)
        for d in range(3):
            masks[d * BZ + s : d * BZ + s + 1, :] = jnp.full((1, L), mask[0, d, 0, s].astype(F32), F32)
    copies[0].wait()
    for out, rest, (sources, _) in zip((even, odd), (even_rest, odd_rest), chosen):
        for k in range(MOVE):
            for c in range(NC):
                box = k * NC + c
                out[4 * box : 4 * box + 2, :] = boxes[sources[k], c, :2]
                out[4 * box + 2 : 4 * box + 4, :] = boxes[sources[k], c, E - 2 :]
                rest[12 * box : 12 * box + 12, :] = boxes[sources[k], c, 2 : E - 2]


def stays(slots):
    label = (subs() + 1).astype(F32)
    return [slots[s : s + 1, :] == label for s in range(BZ)]


def stayed_tile(found, boxes, c, x, h):
    tile = jnp.zeros((BZ, L), F32)
    for s in range(BZ):
        tile = jnp.where(found[s], boxes[s, c, x : x + 1, h * L : h * L + L], tile)
    return tile


def stay_kernel(shape, boxes, slots, moved):
    found = stays(slots)
    for c in range(NC):
        for x in range(E):
            row = (c * E + x) * BZ
            for h in range(2):
                moved[h, row : row + BZ, :] = stayed_tile(found, boxes, c, x, h)


def arrivals(even, odd):
    sub = subs()
    found = []
    for parcel in (even, odd):
        for k in range(MOVE):
            label = parcel[AHEAD + k : AHEAD + k + 1, L:]
            found.append((parcel, k, label == (sub + 1).astype(F32)))
    return found


def merged(found, tile, c, x, h, rests=None):
    for i, (parcel, k, hit) in enumerate(found):
        if x in EDGES:
            source, at = parcel, (k * NC + c) * 4 + EDGES.index(x)
        else:
            source, at = rests[i // MOVE], (k * NC + c) * 12 + x - 2
        tile = jnp.where(hit, source[at : at + 1, h * L : h * L + L], tile)
    return tile


def spread(tile, lane):
    return pick_lanes(tile, jnp.full((BZ, L), lane, I32))


def plane_row(layer, h, c):
    return ((layer * 2 + h) * NC + c) * BZ


def xsend_kernel(shape, even, odd, boxes, slots, old_rates, core, link, rates):
    gx, _, _ = place_of(shape)
    first = gx % 2 == 0
    kept, found = stays(slots), arrivals(even, odd)
    lane = lanes()
    together = jnp.zeros((BZ, L), F32)
    for c in range(NC):
        tile = jnp.zeros((BZ, L), F32)
        for s in range(BZ):
            tile = jnp.where(kept[s], old_rates[s * NC + c : s * NC + c + 1, :], tile)
        for parcel, k, hit in found:
            line = jnp.broadcast_to(parcel[AHEAD + k : AHEAD + k + 1, :L], (BZ, L))
            tile = jnp.where(hit, spread(line, c), tile)
        rates[c * BZ : c * BZ + BZ, :] = tile
        together = jnp.where(lane == c, tile, together)
        for layer in range(2):
            for h in range(2):
                sides = [merged(found, stayed_tile(kept, boxes, c, x, h), c, x, h) for x in (layer, E - 1 - layer)]
                at = plane_row(layer, h, c)
                core[at : at + BZ, :] = jnp.where(first, sides[1], sides[0])
                link[at : at + BZ, :] = jnp.where(first, sides[0], sides[1])
    core[FACE:, :] = together
    link[FACE:, :] = together


def merge_kernel(shape, even, odd, even_rest, odd_rest, moved, out, near, far):
    _, gy, _ = place_of(shape)
    first = gy % 2 == 0
    found = arrivals(even, odd)
    lane = lanes()
    for c in range(NC):
        low = [[None, None], [None, None]]
        high = [[None, None], [None, None]]
        for x in range(E):
            row = (c * E + x) * BZ
            at = L // 8 * (x % 8)
            here = lane // E == x % 8
            half = x // 8
            for h in range(2):
                tile = merged(found, moved[h, row : row + BZ, :], c, x, h, (even_rest, odd_rest))
                out[h, row : row + BZ, :] = tile
                for layer in range(2):
                    keep, start = ((low, E * layer) if h == 0 else (high, L - E - E * layer))
                    strip = rl(tile, at - start)
                    old = keep[layer][half]
                    keep[layer][half] = strip if old is None else jnp.where(here, strip, old)
        for layer in range(2):
            for h in range(2):
                at = plane_row(layer, h, c)
                near[at : at + BZ, :] = jnp.where(first, high[layer][h], low[layer][h])
                far[at : at + BZ, :] = jnp.where(first, low[layer][h], high[layer][h])


def ends(shape):
    gx, gy, _ = place_of(shape)
    x_first, y_first = gx % 2 == 0, gy % 2 == 0
    link_ok = jnp.where(x_first, gx > 0, gx < shape[0] - 1)
    far_ok = jnp.where(y_first, gy > 0, gy < shape[1] - 1)
    return x_first, y_first, link_ok, far_ok


def ysend_kernel(shape, link, core, rates, near, far, near_out, far_out):
    x_first, y_first, link_ok, _ = ends(shape)
    lane = lanes()
    near_out[:FACE, :] = near[...]
    far_out[:FACE, :] = far[...]
    bottoms = [jnp.zeros((BZ, L), F32)] * 2
    tops = [jnp.zeros((BZ, L), F32)] * 2
    for c in range(NC):
        lines = []
        for h in range(2):
            at = plane_row(0, h, c)
            a = core[at : at + BZ, :]
            b = jnp.where(link_ok, link[at : at + BZ, :], 0.0)
            lines.append((jnp.where(x_first, b, a), jnp.where(x_first, a, b)))
        i, at = divmod(c, 4)
        at *= 2 * E
        low = (lane >= at) & (lane < at + E)
        high = (lane >= at + E) & (lane < at + 2 * E)
        bottoms[i] = jnp.where(low, rl(lines[0][0], at), jnp.where(high, rl(lines[0][1], at + E), bottoms[i]))
        tops[i] = jnp.where(low, rl(lines[1][0], at + E), jnp.where(high, rl(lines[1][1], at + 2 * E), tops[i]))
        rate = rates[c * BZ : c * BZ + BZ, :]
        bottoms[1] = jnp.where(lane == L // 2 + c, rate, bottoms[1])
        tops[1] = jnp.where(lane == L // 2 + c, rate, tops[1])
    for i in range(2):
        at = FACE + i * BZ
        near_out[at : at + BZ, :] = jnp.where(y_first, tops[i], bottoms[i])
        far_out[at : at + BZ, :] = jnp.where(y_first, bottoms[i], tops[i])


def extra_at(ref, c):
    i, at = divmod(c, 4)
    return rl(ref[FACE + i * BZ : FACE + i * BZ + BZ, :], -2 * E * at)


def y_rate(ref, c):
    return spread(ref[FACE + BZ : FACE + 2 * BZ, :], L // 2 + c)


def z_parts(x, lane, sub, swap):
    z = lane % E
    down = jnp.where(sub == 0, 0.0, rs(x, 1))
    up = jnp.where(sub == BZ - 1, 0.0, rs(x, -1))
    ends_ = pick_lanes(jnp.where(z == E - 1, down, up), swap)
    return jnp.where(z == 0, ends_, rl(x, 1)) + jnp.where(z == E - 1, ends_, rl(x, -1))


def swap_index(lane):
    z = lane % E
    return jnp.where(z == 0, lane + E - 1, jnp.where(z == E - 1, lane - E + 1, lane))


def inner(pair, lane, sub, swap):
    a, b = pair
    a1, b1, a2, b2 = rl(a, E), rl(b, E), rl(a, -E), rl(b, -E)
    low, high = lane < E, lane >= L - E
    first = jnp.where(low, 0.0, a1) + jnp.where(high, b2, a2) + z_parts(a, lane, sub, swap)
    second = jnp.where(low, a1, b1) + jnp.where(high, 0.0, b2) + z_parts(b, lane, sub, swap)
    return first, second


def pair_at(ref, layer, c):
    return tuple(ref[plane_row(layer, h, c) : plane_row(layer, h, c) + BZ, :] for h in range(2))


def tile_at(ref, c, x):
    row = (c * E + x) * BZ
    return tuple(ref[h, row : row + BZ, :] for h in range(2))


def z_differences(tiles, sub, upper):
    down = [jnp.where(sub == 0, 0.0, t) for t in [rs(t, 1) for t in tiles]]
    up = [jnp.where(sub == BZ - 1, 0.0, t) for t in [rs(t, -1) for t in tiles]]
    high = [rl(t, 1 - E) for t in [jnp.where(upper, t, d) for t, d in zip(tiles, down)]]
    return [jnp.where(upper, u - g, g - t) for g, u, t in zip(high, up, tiles)]


def sweep_kernel(shape, moved, rates, link, core, core_sent, link_sent, out, core_first, link_first, tops):
    x_first, _, link_ok, _ = ends(shape)
    _, gy, _ = place_of(shape)
    lane, sub = lanes(), subs()
    swap = swap_index(lane)
    upper = sub % 2 == 1
    z = lane % E
    for c in range(NC):
        rate = rates[c * BZ : c * BZ + BZ, :]
        scale = 1.0 / (1.0 + 6.0 * rate)
        ghost = []
        for got, sent, kept, ok in ((core, core_sent, core_first, None), (link, link_sent, link_first, link_ok)):
            g0, g1, own = pair_at(got, 0, c), pair_at(got, 1, c), pair_at(sent, 0, c)
            g_rate = spread(got[FACE:, :], c)
            if ok is not None:
                g0, g1 = (tuple(jnp.where(ok, t, 0.0) for t in g) for g in (g0, g1))
                g_rate = jnp.where(ok, g_rate, 0.0)
            kept[2 * PLANE + c * BZ : 2 * PLANE + c * BZ + BZ, :] = g_rate
            ghost.append(g0)
            g_scale = 1.0 / (1.0 + 6.0 * g_rate)
            sums = inner(g0, lane, sub, swap)
            for h in range(2):
                value = (g0[h] + g_rate * (sums[h] + g1[h] + own[h])) * g_scale
                if ok is not None:
                    value = jnp.where(ok, value, 0.0)
                row = (h * NC + c) * BZ
                kept[row : row + BZ, :] = value
        low = [jnp.where(x_first, b, a) for a, b in zip(*ghost)]
        high = [jnp.where(x_first, a, b) for a, b in zip(*ghost)]
        for x in range(E):
            here = tile_at(moved, c, x)
            before = low if x == 0 else tile_at(moved, c, x - 1)
            after = high if x == E - 1 else tile_at(moved, c, x + 1)
            sums = inner(here, lane, sub, swap)
            row = (c * E + x) * BZ
            for h in range(2):
                out[h, row : row + BZ, :] = (here[h] + rate * (sums[h] + before[h] + after[h])) * scale
    every = [(h, c, k) for c in range(NC) for h in range(2) for k in range(E // 2)]
    d = []
    for h, c, k in every:
        row = (c * E + 2 * k) * BZ
        d.append(out[h, row : row + BZ, :] + out[h, row + BZ : row + 2 * BZ, :])
    d = z_differences(d, sub, upper)
    d = [t + r for t, r in zip(d, [rl(t, -E) for t in d])]
    d = [rl(t, k) for t, (_, _, k) in zip(d, every)]
    faces = {}
    for t, (h, c, k) in zip(d, every):
        faces[h, c] = t if k == 0 else jnp.where(z == k, t, faces[h, c])
    y8 = lane % 8
    source = (y8 % 4) * (2 * E) + lane // E
    picked = {key: pick_lanes(t, source) for key, t in faces.items()}
    for c in range(NC):
        top = jnp.where(y8 < 4, picked[0, c], picked[1, c])
        tops[c * BZ : c * BZ + BZ, :] = jnp.where(z // 8 == gy % 2, top, 0.0)


def coarse_plane(pair, parity, lane, sub):
    sums = []
    for t in pair:
        t = t + rl(t, -1)
        sums.append(t + rl(t, -E))
    source = (lane // E % 4) * (2 * E) + 2 * (lane % 8)
    out = jnp.where(lane < L // 2, pick_lanes(sums[0], source), pick_lanes(sums[1], source))
    return jnp.where(lane % E // 8 == sub % 2, 0.25 * out, 0.0)


def strips(low, high, x, low_lane, high_lane):
    shift = E * (x % 8)
    return (
        jnp.where(low_lane, rl(low[x // 8], -shift), 0.0),
        jnp.where(high_lane, rl(high[x // 8], L - E - shift), 0.0),
    )


def corner(extra, low_lane, high_lane):
    return jnp.where(low_lane, extra, 0.0), jnp.where(high_lane, rl(extra, L - 2 * E), 0.0)


def y_ghosts(got, ok, c):
    g0, g1, extra = pair_at(got, 0, c), pair_at(got, 1, c), extra_at(got, c)
    if ok is not None:
        g0, g1 = (tuple(jnp.where(ok, t, 0.0) for t in g) for g in (g0, g1))
        extra = jnp.where(ok, extra, 0.0)
    return g0, g1, extra


def y_first_sweep(got, sent, ok, ghost, c, lane, sub, swap):
    g0, g1, extra = ghost
    own = pair_at(sent, 0, c)
    g_rate = y_rate(got, c)
    if ok is not None:
        g_rate = jnp.where(ok, g_rate, 0.0)
    g_scale = 1.0 / (1.0 + 6.0 * g_rate)
    sums, line = inner(g0, lane, sub, swap), corner(extra, lane < E, lane >= L - E)
    values = [(g0[h] + g_rate * (sums[h] + line[h] + g1[h] + own[h])) * g_scale for h in range(2)]
    return values if ok is None else [jnp.where(ok, t, 0.0) for t in values]


def x_first_sweep(part, ok, at_low, low_line, high_line, c, low_lane, high_lane):
    g_rate = part[2 * PLANE + c * BZ : 2 * PLANE + c * BZ + BZ, :]
    g_weight = g_rate / (1.0 + 6.0 * g_rate)
    bottom = jnp.where(at_low, low_line, rl(low_line, -E))
    top = jnp.where(at_low, rl(high_line, L - E), rl(high_line, L - 2 * E))
    values = []
    for h, (line, there) in enumerate(((bottom, low_lane), (top, high_lane))):
        row = (h * NC + c) * BZ
        values.append(part[row : row + BZ, :] + g_weight * jnp.where(there, line, 0.0))
    return values if ok is None else [jnp.where(ok, t, 0.0) for t in values]


def flux_kernel(
    shape, partial, moved_rates, masks, tops, link_first, far, near, far_sent, own_far, y_far, kept, sent
):
    x_first, y_first, link_ok, far_ok = ends(shape)
    gx, gy, _ = place_of(shape)
    par_x, par_y = gx % 2, gy % 2
    lane, sub = lanes(), subs()
    swap = swap_index(lane)
    upper = sub % 2 == 1
    z = lane % E
    low_lane, high_lane = lane < E, lane >= L - E
    each = range(NC)
    rate = [moved_rates[c * BZ : c * BZ + BZ, :] for c in each]
    scale = [1.0 / (1.0 + 6.0 * r) for r in rate]
    weight = [r * q for r, q in zip(rate, scale)]
    near_g = [y_ghosts(near, None, c) for c in each]
    far_g = [y_ghosts(far, far_ok, c) for c in each]
    far_f = []
    for c in each:
        values = y_first_sweep(far, far_sent, far_ok, far_g[c], c, lane, sub, swap)
        for h in range(2):
            row = (h * NC + c) * BZ
            y_far[row : row + BZ, :] = values[h]
        far_f.append(values)
    far_r = [g[0] for g in far_g]

    def by_side(which, c):
        a, b = near_g[c][which], far_g[c][which]
        if which == 2:
            return jnp.where(y_first, b, a), jnp.where(y_first, a, b)
        return [jnp.where(y_first, q, p) for p, q in zip(a, b)], [jnp.where(y_first, p, q) for p, q in zip(a, b)]

    faces_y = []
    for c in each:
        own = pair_at(own_far, 0, c)
        flux = [far_f[c][h] - own[h] - weight[c] * far_r[c][h] for h in range(2)]
        face = coarse_plane(flux, par_x, lane, sub) * (rate[c] * masks[BZ : 2 * BZ, :])
        faces_y.append(face + rs(face, 1))
    faces_x = []
    for c in each:
        ghost = x_first_sweep(link_first, link_ok, x_first, *by_side(2, c), c, low_lane, high_lane)
        low_r, high_r = by_side(0, c)
        at_0, at_15 = (strips(low_r, high_r, x, low_lane, high_lane) for x in (0, E - 1))
        cells_0, cells_15 = tile_at(partial, c, 0), tile_at(partial, c, E - 1)
        flux = []
        for h in range(2):
            cell = jnp.where(x_first, cells_0[h], cells_15[h])
            cell = cell + weight[c] * jnp.where(x_first, at_0[h], at_15[h])
            flux.append(ghost[h] - cell)
        face = coarse_plane(flux, par_y, lane, sub) * (rate[c] * masks[0:BZ, :])
        faces_x.append(face + rs(face, -1))
    faces_z = []
    source = (lane // E % 4) * (2 * E) + jnp.where(lane % 8 == 7, 7, 0)
    d = []
    for c in each:
        for side in by_side(0, c):
            d += [weight[c] * t for t in side]
    d = [t + r for t, r in zip(d, [rl(t, -E) for t in d])]
    d = z_differences(d, sub, upper)
    halves = []
    for c in each:
        for h in range(2):
            halves.append(jnp.where(z == 7, rl(d[4 * c + 2 + h], 7), d[4 * c + h]))
    halves = [pick_lanes(t, source) for t in halves]
    for c in each:
        add = jnp.where(lane < L // 2, halves[2 * c], halves[2 * c + 1])
        add = jnp.where((z == 8 * par_y) | (z == 8 * par_y + 7), add, 0.0)
        faces_z.append((tops[c * BZ : c * BZ + BZ, :] + add) * (0.25 * rate[c] * masks[2 * BZ :, :]))
    left = sub % 4 < 2
    for c in each:
        outer = jnp.where(upper, faces_y[c], faces_x[c])
        columns = (jnp.where(left, outer, rs(faces_z[c], 2)), jnp.where(left, rs(outer, -2), faces_z[c]))
        row = c * BZ
        kept[row : row + BZ, :] = jnp.where(y_first, columns[0], columns[1])
        sent[row : row + BZ, :] = jnp.where(y_first, columns[1], columns[0])


def half_kernel(shape, kept, got, _, mine, sent):
    gx, _, _ = place_of(shape)
    first = gx % 2 == 0
    top = subs() < 4
    for i in range(NC):
        a, b = kept[i * BZ : i * BZ + BZ, :], got[i * BZ : i * BZ + BZ, :]
        rows = (jnp.where(top, a, rs(b, 4)), jnp.where(top, rs(a, 4), b))
        mine[i * BZ : i * BZ + BZ, :] = jnp.where(first, rows[0], rows[1])
        sent[i * BZ : i * BZ + BZ, :] = jnp.where(first, rows[1], rows[0])


def register_kernel(shape, mine, got, out):
    x_first, y_first, _, _ = ends(shape)
    sub = subs()
    for c in range(NC):
        m, g = mine[c * BZ : c * BZ + BZ, :], got[c * BZ : c * BZ + BZ, :]
        m4, g4 = rs(m, 4), rs(g, 4)
        for h in range(2):
            same_y, same_x = (y_first, x_first) if h == 0 else (~y_first, ~x_first)
            a, b = jnp.where(same_y, m, m4), jnp.where(same_y, g, g4)
            x0, x1 = jnp.where(x_first, a, b), jnp.where(x_first, b, a)
            t, t4 = jnp.where(same_x, m, g), jnp.where(same_x, m4, g4)
            y0, y1 = jnp.where(y_first, rs(t, 1), rs(t, 5)), jnp.where(y_first, rs(t, 6), rs(t, 2))
            rows = jnp.where(sub == 0, x0, jnp.where(sub == 1, rs(x1, 1), rs(t + t4, 2)))
            rows = jnp.where(sub == 2, y0, jnp.where(sub == 3, y1, rows))
            out[0, 0, c, :, h * L : h * L + L] = rows[:6]


def second_kernel(shape, moved, rates, partial, core_first, link_first, far_sent, out, own_far):
    x_first, _, _, _ = ends(shape)
    lane, sub = lanes(), subs()
    swap = swap_index(lane)
    for c in range(NC):
        rate = rates[c * BZ : c * BZ + BZ, :]
        scale = 1.0 / (1.0 + 6.0 * rate)
        own, own1 = pair_at(far_sent, 0, c), pair_at(far_sent, 1, c)
        sums, line = inner(own, lane, sub, swap), corner(extra_at(far_sent, c), lane < E, lane >= L - E)
        for h in range(2):
            row = (h * NC + c) * BZ
            own_far[row : row + BZ, :] = (own[h] + rate * (sums[h] + line[h] + own1[h])) * scale
        core, link = pair_at(core_first, 0, c), pair_at(link_first, 0, c)
        low = [jnp.where(x_first, b, a) for a, b in zip(core, link)]
        high = [jnp.where(x_first, a, b) for a, b in zip(core, link)]
        for x in range(E):
            here = tile_at(partial, c, x)
            before = low if x == 0 else tile_at(partial, c, x - 1)
            after = high if x == E - 1 else tile_at(partial, c, x + 1)
            sums = inner(here, lane, sub, swap)
            start = tile_at(moved, c, x)
            row = (c * E + x) * BZ
            for h in range(2):
                out[h, row : row + BZ, :] = start[h] + rate * (sums[h] + before[h] + after[h])


def smooth_kernel(
    shape, rates, partial, core_first, link_first, far, near, near_sent, y_far, out, done, planes, held, boxes, sem
):
    done[...] = jnp.zeros((BZ, L), F32)
    x_first, y_first, _, far_ok = ends(shape)
    lane, sub = lanes(), subs()
    swap = swap_index(lane)
    low_lane, high_lane = lane < E, lane >= L - E

    def by_side(a, b, a_first):
        low = [jnp.where(a_first, q, p) for p, q in zip(a, b)]
        high = [jnp.where(a_first, p, q) for p, q in zip(a, b)]
        return low, high

    for c in range(NC):
        rate = rates[c * BZ : c * BZ + BZ, :]
        weight = rate / (1.0 + 6.0 * rate)
        near_g, far_g = y_ghosts(near, None, c), y_ghosts(far, far_ok, c)
        near_f = y_first_sweep(near, near_sent, None, near_g, c, lane, sub, swap)
        ghosts_f = by_side(near_f, pair_at(y_far, 0, c), y_first)
        ghosts_r = by_side(near_g[0], far_g[0], y_first)
        lines = by_side(near_g[2:], far_g[2:], y_first)
        x_rates = [ref[2 * PLANE + c * BZ : 2 * PLANE + c * BZ + BZ, :] for ref in (core_first, link_first)]
        x_weights = [t / (1.0 + 6.0 * t) for t in x_rates]
        (low_w,), (high_w,) = by_side(x_weights[:1], x_weights[1:], x_first)
        for side in range(2):
            added = [weight * t for t in ghosts_r[side]]
            (line,) = lines[side]
            sums = inner(added, lane, sub, swap)
            ends_ = (jnp.where(low_lane, low_w * line, 0.0), jnp.where(high_lane, high_w * rl(line, L - 2 * E), 0.0))
            for h in range(2):
                row = ((side * 2 + h) * NC + c) * BZ
                planes[0, row : row + BZ, :] = rate * (sums[h] + ends_[h] + ghosts_f[side][h])
                planes[1, row : row + BZ, :] = rate * added[h]
    next_low = (lane >= E) & (lane < 2 * E)
    next_high = (lane >= L - 2 * E) & (lane < L - E)
    copies = []
    for c in range(NC):
        rate = rates[c * BZ : c * BZ + BZ, :]
        scale = 1.0 / (1.0 + 6.0 * rate)
        for x in range(E):
            row = (c * E + x) * BZ
            shift = E * (x % 8)
            for h, (here, there, at) in enumerate(((low_lane, next_low, 0), (high_lane, next_high, L - E))):
                plane = ((h * 2 + x // 8) * NC + c) * BZ
                first = rl(planes[0, plane : plane + BZ, :], at - shift)
                second = rl(planes[1, plane : plane + BZ, :], (at - E if h else E) - shift)
                add = jnp.where(here, first, jnp.where(there, second, 0.0))
                held[h, row : row + BZ, :] = (partial[h, row : row + BZ, :] + add) * scale
        for s in range(BZ):
            for h in range(2):
                boxes[c, s, :, h * L : h * L + L] = held[h, pl.ds(c * E * BZ + s, E, stride=BZ), :]
        copies.append(pltpu.make_async_copy(boxes.at[c], out.at[0, 0, :, c], sem.at[c]))
        copies[-1].start()
    for copy in copies:
        copy.wait()


def body(shape, fields_old, coeff_old, new_place, cf_mask):
    rows, columns = shape
    count = rows * columns
    both = ("gx", "gy")

    def swap(array, pairs):
        return lax.ppermute(array, both, pairs)

    even_pairs = [(i, i ^ 1) for i in range(count)]
    odd_pairs = [(i, (i + 1) % count if i % 2 else (i - 1) % count) for i in range(count)]
    at = lambda a, b: a * columns + b
    core_pairs = [(at(a, b), at(a ^ 1, b)) for a in range(rows) for b in range(columns)]
    link_pairs = [
        (at(a, b), at((a + 1) % rows if a % 2 else (a - 1) % rows, b)) for a in range(rows) for b in range(columns)
    ]
    far_pairs = [
        (at(a, b), at(a ^ 1, b) if b in (0, columns - 1) else at(a, b + 1 if b % 2 else b - 1))
        for a in range(rows)
        for b in range(columns)
    ]
    k = lambda f: functools.partial(f, shape)
    coeff_old = coeff_old.transpose(0, 3, 1, 2)
    cf_mask = cf_mask.transpose(0, 2, 1, 3)
    big = (2, NC * E * BZ, L)

    plane = ((2 * PLANE, L), "vmem")
    even, odd, even_rest, odd_rest, boxes, slots, rates, masks = call(
        k(pack_kernel),
        [(a, "hbm") for a in (new_place, coeff_old, cf_mask, fields_old)],
        [
            ((PARCEL, 2 * L), "vmem"),
            ((PARCEL, 2 * L), "vmem"),
            ((REST, 2 * L), "vmem"),
            ((REST, 2 * L), "vmem"),
            ((BZ, NC, E, 2 * L), "vmem"),
            ((BZ, L), "vmem"),
            ((PLANE, L), "vmem"),
            ((3 * BZ, L), "vmem"),
        ],
        [
            SM((1, 1, BZ), I32),
            SM((1, NC, 1, BZ), F32),
            SM((1, 3, 1, BZ), I32),
            pltpu.SemaphoreType.DMA((4,)),
        ],
    )
    even_got = swap(even, even_pairs)
    odd_got = swap(odd, odd_pairs)
    even_rest_got = swap(even_rest, even_pairs)
    odd_rest_got = swap(odd_rest, odd_pairs)
    core, link, rates = call(
        k(xsend_kernel),
        [(a, "vmem") for a in (even_got, odd_got, boxes, slots, rates)],
        [((XFACE, L), "vmem"), ((XFACE, L), "vmem"), ((PLANE, L), "vmem")],
    )
    (stayed,) = call(k(stay_kernel), [(boxes, "vmem"), (slots, "vmem")], [(big, "vmem")])
    core_got = swap(core, core_pairs)
    link_got = swap(link, link_pairs)
    moved, near, far = call(
        k(merge_kernel),
        [(a, "vmem") for a in (even_got, odd_got, even_rest_got, odd_rest_got, stayed)],
        [(big, "vmem"), ((FACE, L), "vmem"), ((FACE, L), "vmem")],
    )
    near, far = call(
        k(ysend_kernel),
        [(a, "vmem") for a in (link_got, core_got, rates, near, far)],
        [((YFACE, L), "vmem"), ((YFACE, L), "vmem")],
    )
    near_got = swap(near, even_pairs)
    far_got = swap(far, far_pairs)
    part, core_first, link_first, tops = call(
        k(sweep_kernel),
        [(a, "vmem") for a in (moved, rates, link_got, core_got, core, link)],
        [(big, "vmem"), ((3 * PLANE, L), "vmem"), ((3 * PLANE, L), "vmem"), ((PLANE, L), "vmem")],
    )
    second, own_far = call(
        k(second_kernel),
        [(a, "vmem") for a in (moved, rates, part, core_first, link_first, far)],
        [(big, "vmem"), plane],
    )
    y_far, kept, sent = call(
        k(flux_kernel),
        [(a, "vmem") for a in (part, rates, masks, tops, link_first, far_got, near_got, far, own_far)],
        [plane, ((PLANE, L), "vmem"), ((PLANE, L), "vmem")],
    )
    got = swap(sent, even_pairs)

    smoothed, done = call(
        k(smooth_kernel),
        [(a, "vmem") for a in (rates, second, core_first, link_first, far_got, near_got, near, y_far)],
        [((1, 1, BZ, NC, E, 2 * L), "hbm"), ((BZ, L), "vmem")],
        [
            VM((2, 4 * PLANE, L), F32),
            VM(big, F32),
            VM((NC, BZ, E, 2 * L), F32),
            pltpu.SemaphoreType.DMA((NC,)),
        ],
    )
    mine, sent = call(k(half_kernel), [(a, "vmem") for a in (kept, got, done)], [((PLANE, L), "vmem")] * 2)
    got = swap(sent, core_pairs)
    (registers,) = call(
        k(register_kernel), [(mine, "vmem"), (got, "vmem")], [((1, 1, NC, 6, 2 * L), "out")]
    )
    return smoothed, registers


def solution(mesh):
    shape = (mesh.shape["gx"], mesh.shape["gy"])
    return jax.shard_map(
        functools.partial(body, shape),
        mesh=mesh,
        in_specs=(
            P("gx", "gy", None, None, None, None),
            P("gx", "gy", None, None),
            P("gx", "gy", None),
            P("gx", "gy", None, None),
        ),
        out_specs=(P("gx", "gy", None, None, None, None), P("gx", "gy", None, None, None)),
        check_vma=False,
    )
```

```python
import functools

import jax
import jax.numpy as jnp
from jax import lax
from jax.experimental import pallas as pl
from jax.experimental.pallas import tpu as pltpu
from jax.sharding import PartitionSpec as P

NC = 5
E = 16
BZ = 8
MOVE = 2
L = 128
F32 = jnp.float32
I32 = jnp.int32

PLANE = NC * BZ
FACE = 4 * PLANE
EDGES = (0, 1, E - 2, E - 1)
AHEAD = MOVE * NC * 4
PARCEL = 48
REST = MOVE * NC * 12
XFACE = FACE + BZ
YFACE = FACE + 2 * BZ

VM = pltpu.VMEM
SM = pltpu.SMEM


def call(kernel, ins, outs, scratch=(), aliases=None, flops=1000, **kw):
    given, in_specs = [], []
    for array, space in ins:
        if space == "vmem":
            given.append(pltpu.with_memory_space_constraint(array, VM))
            in_specs.append(pl.BlockSpec(memory_space=VM))
        else:
            given.append(pltpu.with_memory_space_constraint(array, pltpu.HBM))
            in_specs.append(pl.BlockSpec(memory_space=pltpu.HBM))
    shapes, out_specs = [], []
    for shape, space in outs:
        if space == "vmem":
            shapes.append(VM(shape, F32))
            out_specs.append(pl.BlockSpec(memory_space=VM))
        else:
            shapes.append(jax.ShapeDtypeStruct(shape, F32))
            out_specs.append(pl.BlockSpec(memory_space=pltpu.HBM if space == "hbm" else VM))
    return pl.pallas_call(
        kernel,
        out_shape=shapes,
        in_specs=in_specs,
        out_specs=out_specs,
        scratch_shapes=list(scratch),
        input_output_aliases=aliases or {},
        cost_estimate=pl.CostEstimate(flops=flops, bytes_accessed=0, transcendentals=0),
        compiler_params=pltpu.CompilerParams(vmem_limit_bytes=24 * 1024 * 1024),
        **kw,
    )(*given)


def lanes():
    return lax.broadcasted_iota(I32, (BZ, L), 1)


def subs():
    return lax.broadcasted_iota(I32, (BZ, L), 0)


def rl(x, shift):
    shift %= L
    return x if shift == 0 else pltpu.roll(x, shift, 1)


def rs(x, shift):
    shift %= BZ
    return x if shift == 0 else pltpu.roll(x, shift, 0)


def pick_lanes(x, index):
    return jnp.take_along_axis(x, index, axis=1)


def place_of(mesh_shape):
    gx = lax.axis_index("gx")
    gy = lax.axis_index("gy")
    return gx, gy, gx * mesh_shape[1] + gy


def sources_of(place, owner):
    count = jnp.int32(0)
    sources = [jnp.int32(0)] * MOVE
    labels = [jnp.int32(0)] * MOVE
    for s in range(BZ):
        value = place[s]
        hit = value // BZ == owner
        for k in range(MOVE):
            taken = hit & (count == k)
            sources[k] = jnp.where(taken, s, sources[k])
            labels[k] = jnp.where(taken, value % BZ + 1, labels[k])
        count = count + hit.astype(I32)
    return sources, labels


def fill_rest(rest, boxes, sources):
    for k in range(MOVE):
        for c in range(NC):
            box = k * NC + c
            rest[12 * box : 12 * box + 12, :] = boxes[sources[k], c, 2 : E - 2]


def pack_kernel(
    shape, place_hbm, coeff_hbm, mask_hbm, fields_hbm, even, odd, even_rest, odd_rest, boxes, slots, rates, masks,
    place_s, coeff, mask, sem,
):
    pairs = ((fields_hbm.at[0, 0], boxes), (place_hbm, place_s), (coeff_hbm, coeff), (mask_hbm, mask))
    copies = [pltpu.make_async_copy(a, b, sem.at[i]) for i, (a, b) in enumerate(pairs)]
    for copy in copies:
        copy.start()
    _, _, me = place_of(shape)
    ahead = 1 - 2 * (me % 2)
    lane = lax.broadcasted_iota(I32, (1, L), 1)
    for copy in copies[1:]:
        copy.wait()
    place = [place_s[0, 0, s] for s in range(BZ)]
    chosen = [sources_of(place, me + ahead), sources_of(place, me - ahead)]
    for out, (sources, labels) in zip((even, odd), chosen):
        out[AHEAD:PARCEL, :] = jnp.zeros((PARCEL - AHEAD, 2 * L), F32)
        for k in range(MOVE):
            out[AHEAD + k : AHEAD + k + 1, L:] = jnp.full((1, L), labels[k].astype(F32), F32)
            line = jnp.zeros((1, L), F32)
            for c in range(NC):
                line = jnp.where(lane == c, coeff[0, c, 0, sources[k]], line)
            out[AHEAD + k : AHEAD + k + 1, :L] = line
    for s in range(BZ):
        label = jnp.where(place[s] // BZ == me, place[s] % BZ + 1, 0)
        slots[s : s + 1, :] = jnp.full((1, L), label.astype(F32), F32)
        for c in range(NC):
            rates[s * NC + c : s * NC + c + 1, :] = jnp.full((1, L), coeff[0, c, 0, s], F32)
        for d in range(3):
            masks[d * BZ + s : d * BZ + s + 1, :] = jnp.full((1, L), mask[0, d, 0, s].astype(F32), F32)
    copies[0].wait()
    for out, rest, (sources, _) in zip((even, odd), (even_rest, odd_rest), chosen):
        for k in range(MOVE):
            for c in range(NC):
                box = k * NC + c
                out[4 * box : 4 * box + 2, :] = boxes[sources[k], c, :2]
                out[4 * box + 2 : 4 * box + 4, :] = boxes[sources[k], c, E - 2 :]
                rest[12 * box : 12 * box + 12, :] = boxes[sources[k], c, 2 : E - 2]


def stays(slots):
    label = (subs() + 1).astype(F32)
    return [slots[s : s + 1, :] == label for s in range(BZ)]


def stayed_tile(found, boxes, c, x, h):
    tile = jnp.zeros((BZ, L), F32)
    for s in range(BZ):
        tile = jnp.where(found[s], boxes[s, c, x : x + 1, h * L : h * L + L], tile)
    return tile


def stay_kernel(shape, boxes, slots, moved):
    found = stays(slots)
    for c in range(NC):
        for x in range(E):
            row = (c * E + x) * BZ
            for h in range(2):
                moved[h, row : row + BZ, :] = stayed_tile(found, boxes, c, x, h)


def arrivals(even, odd):
    sub = subs()
    found = []
    for parcel in (even, odd):
        for k in range(MOVE):
            label = parcel[AHEAD + k : AHEAD + k + 1, L:]
            found.append((parcel, k, label == (sub + 1).astype(F32)))
    return found


def merged(found, tile, c, x, h, rests=None):
    for i, (parcel, k, hit) in enumerate(found):
        if x in EDGES:
            source, at = parcel, (k * NC + c) * 4 + EDGES.index(x)
        else:
            source, at = rests[i // MOVE], (k * NC + c) * 12 + x - 2
        tile = jnp.where(hit, source[at : at + 1, h * L : h * L + L], tile)
    return tile


def spread(tile, lane):
    return pick_lanes(tile, jnp.full((BZ, L), lane, I32))


def plane_row(layer, h, c):
    return ((layer * 2 + h) * NC + c) * BZ


def xsend_kernel(shape, even, odd, boxes, slots, old_rates, core, link, rates):
    gx, _, _ = place_of(shape)
    first = gx % 2 == 0
    kept, found = stays(slots), arrivals(even, odd)
    lane = lanes()
    together = jnp.zeros((BZ, L), F32)
    for c in range(NC):
        tile = jnp.zeros((BZ, L), F32)
        for s in range(BZ):
            tile = jnp.where(kept[s], old_rates[s * NC + c : s * NC + c + 1, :], tile)
        for parcel, k, hit in found:
            line = jnp.broadcast_to(parcel[AHEAD + k : AHEAD + k + 1, :L], (BZ, L))
            tile = jnp.where(hit, spread(line, c), tile)
        rates[c * BZ : c * BZ + BZ, :] = tile
        together = jnp.where(lane == c, tile, together)
        for layer in range(2):
            for h in range(2):
                sides = [merged(found, stayed_tile(kept, boxes, c, x, h), c, x, h) for x in (layer, E - 1 - layer)]
                at = plane_row(layer, h, c)
                core[at : at + BZ, :] = jnp.where(first, sides[1], sides[0])
                link[at : at + BZ, :] = jnp.where(first, sides[0], sides[1])
    core[FACE:, :] = together
    link[FACE:, :] = together


def merge_kernel(shape, even, odd, even_rest, odd_rest, moved, out, near, far):
    _, gy, _ = place_of(shape)
    first = gy % 2 == 0
    found = arrivals(even, odd)
    lane = lanes()
    for c in range(NC):
        low = [[None, None], [None, None]]
        high = [[None, None], [None, None]]
        for x in range(E):
            row = (c * E + x) * BZ
            at = L // 8 * (x % 8)
            here = lane // E == x % 8
            half = x // 8
            for h in range(2):
                tile = merged(found, moved[h, row : row + BZ, :], c, x, h, (even_rest, odd_rest))
                out[h, row : row + BZ, :] = tile
                for layer in range(2):
                    keep, start = ((low, E * layer) if h == 0 else (high, L - E - E * layer))
                    strip = rl(tile, at - start)
                    old = keep[layer][half]
                    keep[layer][half] = strip if old is None else jnp.where(here, strip, old)
        for layer in range(2):
            for h in range(2):
                at = plane_row(layer, h, c)
                near[at : at + BZ, :] = jnp.where(first, high[layer][h], low[layer][h])
                far[at : at + BZ, :] = jnp.where(first, low[layer][h], high[layer][h])


def ends(shape):
    gx, gy, _ = place_of(shape)
    x_first, y_first = gx % 2 == 0, gy % 2 == 0
    link_ok = jnp.where(x_first, gx > 0, gx < shape[0] - 1)
    far_ok = jnp.where(y_first, gy > 0, gy < shape[1] - 1)
    return x_first, y_first, link_ok, far_ok


def ysend_kernel(shape, link, core, rates, near, far, near_out, far_out):
    x_first, y_first, link_ok, _ = ends(shape)
    lane = lanes()
    near_out[:FACE, :] = near[...]
    far_out[:FACE, :] = far[...]
    bottoms = [jnp.zeros((BZ, L), F32)] * 2
    tops = [jnp.zeros((BZ, L), F32)] * 2
    for c in range(NC):
        lines = []
        for h in range(2):
            at = plane_row(0, h, c)
            a = core[at : at + BZ, :]
            b = jnp.where(link_ok, link[at : at + BZ, :], 0.0)
            lines.append((jnp.where(x_first, b, a), jnp.where(x_first, a, b)))
        i, at = divmod(c, 4)
        at *= 2 * E
        low = (lane >= at) & (lane < at + E)
        high = (lane >= at + E) & (lane < at + 2 * E)
        bottoms[i] = jnp.where(low, rl(lines[0][0], at), jnp.where(high, rl(lines[0][1], at + E), bottoms[i]))
        tops[i] = jnp.where(low, rl(lines[1][0], at + E), jnp.where(high, rl(lines[1][1], at + 2 * E), tops[i]))
        rate = rates[c * BZ : c * BZ + BZ, :]
        bottoms[1] = jnp.where(lane == L // 2 + c, rate, bottoms[1])
        tops[1] = jnp.where(lane == L // 2 + c, rate, tops[1])
    for i in range(2):
        at = FACE + i * BZ
        near_out[at : at + BZ, :] = jnp.where(y_first, tops[i], bottoms[i])
        far_out[at : at + BZ, :] = jnp.where(y_first, bottoms[i], tops[i])


def extra_at(ref, c):
    i, at = divmod(c, 4)
    return rl(ref[FACE + i * BZ : FACE + i * BZ + BZ, :], -2 * E * at)


def y_rate(ref, c):
    return spread(ref[FACE + BZ : FACE + 2 * BZ, :], L // 2 + c)


def z_parts(x, lane, sub, swap):
    z = lane % E
    down = jnp.where(sub == 0, 0.0, rs(x, 1))
    up = jnp.where(sub == BZ - 1, 0.0, rs(x, -1))
    ends_ = pick_lanes(jnp.where(z == E - 1, down, up), swap)
    return jnp.where(z == 0, ends_, rl(x, 1)) + jnp.where(z == E - 1, ends_, rl(x, -1))


def swap_index(lane):
    z = lane % E
    return jnp.where(z == 0, lane + E - 1, jnp.where(z == E - 1, lane - E + 1, lane))


def inner(pair, lane, sub, swap):
    a, b = pair
    a1, b1, a2, b2 = rl(a, E), rl(b, E), rl(a, -E), rl(b, -E)
    low, high = lane < E, lane >= L - E
    first = jnp.where(low, 0.0, a1) + jnp.where(high, b2, a2) + z_parts(a, lane, sub, swap)
    second = jnp.where(low, a1, b1) + jnp.where(high, 0.0, b2) + z_parts(b, lane, sub, swap)
    return first, second


def pair_at(ref, layer, c):
    return tuple(ref[plane_row(layer, h, c) : plane_row(layer, h, c) + BZ, :] for h in range(2))


def tile_at(ref, c, x):
    row = (c * E + x) * BZ
    return tuple(ref[h, row : row + BZ, :] for h in range(2))


def z_differences(tiles, sub, upper):
    down = [jnp.where(sub == 0, 0.0, t) for t in [rs(t, 1) for t in tiles]]
    up = [jnp.where(sub == BZ - 1, 0.0, t) for t in [rs(t, -1) for t in tiles]]
    high = [rl(t, 1 - E) for t in [jnp.where(upper, t, d) for t, d in zip(tiles, down)]]
    return [jnp.where(upper, u - g, g - t) for g, u, t in zip(high, up, tiles)]


def sweep_kernel(shape, moved, rates, link, core, core_sent, link_sent, out, core_first, link_first, tops):
    x_first, _, link_ok, _ = ends(shape)
    _, gy, _ = place_of(shape)
    lane, sub = lanes(), subs()
    swap = swap_index(lane)
    upper = sub % 2 == 1
    z = lane % E
    for c in range(NC):
        rate = rates[c * BZ : c * BZ + BZ, :]
        scale = 1.0 / (1.0 + 6.0 * rate)
        ghost = []
        for got, sent, kept, ok in ((core, core_sent, core_first, None), (link, link_sent, link_first, link_ok)):
            g0, g1, own = pair_at(got, 0, c), pair_at(got, 1, c), pair_at(sent, 0, c)
            g_rate = spread(got[FACE:, :], c)
            if ok is not None:
                g0, g1 = (tuple(jnp.where(ok, t, 0.0) for t in g) for g in (g0, g1))
                g_rate = jnp.where(ok, g_rate, 0.0)
            kept[2 * PLANE + c * BZ : 2 * PLANE + c * BZ + BZ, :] = g_rate
            ghost.append(g0)
            g_scale = 1.0 / (1.0 + 6.0 * g_rate)
            sums = inner(g0, lane, sub, swap)
            for h in range(2):
                value = (g0[h] + g_rate * (sums[h] + g1[h] + own[h])) * g_scale
                if ok is not None:
                    value = jnp.where(ok, value, 0.0)
                row = (h * NC + c) * BZ
                kept[row : row + BZ, :] = value
        low = [jnp.where(x_first, b, a) for a, b in zip(*ghost)]
        high = [jnp.where(x_first, a, b) for a, b in zip(*ghost)]
        for x in range(E):
            here = tile_at(moved, c, x)
            before = low if x == 0 else tile_at(moved, c, x - 1)
            after = high if x == E - 1 else tile_at(moved, c, x + 1)
            sums = inner(here, lane, sub, swap)
            row = (c * E + x) * BZ
            for h in range(2):
                out[h, row : row + BZ, :] = (here[h] + rate * (sums[h] + before[h] + after[h])) * scale
    every = [(h, c, k) for c in range(NC) for h in range(2) for k in range(E // 2)]
    d = []
    for h, c, k in every:
        row = (c * E + 2 * k) * BZ
        d.append(out[h, row : row + BZ, :] + out[h, row + BZ : row + 2 * BZ, :])
    d = z_differences(d, sub, upper)
    d = [t + r for t, r in zip(d, [rl(t, -E) for t in d])]
    d = [rl(t, k) for t, (_, _, k) in zip(d, every)]
    faces = {}
    for t, (h, c, k) in zip(d, every):
        faces[h, c] = t if k == 0 else jnp.where(z == k, t, faces[h, c])
    y8 = lane % 8
    source = (y8 % 4) * (2 * E) + lane // E
    picked = {key: pick_lanes(t, source) for key, t in faces.items()}
    for c in range(NC):
        top = jnp.where(y8 < 4, picked[0, c], picked[1, c])
        tops[c * BZ : c * BZ + BZ, :] = jnp.where(z // 8 == gy % 2, top, 0.0)


def coarse_plane(pair, parity, lane, sub):
    sums = []
    for t in pair:
        t = t + rl(t, -1)
        sums.append(t + rl(t, -E))
    source = (lane // E % 4) * (2 * E) + 2 * (lane % 8)
    out = jnp.where(lane < L // 2, pick_lanes(sums[0], source), pick_lanes(sums[1], source))
    return jnp.where(lane % E // 8 == sub % 2, 0.25 * out, 0.0)


def strips(low, high, x, low_lane, high_lane):
    shift = E * (x % 8)
    return (
        jnp.where(low_lane, rl(low[x // 8], -shift), 0.0),
        jnp.where(high_lane, rl(high[x // 8], L - E - shift), 0.0),
    )


def corner(extra, low_lane, high_lane):
    return jnp.where(low_lane, extra, 0.0), jnp.where(high_lane, rl(extra, L - 2 * E), 0.0)


def y_ghosts(got, ok, c):
    g0, g1, extra = pair_at(got, 0, c), pair_at(got, 1, c), extra_at(got, c)
    if ok is not None:
        g0, g1 = (tuple(jnp.where(ok, t, 0.0) for t in g) for g in (g0, g1))
        extra = jnp.where(ok, extra, 0.0)
    return g0, g1, extra


def y_first_sweep(got, sent, ok, ghost, c, lane, sub, swap):
    g0, g1, extra = ghost
    own = pair_at(sent, 0, c)
    g_rate = y_rate(got, c)
    if ok is not None:
        g_rate = jnp.where(ok, g_rate, 0.0)
    g_scale = 1.0 / (1.0 + 6.0 * g_rate)
    sums, line = inner(g0, lane, sub, swap), corner(extra, lane < E, lane >= L - E)
    values = [(g0[h] + g_rate * (sums[h] + line[h] + g1[h] + own[h])) * g_scale for h in range(2)]
    return values if ok is None else [jnp.where(ok, t, 0.0) for t in values]


def x_first_sweep(part, ok, at_low, low_line, high_line, c, low_lane, high_lane):
    g_rate = part[2 * PLANE + c * BZ : 2 * PLANE + c * BZ + BZ, :]
    g_weight = g_rate / (1.0 + 6.0 * g_rate)
    bottom = jnp.where(at_low, low_line, rl(low_line, -E))
    top = jnp.where(at_low, rl(high_line, L - E), rl(high_line, L - 2 * E))
    values = []
    for h, (line, there) in enumerate(((bottom, low_lane), (top, high_lane))):
        row = (h * NC + c) * BZ
        values.append(part[row : row + BZ, :] + g_weight * jnp.where(there, line, 0.0))
    return values if ok is None else [jnp.where(ok, t, 0.0) for t in values]


def flux_kernel(
    shape, partial, moved_rates, masks, tops, link_first, far, near, far_sent, own_far, y_far, kept, sent
):
    x_first, y_first, link_ok, far_ok = ends(shape)
    gx, gy, _ = place_of(shape)
    par_x, par_y = gx % 2, gy % 2
    lane, sub = lanes(), subs()
    swap = swap_index(lane)
    upper = sub % 2 == 1
    z = lane % E
    low_lane, high_lane = lane < E, lane >= L - E
    each = range(NC)
    rate = [moved_rates[c * BZ : c * BZ + BZ, :] for c in each]
    scale = [1.0 / (1.0 + 6.0 * r) for r in rate]
    weight = [r * q for r, q in zip(rate, scale)]
    near_g = [y_ghosts(near, None, c) for c in each]
    far_g = [y_ghosts(far, far_ok, c) for c in each]
    far_f = []
    for c in each:
        values = y_first_sweep(far, far_sent, far_ok, far_g[c], c, lane, sub, swap)
        for h in range(2):
            row = (h * NC + c) * BZ
            y_far[row : row + BZ, :] = values[h]
        far_f.append(values)
    far_r = [g[0] for g in far_g]

    def by_side(which, c):
        a, b = near_g[c][which], far_g[c][which]
        if which == 2:
            return jnp.where(y_first, b, a), jnp.where(y_first, a, b)
        return [jnp.where(y_first, q, p) for p, q in zip(a, b)], [jnp.where(y_first, p, q) for p, q in zip(a, b)]

    faces_y = []
    for c in each:
        own = pair_at(own_far, 0, c)
        flux = [far_f[c][h] - own[h] - weight[c] * far_r[c][h] for h in range(2)]
        face = coarse_plane(flux, par_x, lane, sub) * (rate[c] * masks[BZ : 2 * BZ, :])
        faces_y.append(face + rs(face, 1))
    faces_x = []
    for c in each:
        ghost = x_first_sweep(link_first, link_ok, x_first, *by_side(2, c), c, low_lane, high_lane)
        low_r, high_r = by_side(0, c)
        at_0, at_15 = (strips(low_r, high_r, x, low_lane, high_lane) for x in (0, E - 1))
        cells_0, cells_15 = tile_at(partial, c, 0), tile_at(partial, c, E - 1)
        flux = []
        for h in range(2):
            cell = jnp.where(x_first, cells_0[h], cells_15[h])
            cell = cell + weight[c] * jnp.where(x_first, at_0[h], at_15[h])
            flux.append(ghost[h] - cell)
        face = coarse_plane(flux, par_y, lane, sub) * (rate[c] * masks[0:BZ, :])
        faces_x.append(face + rs(face, -1))
    faces_z = []
    source = (lane // E % 4) * (2 * E) + jnp.where(lane % 8 == 7, 7, 0)
    d = []
    for c in each:
        for side in by_side(0, c):
            d += [weight[c] * t for t in side]
    d = [t + r for t, r in zip(d, [rl(t, -E) for t in d])]
    d = z_differences(d, sub, upper)
    halves = []
    for c in each:
        for h in range(2):
            halves.append(jnp.where(z == 7, rl(d[4 * c + 2 + h], 7), d[4 * c + h]))
    halves = [pick_lanes(t, source) for t in halves]
    for c in each:
        add = jnp.where(lane < L // 2, halves[2 * c], halves[2 * c + 1])
        add = jnp.where((z == 8 * par_y) | (z == 8 * par_y + 7), add, 0.0)
        faces_z.append((tops[c * BZ : c * BZ + BZ, :] + add) * (0.25 * rate[c] * masks[2 * BZ :, :]))
    left = sub % 4 < 2
    for c in each:
        outer = jnp.where(upper, faces_y[c], faces_x[c])
        columns = (jnp.where(left, outer, rs(faces_z[c], 2)), jnp.where(left, rs(outer, -2), faces_z[c]))
        row = c * BZ
        kept[row : row + BZ, :] = jnp.where(y_first, columns[0], columns[1])
        sent[row : row + BZ, :] = jnp.where(y_first, columns[1], columns[0])


def register_kernel(shape, kept, by_both, by_column, by_row, _, out):
    x_first, y_first, _, _ = ends(shape)
    sub = subs()
    for c in range(NC):
        own, column, row, both = (ref[c * BZ : c * BZ + BZ, :] for ref in (kept, by_column, by_row, by_both))
        m, m4, g, g4 = (jnp.where(x_first, t, rs(t, 4)) for t in (own, column, row, both))
        for h in range(2):
            same_y, same_x = (y_first, x_first) if h == 0 else (~y_first, ~x_first)
            a, b = jnp.where(same_y, m, m4), jnp.where(same_y, g, g4)
            x0, x1 = jnp.where(x_first, a, b), jnp.where(x_first, b, a)
            t, t4 = jnp.where(same_x, m, g), jnp.where(same_x, m4, g4)
            y0, y1 = jnp.where(y_first, rs(t, 1), rs(t4, 1)), jnp.where(y_first, rs(t4, 2), rs(t, 2))
            rows = jnp.where(sub == 0, x0, jnp.where(sub == 1, rs(x1, 1), rs(t + t4, 2)))
            rows = jnp.where(sub == 2, y0, jnp.where(sub == 3, y1, rows))
            out[0, 0, c, :, h * L : h * L + L] = rows[:6]


def second_kernel(shape, moved, rates, partial, core_first, link_first, far_sent, out, own_far):
    x_first, _, _, _ = ends(shape)
    lane, sub = lanes(), subs()
    swap = swap_index(lane)
    for c in range(NC):
        rate = rates[c * BZ : c * BZ + BZ, :]
        scale = 1.0 / (1.0 + 6.0 * rate)
        own, own1 = pair_at(far_sent, 0, c), pair_at(far_sent, 1, c)
        sums, line = inner(own, lane, sub, swap), corner(extra_at(far_sent, c), lane < E, lane >= L - E)
        for h in range(2):
            row = (h * NC + c) * BZ
            own_far[row : row + BZ, :] = (own[h] + rate * (sums[h] + line[h] + own1[h])) * scale
        core, link = pair_at(core_first, 0, c), pair_at(link_first, 0, c)
        low = [jnp.where(x_first, b, a) for a, b in zip(core, link)]
        high = [jnp.where(x_first, a, b) for a, b in zip(core, link)]
        for x in range(E):
            here = tile_at(partial, c, x)
            before = low if x == 0 else tile_at(partial, c, x - 1)
            after = high if x == E - 1 else tile_at(partial, c, x + 1)
            sums = inner(here, lane, sub, swap)
            start = tile_at(moved, c, x)
            row = (c * E + x) * BZ
            for h in range(2):
                out[h, row : row + BZ, :] = start[h] + rate * (sums[h] + before[h] + after[h])


def smooth_kernel(
    shape, rates, partial, core_first, link_first, far, near, near_sent, y_far, out, done, planes, held, boxes, sem
):
    done[...] = jnp.zeros((BZ, L), F32)
    x_first, y_first, _, far_ok = ends(shape)
    lane, sub = lanes(), subs()
    swap = swap_index(lane)
    low_lane, high_lane = lane < E, lane >= L - E

    def by_side(a, b, a_first):
        low = [jnp.where(a_first, q, p) for p, q in zip(a, b)]
        high = [jnp.where(a_first, p, q) for p, q in zip(a, b)]
        return low, high

    for c in range(NC):
        rate = rates[c * BZ : c * BZ + BZ, :]
        weight = rate / (1.0 + 6.0 * rate)
        near_g, far_g = y_ghosts(near, None, c), y_ghosts(far, far_ok, c)
        near_f = y_first_sweep(near, near_sent, None, near_g, c, lane, sub, swap)
        ghosts_f = by_side(near_f, pair_at(y_far, 0, c), y_first)
        ghosts_r = by_side(near_g[0], far_g[0], y_first)
        lines = by_side(near_g[2:], far_g[2:], y_first)
        x_rates = [ref[2 * PLANE + c * BZ : 2 * PLANE + c * BZ + BZ, :] for ref in (core_first, link_first)]
        x_weights = [t / (1.0 + 6.0 * t) for t in x_rates]
        (low_w,), (high_w,) = by_side(x_weights[:1], x_weights[1:], x_first)
        for side in range(2):
            added = [weight * t for t in ghosts_r[side]]
            (line,) = lines[side]
            sums = inner(added, lane, sub, swap)
            ends_ = (jnp.where(low_lane, low_w * line, 0.0), jnp.where(high_lane, high_w * rl(line, L - 2 * E), 0.0))
            for h in range(2):
                row = ((side * 2 + h) * NC + c) * BZ
                planes[0, row : row + BZ, :] = rate * (sums[h] + ends_[h] + ghosts_f[side][h])
                planes[1, row : row + BZ, :] = rate * added[h]
    next_low = (lane >= E) & (lane < 2 * E)
    next_high = (lane >= L - 2 * E) & (lane < L - E)
    copies = []
    for c in range(NC):
        rate = rates[c * BZ : c * BZ + BZ, :]
        scale = 1.0 / (1.0 + 6.0 * rate)
        for x in range(E):
            row = (c * E + x) * BZ
            shift = E * (x % 8)
            for h, (here, there, at) in enumerate(((low_lane, next_low, 0), (high_lane, next_high, L - E))):
                plane = ((h * 2 + x // 8) * NC + c) * BZ
                first = rl(planes[0, plane : plane + BZ, :], at - shift)
                second = rl(planes[1, plane : plane + BZ, :], (at - E if h else E) - shift)
                add = jnp.where(here, first, jnp.where(there, second, 0.0))
                held[h, row : row + BZ, :] = (partial[h, row : row + BZ, :] + add) * scale
        for s in range(BZ):
            for h in range(2):
                boxes[c, s, :, h * L : h * L + L] = held[h, pl.ds(c * E * BZ + s, E, stride=BZ), :]
        copies.append(pltpu.make_async_copy(boxes.at[c], out.at[0, 0, :, c], sem.at[c]))
        copies[-1].start()
    for copy in copies:
        copy.wait()


def body(shape, fields_old, coeff_old, new_place, cf_mask):
    rows, columns = shape
    count = rows * columns
    both = ("gx", "gy")

    def swap(array, pairs):
        return lax.ppermute(array, both, pairs)

    even_pairs = [(i, i ^ 1) for i in range(count)]
    odd_pairs = [(i, (i + 1) % count if i % 2 else (i - 1) % count) for i in range(count)]
    at = lambda a, b: a * columns + b
    core_pairs = [(at(a, b), at(a ^ 1, b)) for a in range(rows) for b in range(columns)]
    both_pairs = [(at(a, b), at(a ^ 1, b ^ 1)) for a in range(rows) for b in range(columns)]
    link_pairs = [
        (at(a, b), at((a + 1) % rows if a % 2 else (a - 1) % rows, b)) for a in range(rows) for b in range(columns)
    ]
    far_pairs = [
        (at(a, b), at(a ^ 1, b) if b in (0, columns - 1) else at(a, b + 1 if b % 2 else b - 1))
        for a in range(rows)
        for b in range(columns)
    ]
    k = lambda f: functools.partial(f, shape)
    coeff_old = coeff_old.transpose(0, 3, 1, 2)
    cf_mask = cf_mask.transpose(0, 2, 1, 3)
    big = (2, NC * E * BZ, L)

    plane = ((2 * PLANE, L), "vmem")
    even, odd, even_rest, odd_rest, boxes, slots, rates, masks = call(
        k(pack_kernel),
        [(a, "hbm") for a in (new_place, coeff_old, cf_mask, fields_old)],
        [
            ((PARCEL, 2 * L), "vmem"),
            ((PARCEL, 2 * L), "vmem"),
            ((REST, 2 * L), "vmem"),
            ((REST, 2 * L), "vmem"),
            ((BZ, NC, E, 2 * L), "vmem"),
            ((BZ, L), "vmem"),
            ((PLANE, L), "vmem"),
            ((3 * BZ, L), "vmem"),
        ],
        [
            SM((1, 1, BZ), I32),
            SM((1, NC, 1, BZ), F32),
            SM((1, 3, 1, BZ), I32),
            pltpu.SemaphoreType.DMA((4,)),
        ],
    )
    even_got = swap(even, even_pairs)
    odd_got = swap(odd, odd_pairs)
    even_rest_got = swap(even_rest, even_pairs)
    odd_rest_got = swap(odd_rest, odd_pairs)
    core, link, rates = call(
        k(xsend_kernel),
        [(a, "vmem") for a in (even_got, odd_got, boxes, slots, rates)],
        [((XFACE, L), "vmem"), ((XFACE, L), "vmem"), ((PLANE, L), "vmem")],
    )
    (stayed,) = call(k(stay_kernel), [(boxes, "vmem"), (slots, "vmem")], [(big, "vmem")])
    core_got = swap(core, core_pairs)
    link_got = swap(link, link_pairs)
    moved, near, far = call(
        k(merge_kernel),
        [(a, "vmem") for a in (even_got, odd_got, even_rest_got, odd_rest_got, stayed)],
        [(big, "vmem"), ((FACE, L), "vmem"), ((FACE, L), "vmem")],
    )
    near, far = call(
        k(ysend_kernel),
        [(a, "vmem") for a in (link_got, core_got, rates, near, far)],
        [((YFACE, L), "vmem"), ((YFACE, L), "vmem")],
    )
    near_got = swap(near, even_pairs)
    far_got = swap(far, far_pairs)
    part, core_first, link_first, tops = call(
        k(sweep_kernel),
        [(a, "vmem") for a in (moved, rates, link_got, core_got, core, link)],
        [(big, "vmem"), ((3 * PLANE, L), "vmem"), ((3 * PLANE, L), "vmem"), ((PLANE, L), "vmem")],
    )
    second, own_far = call(
        k(second_kernel),
        [(a, "vmem") for a in (moved, rates, part, core_first, link_first, far)],
        [(big, "vmem"), plane],
    )
    y_far, kept, sent = call(
        k(flux_kernel),
        [(a, "vmem") for a in (part, rates, masks, tops, link_first, far_got, near_got, far, own_far)],
        [plane, ((PLANE, L), "vmem"), ((PLANE, L), "vmem")],
    )
    by_both = swap(sent, both_pairs)
    by_column = swap(sent, even_pairs)
    by_row = swap(kept, core_pairs)
    smoothed, done = call(
        k(smooth_kernel),
        [(a, "vmem") for a in (rates, second, core_first, link_first, far_got, near_got, near, y_far)],
        [((1, 1, BZ, NC, E, 2 * L), "hbm"), ((BZ, L), "vmem")],
        [
            VM((2, 4 * PLANE, L), F32),
            VM(big, F32),
            VM((NC, BZ, E, 2 * L), F32),
            pltpu.SemaphoreType.DMA((NC,)),
        ],
    )
    (registers,) = call(
        k(register_kernel),
        [(a, "vmem") for a in (kept, by_both, by_column, by_row, done)],
        [((1, 1, NC, 6, 2 * L), "out")],
    )
    return smoothed, registers


def solution(mesh):
    shape = (mesh.shape["gx"], mesh.shape["gy"])
    return jax.shard_map(
        functools.partial(body, shape),
        mesh=mesh,
        in_specs=(
            P("gx", "gy", None, None, None, None),
            P("gx", "gy", None, None),
            P("gx", "gy", None),
            P("gx", "gy", None, None),
        ),
        out_specs=(P("gx", "gy", None, None, None, None), P("gx", "gy", None, None, None)),
        check_vma=False,
    )
```

```python
import functools

import jax
import jax.numpy as jnp
from jax import lax
from jax.experimental import pallas as pl
from jax.experimental.pallas import tpu as pltpu
from jax.sharding import PartitionSpec as P

NC = 5
E = 16
BZ = 8
MOVE = 2
L = 128
F32 = jnp.float32
I32 = jnp.int32

PLANE = NC * BZ
FACE = 4 * PLANE
EDGES = (0, 1, E - 2, E - 1)
AHEAD = MOVE * NC * 4
PARCEL = 48
REST = MOVE * NC * 12
XFACE = FACE + BZ
YFACE = FACE + 2 * BZ
YNEAR = 2 * PLANE + 2 * BZ

VM = pltpu.VMEM
SM = pltpu.SMEM


def call(kernel, ins, outs, scratch=(), aliases=None, flops=1000, **kw):
    given, in_specs = [], []
    for array, space in ins:
        if space == "vmem":
            given.append(pltpu.with_memory_space_constraint(array, VM))
            in_specs.append(pl.BlockSpec(memory_space=VM))
        else:
            given.append(pltpu.with_memory_space_constraint(array, pltpu.HBM))
            in_specs.append(pl.BlockSpec(memory_space=pltpu.HBM))
    shapes, out_specs = [], []
    for shape, space in outs:
        if space == "vmem":
            shapes.append(VM(shape, F32))
            out_specs.append(pl.BlockSpec(memory_space=VM))
        else:
            shapes.append(jax.ShapeDtypeStruct(shape, F32))
            out_specs.append(pl.BlockSpec(memory_space=pltpu.HBM if space == "hbm" else VM))
    return pl.pallas_call(
        kernel,
        out_shape=shapes,
        in_specs=in_specs,
        out_specs=out_specs,
        scratch_shapes=list(scratch),
        input_output_aliases=aliases or {},
        cost_estimate=pl.CostEstimate(flops=flops, bytes_accessed=0, transcendentals=0),
        compiler_params=pltpu.CompilerParams(vmem_limit_bytes=24 * 1024 * 1024),
        **kw,
    )(*given)


def lanes():
    return lax.broadcasted_iota(I32, (BZ, L), 1)


def subs():
    return lax.broadcasted_iota(I32, (BZ, L), 0)


def rl(x, shift):
    shift %= L
    return x if shift == 0 else pltpu.roll(x, shift, 1)


def rs(x, shift):
    shift %= BZ
    return x if shift == 0 else pltpu.roll(x, shift, 0)


def pick_lanes(x, index):
    return jnp.take_along_axis(x, index, axis=1)


def place_of(mesh_shape):
    gx = lax.axis_index("gx")
    gy = lax.axis_index("gy")
    return gx, gy, gx * mesh_shape[1] + gy


def sources_of(place, owner):
    count = jnp.int32(0)
    sources = [jnp.int32(0)] * MOVE
    labels = [jnp.int32(0)] * MOVE
    for s in range(BZ):
        value = place[s]
        hit = value // BZ == owner
        for k in range(MOVE):
            taken = hit & (count == k)
            sources[k] = jnp.where(taken, s, sources[k])
            labels[k] = jnp.where(taken, value % BZ + 1, labels[k])
        count = count + hit.astype(I32)
    return sources, labels


def fill_rest(rest, boxes, sources):
    for k in range(MOVE):
        for c in range(NC):
            box = k * NC + c
            rest[12 * box : 12 * box + 12, :] = boxes[sources[k], c, 2 : E - 2]


def pack_kernel(
    shape, place_hbm, coeff_hbm, mask_hbm, fields_hbm, even, odd, even_rest, odd_rest, boxes, slots, rates, masks,
    place_s, coeff, mask, sem,
):
    pairs = ((fields_hbm.at[0, 0], boxes), (place_hbm, place_s), (coeff_hbm, coeff), (mask_hbm, mask))
    copies = [pltpu.make_async_copy(a, b, sem.at[i]) for i, (a, b) in enumerate(pairs)]
    for copy in copies:
        copy.start()
    _, _, me = place_of(shape)
    ahead = 1 - 2 * (me % 2)
    lane = lax.broadcasted_iota(I32, (1, L), 1)
    for copy in copies[1:]:
        copy.wait()
    place = [place_s[0, 0, s] for s in range(BZ)]
    chosen = [sources_of(place, me + ahead), sources_of(place, me - ahead)]
    for out, (sources, labels) in zip((even, odd), chosen):
        out[AHEAD:PARCEL, :] = jnp.zeros((PARCEL - AHEAD, 2 * L), F32)
        for k in range(MOVE):
            out[AHEAD + k : AHEAD + k + 1, L:] = jnp.full((1, L), labels[k].astype(F32), F32)
            line = jnp.zeros((1, L), F32)
            for c in range(NC):
                line = jnp.where(lane == c, coeff[0, c, 0, sources[k]], line)
            out[AHEAD + k : AHEAD + k + 1, :L] = line
    for s in range(BZ):
        label = jnp.where(place[s] // BZ == me, place[s] % BZ + 1, 0)
        slots[s : s + 1, :] = jnp.full((1, L), label.astype(F32), F32)
        for c in range(NC):
            rates[s * NC + c : s * NC + c + 1, :] = jnp.full((1, L), coeff[0, c, 0, s], F32)
        for d in range(3):
            masks[d * BZ + s : d * BZ + s + 1, :] = jnp.full((1, L), mask[0, d, 0, s].astype(F32), F32)
    copies[0].wait()
    for out, rest, (sources, _) in zip((even, odd), (even_rest, odd_rest), chosen):
        for k in range(MOVE):
            for c in range(NC):
                box = k * NC + c
                out[4 * box : 4 * box + 2, :] = boxes[sources[k], c, :2]
                out[4 * box + 2 : 4 * box + 4, :] = boxes[sources[k], c, E - 2 :]
                rest[12 * box : 12 * box + 12, :] = boxes[sources[k], c, 2 : E - 2]


def stays(slots):
    label = (subs() + 1).astype(F32)
    return [slots[s : s + 1, :] == label for s in range(BZ)]


def stayed_tile(found, boxes, c, x, h):
    tile = jnp.zeros((BZ, L), F32)
    for s in range(BZ):
        tile = jnp.where(found[s], boxes[s, c, x : x + 1, h * L : h * L + L], tile)
    return tile


def stay_kernel(shape, boxes, slots, moved):
    found = stays(slots)
    for c in range(NC):
        for x in range(E):
            row = (c * E + x) * BZ
            for h in range(2):
                moved[h, row : row + BZ, :] = stayed_tile(found, boxes, c, x, h)


def arrivals(even, odd):
    sub = subs()
    found = []
    for parcel in (even, odd):
        for k in range(MOVE):
            label = parcel[AHEAD + k : AHEAD + k + 1, L:]
            found.append((parcel, k, label == (sub + 1).astype(F32)))
    return found


def merged(found, tile, c, x, h, rests=None):
    for i, (parcel, k, hit) in enumerate(found):
        if x in EDGES:
            source, at = parcel, (k * NC + c) * 4 + EDGES.index(x)
        else:
            source, at = rests[i // MOVE], (k * NC + c) * 12 + x - 2
        tile = jnp.where(hit, source[at : at + 1, h * L : h * L + L], tile)
    return tile


def spread(tile, lane):
    return pick_lanes(tile, jnp.full((BZ, L), lane, I32))


def plane_row(layer, h, c):
    return ((layer * 2 + h) * NC + c) * BZ


def xsend_kernel(shape, even, odd, boxes, slots, old_rates, core, link, rates):
    gx, _, _ = place_of(shape)
    first = gx % 2 == 0
    kept, found = stays(slots), arrivals(even, odd)
    lane = lanes()
    together = jnp.zeros((BZ, L), F32)
    for c in range(NC):
        tile = jnp.zeros((BZ, L), F32)
        for s in range(BZ):
            tile = jnp.where(kept[s], old_rates[s * NC + c : s * NC + c + 1, :], tile)
        for parcel, k, hit in found:
            line = jnp.broadcast_to(parcel[AHEAD + k : AHEAD + k + 1, :L], (BZ, L))
            tile = jnp.where(hit, spread(line, c), tile)
        rates[c * BZ : c * BZ + BZ, :] = tile
        together = jnp.where(lane == c, tile, together)
        for layer in range(2):
            for h in range(2):
                sides = [merged(found, stayed_tile(kept, boxes, c, x, h), c, x, h) for x in (layer, E - 1 - layer)]
                at = plane_row(layer, h, c)
                core[at : at + BZ, :] = jnp.where(first, sides[1], sides[0])
                link[at : at + BZ, :] = jnp.where(first, sides[0], sides[1])
    core[FACE:, :] = together
    link[FACE:, :] = together


def merge_kernel(shape, even, odd, even_rest, odd_rest, moved, out, near, far):
    _, gy, _ = place_of(shape)
    first = gy % 2 == 0
    found = arrivals(even, odd)
    lane = lanes()
    for c in range(NC):
        low = [[None, None], [None, None]]
        high = [[None, None], [None, None]]
        for x in range(E):
            row = (c * E + x) * BZ
            at = L // 8 * (x % 8)
            here = lane // E == x % 8
            half = x // 8
            for h in range(2):
                tile = merged(found, moved[h, row : row + BZ, :], c, x, h, (even_rest, odd_rest))
                out[h, row : row + BZ, :] = tile
                for layer in range(2):
                    keep, start = ((low, E * layer) if h == 0 else (high, L - E - E * layer))
                    strip = rl(tile, at - start)
                    old = keep[layer][half]
                    keep[layer][half] = strip if old is None else jnp.where(here, strip, old)
        for layer in range(2):
            for h in range(2):
                at = plane_row(layer, h, c)
                near[at : at + BZ, :] = jnp.where(first, high[layer][h], low[layer][h])
                far[at : at + BZ, :] = jnp.where(first, low[layer][h], high[layer][h])


def ends(shape):
    gx, gy, _ = place_of(shape)
    x_first, y_first = gx % 2 == 0, gy % 2 == 0
    link_ok = jnp.where(x_first, gx > 0, gx < shape[0] - 1)
    far_ok = jnp.where(y_first, gy > 0, gy < shape[1] - 1)
    return x_first, y_first, link_ok, far_ok


def ysend_kernel(shape, link, core, rates, near, far, near_out, next_out, far_out):
    x_first, y_first, link_ok, _ = ends(shape)
    lane = lanes()
    near_out[: 2 * PLANE, :] = near[: 2 * PLANE, :]
    next_out[...] = near[2 * PLANE :, :]
    far_out[:FACE, :] = far[...]
    bottoms = [jnp.zeros((BZ, L), F32)] * 2
    tops = [jnp.zeros((BZ, L), F32)] * 2
    for c in range(NC):
        lines = []
        for h in range(2):
            at = plane_row(0, h, c)
            a = core[at : at + BZ, :]
            b = jnp.where(link_ok, link[at : at + BZ, :], 0.0)
            lines.append((jnp.where(x_first, b, a), jnp.where(x_first, a, b)))
        i, at = divmod(c, 4)
        at *= 2 * E
        low = (lane >= at) & (lane < at + E)
        high = (lane >= at + E) & (lane < at + 2 * E)
        bottoms[i] = jnp.where(low, rl(lines[0][0], at), jnp.where(high, rl(lines[0][1], at + E), bottoms[i]))
        tops[i] = jnp.where(low, rl(lines[1][0], at + E), jnp.where(high, rl(lines[1][1], at + 2 * E), tops[i]))
        rate = rates[c * BZ : c * BZ + BZ, :]
        bottoms[1] = jnp.where(lane == L // 2 + c, rate, bottoms[1])
        tops[1] = jnp.where(lane == L // 2 + c, rate, tops[1])
    for i in range(2):
        at = FACE + i * BZ
        near_out[at - 2 * PLANE : at - 2 * PLANE + BZ, :] = jnp.where(y_first, tops[i], bottoms[i])
        far_out[at : at + BZ, :] = jnp.where(y_first, bottoms[i], tops[i])


def extra_at(ref, c, start=FACE):
    i, at = divmod(c, 4)
    return rl(ref[start + i * BZ : start + i * BZ + BZ, :], -2 * E * at)


def y_rate(ref, c):
    return spread(ref[ref.shape[0] - BZ :, :], L // 2 + c)


def z_parts(x, lane, sub, swap):
    z = lane % E
    down = jnp.where(sub == 0, 0.0, rs(x, 1))
    up = jnp.where(sub == BZ - 1, 0.0, rs(x, -1))
    ends_ = pick_lanes(jnp.where(z == E - 1, down, up), swap)
    return jnp.where(z == 0, ends_, rl(x, 1)) + jnp.where(z == E - 1, ends_, rl(x, -1))


def swap_index(lane):
    z = lane % E
    return jnp.where(z == 0, lane + E - 1, jnp.where(z == E - 1, lane - E + 1, lane))


def inner(pair, lane, sub, swap):
    a, b = pair
    a1, b1, a2, b2 = rl(a, E), rl(b, E), rl(a, -E), rl(b, -E)
    low, high = lane < E, lane >= L - E
    first = jnp.where(low, 0.0, a1) + jnp.where(high, b2, a2) + z_parts(a, lane, sub, swap)
    second = jnp.where(low, a1, b1) + jnp.where(high, 0.0, b2) + z_parts(b, lane, sub, swap)
    return first, second


def pair_at(ref, layer, c):
    return tuple(ref[plane_row(layer, h, c) : plane_row(layer, h, c) + BZ, :] for h in range(2))


def tile_at(ref, c, x):
    row = (c * E + x) * BZ
    return tuple(ref[h, row : row + BZ, :] for h in range(2))


def z_differences(tiles, sub, upper):
    down = [jnp.where(sub == 0, 0.0, t) for t in [rs(t, 1) for t in tiles]]
    up = [jnp.where(sub == BZ - 1, 0.0, t) for t in [rs(t, -1) for t in tiles]]
    high = [rl(t, 1 - E) for t in [jnp.where(upper, t, d) for t, d in zip(tiles, down)]]
    return [jnp.where(upper, u - g, g - t) for g, u, t in zip(high, up, tiles)]


def sweep_kernel(shape, moved, rates, link, core, core_sent, link_sent, out, core_first, link_first, tops):
    x_first, _, link_ok, _ = ends(shape)
    _, gy, _ = place_of(shape)
    lane, sub = lanes(), subs()
    swap = swap_index(lane)
    upper = sub % 2 == 1
    z = lane % E
    for c in range(NC):
        rate = rates[c * BZ : c * BZ + BZ, :]
        scale = 1.0 / (1.0 + 6.0 * rate)
        ghost = []
        for got, sent, kept, ok in ((core, core_sent, core_first, None), (link, link_sent, link_first, link_ok)):
            g0, g1, own = pair_at(got, 0, c), pair_at(got, 1, c), pair_at(sent, 0, c)
            g_rate = spread(got[FACE:, :], c)
            if ok is not None:
                g0, g1 = (tuple(jnp.where(ok, t, 0.0) for t in g) for g in (g0, g1))
                g_rate = jnp.where(ok, g_rate, 0.0)
            kept[2 * PLANE + c * BZ : 2 * PLANE + c * BZ + BZ, :] = g_rate
            ghost.append(g0)
            g_scale = 1.0 / (1.0 + 6.0 * g_rate)
            sums = inner(g0, lane, sub, swap)
            for h in range(2):
                value = (g0[h] + g_rate * (sums[h] + g1[h] + own[h])) * g_scale
                if ok is not None:
                    value = jnp.where(ok, value, 0.0)
                row = (h * NC + c) * BZ
                kept[row : row + BZ, :] = value
        low = [jnp.where(x_first, b, a) for a, b in zip(*ghost)]
        high = [jnp.where(x_first, a, b) for a, b in zip(*ghost)]
        for x in range(E):
            here = tile_at(moved, c, x)
            before = low if x == 0 else tile_at(moved, c, x - 1)
            after = high if x == E - 1 else tile_at(moved, c, x + 1)
            sums = inner(here, lane, sub, swap)
            row = (c * E + x) * BZ
            for h in range(2):
                out[h, row : row + BZ, :] = (here[h] + rate * (sums[h] + before[h] + after[h])) * scale
    every = [(h, c, k) for c in range(NC) for h in range(2) for k in range(E // 2)]
    d = []
    for h, c, k in every:
        row = (c * E + 2 * k) * BZ
        d.append(out[h, row : row + BZ, :] + out[h, row + BZ : row + 2 * BZ, :])
    d = z_differences(d, sub, upper)
    d = [t + r for t, r in zip(d, [rl(t, -E) for t in d])]
    d = [rl(t, k) for t, (_, _, k) in zip(d, every)]
    faces = {}
    for t, (h, c, k) in zip(d, every):
        faces[h, c] = t if k == 0 else jnp.where(z == k, t, faces[h, c])
    y8 = lane % 8
    source = (y8 % 4) * (2 * E) + lane // E
    picked = {key: pick_lanes(t, source) for key, t in faces.items()}
    for c in range(NC):
        top = jnp.where(y8 < 4, picked[0, c], picked[1, c])
        tops[c * BZ : c * BZ + BZ, :] = jnp.where(z // 8 == gy % 2, top, 0.0)


def coarse_plane(pair, parity, lane, sub):
    sums = []
    for t in pair:
        t = t + rl(t, -1)
        sums.append(t + rl(t, -E))
    source = (lane // E % 4) * (2 * E) + 2 * (lane % 8)
    out = jnp.where(lane < L // 2, pick_lanes(sums[0], source), pick_lanes(sums[1], source))
    return jnp.where(lane % E // 8 == sub % 2, 0.25 * out, 0.0)


def strips(low, high, x, low_lane, high_lane):
    shift = E * (x % 8)
    return (
        jnp.where(low_lane, rl(low[x // 8], -shift), 0.0),
        jnp.where(high_lane, rl(high[x // 8], L - E - shift), 0.0),
    )


def corner(extra, low_lane, high_lane):
    return jnp.where(low_lane, extra, 0.0), jnp.where(high_lane, rl(extra, L - 2 * E), 0.0)


def y_ghosts(got, ok, c):
    g0, g1, extra = pair_at(got, 0, c), pair_at(got, 1, c), extra_at(got, c)
    if ok is not None:
        g0, g1 = (tuple(jnp.where(ok, t, 0.0) for t in g) for g in (g0, g1))
        extra = jnp.where(ok, extra, 0.0)
    return g0, g1, extra


def near_ghosts(got, following, c):
    second = None if following is None else pair_at(following, 0, c)
    return pair_at(got, 0, c), second, extra_at(got, c, 2 * PLANE)


def y_first_sweep(got, sent, ok, ghost, c, lane, sub, swap):
    g0, g1, extra = ghost
    own = pair_at(sent, 0, c)
    g_rate = y_rate(got, c)
    if ok is not None:
        g_rate = jnp.where(ok, g_rate, 0.0)
    g_scale = 1.0 / (1.0 + 6.0 * g_rate)
    sums, line = inner(g0, lane, sub, swap), corner(extra, lane < E, lane >= L - E)
    values = [(g0[h] + g_rate * (sums[h] + line[h] + g1[h] + own[h])) * g_scale for h in range(2)]
    return values if ok is None else [jnp.where(ok, t, 0.0) for t in values]


def x_first_sweep(part, ok, at_low, low_line, high_line, c, low_lane, high_lane):
    g_rate = part[2 * PLANE + c * BZ : 2 * PLANE + c * BZ + BZ, :]
    g_weight = g_rate / (1.0 + 6.0 * g_rate)
    bottom = jnp.where(at_low, low_line, rl(low_line, -E))
    top = jnp.where(at_low, rl(high_line, L - E), rl(high_line, L - 2 * E))
    values = []
    for h, (line, there) in enumerate(((bottom, low_lane), (top, high_lane))):
        row = (h * NC + c) * BZ
        values.append(part[row : row + BZ, :] + g_weight * jnp.where(there, line, 0.0))
    return values if ok is None else [jnp.where(ok, t, 0.0) for t in values]


def flux_kernel(
    shape, partial, moved_rates, masks, tops, link_first, far, near, far_sent, own_far, y_far, kept, sent
):
    x_first, y_first, link_ok, far_ok = ends(shape)
    gx, gy, _ = place_of(shape)
    par_x, par_y = gx % 2, gy % 2
    lane, sub = lanes(), subs()
    swap = swap_index(lane)
    upper = sub % 2 == 1
    z = lane % E
    low_lane, high_lane = lane < E, lane >= L - E
    each = range(NC)
    rate = [moved_rates[c * BZ : c * BZ + BZ, :] for c in each]
    scale = [1.0 / (1.0 + 6.0 * r) for r in rate]
    weight = [r * q for r, q in zip(rate, scale)]
    near_g = [near_ghosts(near, None, c) for c in each]
    far_g = [y_ghosts(far, far_ok, c) for c in each]
    far_f = []
    for c in each:
        values = y_first_sweep(far, far_sent, far_ok, far_g[c], c, lane, sub, swap)
        for h in range(2):
            row = (h * NC + c) * BZ
            y_far[row : row + BZ, :] = values[h]
        far_f.append(values)
    far_r = [g[0] for g in far_g]

    def by_side(which, c):
        a, b = near_g[c][which], far_g[c][which]
        if which == 2:
            return jnp.where(y_first, b, a), jnp.where(y_first, a, b)
        return [jnp.where(y_first, q, p) for p, q in zip(a, b)], [jnp.where(y_first, p, q) for p, q in zip(a, b)]

    faces_y = []
    for c in each:
        own = pair_at(own_far, 0, c)
        flux = [far_f[c][h] - own[h] - weight[c] * far_r[c][h] for h in range(2)]
        face = coarse_plane(flux, par_x, lane, sub) * (rate[c] * masks[BZ : 2 * BZ, :])
        faces_y.append(face + rs(face, 1))
    faces_x = []
    for c in each:
        ghost = x_first_sweep(link_first, link_ok, x_first, *by_side(2, c), c, low_lane, high_lane)
        low_r, high_r = by_side(0, c)
        at_0, at_15 = (strips(low_r, high_r, x, low_lane, high_lane) for x in (0, E - 1))
        cells_0, cells_15 = tile_at(partial, c, 0), tile_at(partial, c, E - 1)
        flux = []
        for h in range(2):
            cell = jnp.where(x_first, cells_0[h], cells_15[h])
            cell = cell + weight[c] * jnp.where(x_first, at_0[h], at_15[h])
            flux.append(ghost[h] - cell)
        face = coarse_plane(flux, par_y, lane, sub) * (rate[c] * masks[0:BZ, :])
        faces_x.append(face + rs(face, -1))
    faces_z = []
    source = (lane // E % 4) * (2 * E) + jnp.where(lane % 8 == 7, 7, 0)
    d = []
    for c in each:
        for side in by_side(0, c):
            d += [weight[c] * t for t in side]
    d = [t + r for t, r in zip(d, [rl(t, -E) for t in d])]
    d = z_differences(d, sub, upper)
    halves = []
    for c in each:
        for h in range(2):
            halves.append(jnp.where(z == 7, rl(d[4 * c + 2 + h], 7), d[4 * c + h]))
    halves = [pick_lanes(t, source) for t in halves]
    for c in each:
        add = jnp.where(lane < L // 2, halves[2 * c], halves[2 * c + 1])
        add = jnp.where((z == 8 * par_y) | (z == 8 * par_y + 7), add, 0.0)
        faces_z.append((tops[c * BZ : c * BZ + BZ, :] + add) * (0.25 * rate[c] * masks[2 * BZ :, :]))
    left = sub % 4 < 2
    for c in each:
        outer = jnp.where(upper, faces_y[c], faces_x[c])
        columns = (jnp.where(left, outer, rs(faces_z[c], 2)), jnp.where(left, rs(outer, -2), faces_z[c]))
        row = c * BZ
        kept[row : row + BZ, :] = jnp.where(y_first, columns[0], columns[1])
        sent[row : row + BZ, :] = jnp.where(y_first, columns[1], columns[0])


def register_kernel(shape, kept, by_both, by_column, by_row, _, out):
    x_first, y_first, _, _ = ends(shape)
    sub = subs()
    for c in range(NC):
        own, column, row, both = (ref[c * BZ : c * BZ + BZ, :] for ref in (kept, by_column, by_row, by_both))
        m, m4, g, g4 = (jnp.where(x_first, t, rs(t, 4)) for t in (own, column, row, both))
        for h in range(2):
            same_y, same_x = (y_first, x_first) if h == 0 else (~y_first, ~x_first)
            a, b = jnp.where(same_y, m, m4), jnp.where(same_y, g, g4)
            x0, x1 = jnp.where(x_first, a, b), jnp.where(x_first, b, a)
            t, t4 = jnp.where(same_x, m, g), jnp.where(same_x, m4, g4)
            y0, y1 = jnp.where(y_first, rs(t, 1), rs(t4, 1)), jnp.where(y_first, rs(t4, 2), rs(t, 2))
            rows = jnp.where(sub == 0, x0, jnp.where(sub == 1, rs(x1, 1), rs(t + t4, 2)))
            rows = jnp.where(sub == 2, y0, jnp.where(sub == 3, y1, rows))
            out[0, 0, c, :, h * L : h * L + L] = rows[:6]


def second_kernel(shape, moved, rates, partial, core_first, link_first, far_sent, out, own_far):
    x_first, _, _, _ = ends(shape)
    lane, sub = lanes(), subs()
    swap = swap_index(lane)
    for c in range(NC):
        rate = rates[c * BZ : c * BZ + BZ, :]
        scale = 1.0 / (1.0 + 6.0 * rate)
        own, own1 = pair_at(far_sent, 0, c), pair_at(far_sent, 1, c)
        sums, line = inner(own, lane, sub, swap), corner(extra_at(far_sent, c), lane < E, lane >= L - E)
        for h in range(2):
            row = (h * NC + c) * BZ
            own_far[row : row + BZ, :] = (own[h] + rate * (sums[h] + line[h] + own1[h])) * scale
        core, link = pair_at(core_first, 0, c), pair_at(link_first, 0, c)
        low = [jnp.where(x_first, b, a) for a, b in zip(core, link)]
        high = [jnp.where(x_first, a, b) for a, b in zip(core, link)]
        for x in range(E):
            here = tile_at(partial, c, x)
            before = low if x == 0 else tile_at(partial, c, x - 1)
            after = high if x == E - 1 else tile_at(partial, c, x + 1)
            sums = inner(here, lane, sub, swap)
            start = tile_at(moved, c, x)
            row = (c * E + x) * BZ
            for h in range(2):
                out[h, row : row + BZ, :] = start[h] + rate * (sums[h] + before[h] + after[h])


def smooth_kernel(
    shape, rates, partial, core_first, link_first, far, near, following, near_sent, y_far, out, done, planes, held, boxes, sem
):
    done[...] = jnp.zeros((BZ, L), F32)
    x_first, y_first, _, far_ok = ends(shape)
    lane, sub = lanes(), subs()
    swap = swap_index(lane)
    low_lane, high_lane = lane < E, lane >= L - E

    def by_side(a, b, a_first):
        low = [jnp.where(a_first, q, p) for p, q in zip(a, b)]
        high = [jnp.where(a_first, p, q) for p, q in zip(a, b)]
        return low, high

    for c in range(NC):
        rate = rates[c * BZ : c * BZ + BZ, :]
        weight = rate / (1.0 + 6.0 * rate)
        near_g, far_g = near_ghosts(near, following, c), y_ghosts(far, far_ok, c)
        near_f = y_first_sweep(near, near_sent, None, near_g, c, lane, sub, swap)
        ghosts_f = by_side(near_f, pair_at(y_far, 0, c), y_first)
        ghosts_r = by_side(near_g[0], far_g[0], y_first)
        lines = by_side(near_g[2:], far_g[2:], y_first)
        x_rates = [ref[2 * PLANE + c * BZ : 2 * PLANE + c * BZ + BZ, :] for ref in (core_first, link_first)]
        x_weights = [t / (1.0 + 6.0 * t) for t in x_rates]
        (low_w,), (high_w,) = by_side(x_weights[:1], x_weights[1:], x_first)
        for side in range(2):
            added = [weight * t for t in ghosts_r[side]]
            (line,) = lines[side]
            sums = inner(added, lane, sub, swap)
            ends_ = (jnp.where(low_lane, low_w * line, 0.0), jnp.where(high_lane, high_w * rl(line, L - 2 * E), 0.0))
            for h in range(2):
                row = ((side * 2 + h) * NC + c) * BZ
                planes[0, row : row + BZ, :] = rate * (sums[h] + ends_[h] + ghosts_f[side][h])
                planes[1, row : row + BZ, :] = rate * added[h]
    next_low = (lane >= E) & (lane < 2 * E)
    next_high = (lane >= L - 2 * E) & (lane < L - E)
    copies = []
    for c in range(NC):
        rate = rates[c * BZ : c * BZ + BZ, :]
        scale = 1.0 / (1.0 + 6.0 * rate)
        for x in range(E):
            row = (c * E + x) * BZ
            shift = E * (x % 8)
            for h, (here, there, at) in enumerate(((low_lane, next_low, 0), (high_lane, next_high, L - E))):
                plane = ((h * 2 + x // 8) * NC + c) * BZ
                first = rl(planes[0, plane : plane + BZ, :], at - shift)
                second = rl(planes[1, plane : plane + BZ, :], (at - E if h else E) - shift)
                add = jnp.where(here, first, jnp.where(there, second, 0.0))
                held[h, row : row + BZ, :] = (partial[h, row : row + BZ, :] + add) * scale
        for s in range(BZ):
            for h in range(2):
                boxes[c, s, :, h * L : h * L + L] = held[h, pl.ds(c * E * BZ + s, E, stride=BZ), :]
        copies.append(pltpu.make_async_copy(boxes.at[c], out.at[0, 0, :, c], sem.at[c]))
        copies[-1].start()
    for copy in copies:
        copy.wait()


def body(shape, fields_old, coeff_old, new_place, cf_mask):
    rows, columns = shape
    count = rows * columns
    both = ("gx", "gy")

    def swap(array, pairs):
        return lax.ppermute(array, both, pairs)

    even_pairs = [(i, i ^ 1) for i in range(count)]
    odd_pairs = [(i, (i + 1) % count if i % 2 else (i - 1) % count) for i in range(count)]
    at = lambda a, b: a * columns + b
    core_pairs = [(at(a, b), at(a ^ 1, b)) for a in range(rows) for b in range(columns)]
    both_pairs = [(at(a, b), at(a ^ 1, b ^ 1)) for a in range(rows) for b in range(columns)]
    link_pairs = [
        (at(a, b), at((a + 1) % rows if a % 2 else (a - 1) % rows, b)) for a in range(rows) for b in range(columns)
    ]
    far_pairs = [
        (at(a, b), at(a ^ 1, b) if b in (0, columns - 1) else at(a, b + 1 if b % 2 else b - 1))
        for a in range(rows)
        for b in range(columns)
    ]
    k = lambda f: functools.partial(f, shape)
    coeff_old = coeff_old.transpose(0, 3, 1, 2)
    cf_mask = cf_mask.transpose(0, 2, 1, 3)
    big = (2, NC * E * BZ, L)

    plane = ((2 * PLANE, L), "vmem")
    even, odd, even_rest, odd_rest, boxes, slots, rates, masks = call(
        k(pack_kernel),
        [(a, "hbm") for a in (new_place, coeff_old, cf_mask, fields_old)],
        [
            ((PARCEL, 2 * L), "vmem"),
            ((PARCEL, 2 * L), "vmem"),
            ((REST, 2 * L), "vmem"),
            ((REST, 2 * L), "vmem"),
            ((BZ, NC, E, 2 * L), "vmem"),
            ((BZ, L), "vmem"),
            ((PLANE, L), "vmem"),
            ((3 * BZ, L), "vmem"),
        ],
        [
            SM((1, 1, BZ), I32),
            SM((1, NC, 1, BZ), F32),
            SM((1, 3, 1, BZ), I32),
            pltpu.SemaphoreType.DMA((4,)),
        ],
    )
    even_got = swap(even, even_pairs)
    odd_got = swap(odd, odd_pairs)
    even_rest_got = swap(even_rest, even_pairs)
    odd_rest_got = swap(odd_rest, odd_pairs)
    core, link, rates = call(
        k(xsend_kernel),
        [(a, "vmem") for a in (even_got, odd_got, boxes, slots, rates)],
        [((XFACE, L), "vmem"), ((XFACE, L), "vmem"), ((PLANE, L), "vmem")],
    )
    (stayed,) = call(k(stay_kernel), [(boxes, "vmem"), (slots, "vmem")], [(big, "vmem")])
    core_got = swap(core, core_pairs)
    link_got = swap(link, link_pairs)
    moved, near, far = call(
        k(merge_kernel),
        [(a, "vmem") for a in (even_got, odd_got, even_rest_got, odd_rest_got, stayed)],
        [(big, "vmem"), ((FACE, L), "vmem"), ((FACE, L), "vmem")],
    )
    near, following, far = call(
        k(ysend_kernel),
        [(a, "vmem") for a in (link_got, core_got, rates, near, far)],
        [((YNEAR, L), "vmem"), ((2 * PLANE, L), "vmem"), ((YFACE, L), "vmem")],
    )
    near_got = swap(near, even_pairs)
    far_got = swap(far, far_pairs)
    next_got = swap(following, even_pairs)
    part, core_first, link_first, tops = call(
        k(sweep_kernel),
        [(a, "vmem") for a in (moved, rates, link_got, core_got, core, link)],
        [(big, "vmem"), ((3 * PLANE, L), "vmem"), ((3 * PLANE, L), "vmem"), ((PLANE, L), "vmem")],
    )
    second, own_far = call(
        k(second_kernel),
        [(a, "vmem") for a in (moved, rates, part, core_first, link_first, far)],
        [(big, "vmem"), plane],
    )
    y_far, kept, sent = call(
        k(flux_kernel),
        [(a, "vmem") for a in (part, rates, masks, tops, link_first, far_got, near_got, far, own_far)],
        [plane, ((PLANE, L), "vmem"), ((PLANE, L), "vmem")],
    )
    by_both = swap(sent, both_pairs)
    by_column = swap(sent, even_pairs)
    by_row = swap(kept, core_pairs)
    smoothed, done = call(
        k(smooth_kernel),
        [(a, "vmem") for a in (rates, second, core_first, link_first, far_got, near_got, next_got, near, y_far)],
        [((1, 1, BZ, NC, E, 2 * L), "hbm"), ((BZ, L), "vmem")],
        [
            VM((2, 4 * PLANE, L), F32),
            VM(big, F32),
            VM((NC, BZ, E, 2 * L), F32),
            pltpu.SemaphoreType.DMA((NC,)),
        ],
    )
    (registers,) = call(
        k(register_kernel),
        [(a, "vmem") for a in (kept, by_both, by_column, by_row, done)],
        [((1, 1, NC, 6, 2 * L), "out")],
    )
    return smoothed, registers


def solution(mesh):
    shape = (mesh.shape["gx"], mesh.shape["gy"])
    return jax.shard_map(
        functools.partial(body, shape),
        mesh=mesh,
        in_specs=(
            P("gx", "gy", None, None, None, None),
            P("gx", "gy", None, None),
            P("gx", "gy", None),
            P("gx", "gy", None, None),
        ),
        out_specs=(P("gx", "gy", None, None, None, None), P("gx", "gy", None, None, None)),
        check_vma=False,
    )
```

```python
import functools

import jax
import jax.numpy as jnp
from jax import lax
from jax.experimental import pallas as pl
from jax.experimental.pallas import tpu as pltpu
from jax.sharding import PartitionSpec as P

NC = 5
E = 16
BZ = 8
MOVE = 2
L = 128
F32 = jnp.float32
I32 = jnp.int32

PLANE = NC * BZ
FACE = 4 * PLANE
EDGES = (0, 1, E - 2, E - 1)
AHEAD = MOVE * NC * 4
PARCEL = 48
REST = MOVE * NC * 12
XFACE = FACE + BZ
YFACE = FACE + 2 * BZ
YNEAR = 2 * PLANE + 2 * BZ

VM = pltpu.VMEM
SM = pltpu.SMEM


def call(kernel, ins, outs, scratch=(), aliases=None, flops=1000, **kw):
    given, in_specs = [], []
    for array, space in ins:
        if space == "vmem":
            given.append(pltpu.with_memory_space_constraint(array, VM))
            in_specs.append(pl.BlockSpec(memory_space=VM))
        else:
            given.append(pltpu.with_memory_space_constraint(array, pltpu.HBM))
            in_specs.append(pl.BlockSpec(memory_space=pltpu.HBM))
    shapes, out_specs = [], []
    for shape, space in outs:
        if space == "vmem":
            shapes.append(VM(shape, F32))
            out_specs.append(pl.BlockSpec(memory_space=VM))
        else:
            shapes.append(jax.ShapeDtypeStruct(shape, F32))
            out_specs.append(pl.BlockSpec(memory_space=pltpu.HBM if space == "hbm" else VM))
    return pl.pallas_call(
        kernel,
        out_shape=shapes,
        in_specs=in_specs,
        out_specs=out_specs,
        scratch_shapes=list(scratch),
        input_output_aliases=aliases or {},
        cost_estimate=pl.CostEstimate(flops=flops, bytes_accessed=0, transcendentals=0),
        compiler_params=pltpu.CompilerParams(vmem_limit_bytes=24 * 1024 * 1024),
        **kw,
    )(*given)


def lanes():
    return lax.broadcasted_iota(I32, (BZ, L), 1)


def subs():
    return lax.broadcasted_iota(I32, (BZ, L), 0)


def rl(x, shift):
    shift %= L
    return x if shift == 0 else pltpu.roll(x, shift, 1)


def rs(x, shift):
    shift %= BZ
    return x if shift == 0 else pltpu.roll(x, shift, 0)


def pick_lanes(x, index):
    return jnp.take_along_axis(x, index, axis=1)


def place_of(mesh_shape):
    gx = lax.axis_index("gx")
    gy = lax.axis_index("gy")
    return gx, gy, gx * mesh_shape[1] + gy


def sources_of(place, owner):
    count = jnp.int32(0)
    sources = [jnp.int32(0)] * MOVE
    labels = [jnp.int32(0)] * MOVE
    for s in range(BZ):
        value = place[s]
        hit = value // BZ == owner
        for k in range(MOVE):
            taken = hit & (count == k)
            sources[k] = jnp.where(taken, s, sources[k])
            labels[k] = jnp.where(taken, value % BZ + 1, labels[k])
        count = count + hit.astype(I32)
    return sources, labels


def fill_rest(rest, boxes, sources):
    for k in range(MOVE):
        for c in range(NC):
            box = k * NC + c
            rest[12 * box : 12 * box + 12, :] = boxes[sources[k], c, 2 : E - 2]


def pack_kernel(
    shape, place_hbm, coeff_hbm, mask_hbm, fields_hbm, even, odd, even_rest, odd_rest, boxes, slots, rates, masks,
    place_s, coeff, mask, sem,
):
    pairs = ((fields_hbm.at[0, 0], boxes), (place_hbm, place_s), (coeff_hbm, coeff), (mask_hbm, mask))
    copies = [pltpu.make_async_copy(a, b, sem.at[i]) for i, (a, b) in enumerate(pairs)]
    for copy in copies:
        copy.start()
    _, _, me = place_of(shape)
    ahead = 1 - 2 * (me % 2)
    lane = lax.broadcasted_iota(I32, (1, L), 1)
    for copy in copies[1:]:
        copy.wait()
    place = [place_s[0, 0, s] for s in range(BZ)]
    chosen = [sources_of(place, me + ahead), sources_of(place, me - ahead)]
    for out, (sources, labels) in zip((even, odd), chosen):
        out[AHEAD:PARCEL, :] = jnp.zeros((PARCEL - AHEAD, 2 * L), F32)
        for k in range(MOVE):
            out[AHEAD + k : AHEAD + k + 1, L:] = jnp.full((1, L), labels[k].astype(F32), F32)
            line = jnp.zeros((1, L), F32)
            for c in range(NC):
                line = jnp.where(lane == c, coeff[0, c, 0, sources[k]], line)
            out[AHEAD + k : AHEAD + k + 1, :L] = line
    for s in range(BZ):
        label = jnp.where(place[s] // BZ == me, place[s] % BZ + 1, 0)
        slots[s : s + 1, :] = jnp.full((1, L), label.astype(F32), F32)
        for c in range(NC):
            rates[s * NC + c : s * NC + c + 1, :] = jnp.full((1, L), coeff[0, c, 0, s], F32)
        for d in range(3):
            masks[d * BZ + s : d * BZ + s + 1, :] = jnp.full((1, L), mask[0, d, 0, s].astype(F32), F32)
    copies[0].wait()
    for out, rest, (sources, _) in zip((even, odd), (even_rest, odd_rest), chosen):
        for k in range(MOVE):
            for c in range(NC):
                box = k * NC + c
                out[4 * box : 4 * box + 2, :] = boxes[sources[k], c, :2]
                out[4 * box + 2 : 4 * box + 4, :] = boxes[sources[k], c, E - 2 :]
                rest[12 * box : 12 * box + 12, :] = boxes[sources[k], c, 2 : E - 2]


def stays(slots):
    label = (subs() + 1).astype(F32)
    return [slots[s : s + 1, :] == label for s in range(BZ)]


def stayed_tile(found, boxes, c, x, h):
    tile = jnp.zeros((BZ, L), F32)
    for s in range(BZ):
        tile = jnp.where(found[s], boxes[s, c, x : x + 1, h * L : h * L + L], tile)
    return tile


def stay_kernel(shape, boxes, slots, moved):
    found = stays(slots)
    for c in range(NC):
        for x in range(E):
            row = (c * E + x) * BZ
            for h in range(2):
                moved[h, row : row + BZ, :] = stayed_tile(found, boxes, c, x, h)


def arrivals(even, odd):
    sub = subs()
    found = []
    for parcel in (even, odd):
        for k in range(MOVE):
            label = parcel[AHEAD + k : AHEAD + k + 1, L:]
            found.append((parcel, k, label == (sub + 1).astype(F32)))
    return found


def merged(found, tile, c, x, h, rests=None):
    for i, (parcel, k, hit) in enumerate(found):
        if x in EDGES:
            source, at = parcel, (k * NC + c) * 4 + EDGES.index(x)
        else:
            source, at = rests[i // MOVE], (k * NC + c) * 12 + x - 2
        tile = jnp.where(hit, source[at : at + 1, h * L : h * L + L], tile)
    return tile


def spread(tile, lane):
    return pick_lanes(tile, jnp.full((BZ, L), lane, I32))


def plane_row(layer, h, c):
    return ((layer * 2 + h) * NC + c) * BZ


def xsend_kernel(shape, even, odd, boxes, slots, old_rates, core, link, rates):
    gx, _, _ = place_of(shape)
    first = gx % 2 == 0
    kept, found = stays(slots), arrivals(even, odd)
    lane = lanes()
    together = jnp.zeros((BZ, L), F32)
    for c in range(NC):
        tile = jnp.zeros((BZ, L), F32)
        for s in range(BZ):
            tile = jnp.where(kept[s], old_rates[s * NC + c : s * NC + c + 1, :], tile)
        for parcel, k, hit in found:
            line = jnp.broadcast_to(parcel[AHEAD + k : AHEAD + k + 1, :L], (BZ, L))
            tile = jnp.where(hit, spread(line, c), tile)
        rates[c * BZ : c * BZ + BZ, :] = tile
        together = jnp.where(lane == c, tile, together)
        for layer in range(2):
            for h in range(2):
                sides = [merged(found, stayed_tile(kept, boxes, c, x, h), c, x, h) for x in (layer, E - 1 - layer)]
                at = plane_row(layer, h, c)
                core[at : at + BZ, :] = jnp.where(first, sides[1], sides[0])
                link[at : at + BZ, :] = jnp.where(first, sides[0], sides[1])
    core[FACE:, :] = together
    link[FACE:, :] = together


def merge_kernel(shape, even, odd, even_rest, odd_rest, moved, out, near, far):
    _, gy, _ = place_of(shape)
    first = gy % 2 == 0
    found = arrivals(even, odd)
    lane = lanes()
    for c in range(NC):
        low = [[None, None], [None, None]]
        high = [[None, None], [None, None]]
        for x in range(E):
            row = (c * E + x) * BZ
            at = L // 8 * (x % 8)
            here = lane // E == x % 8
            half = x // 8
            for h in range(2):
                tile = merged(found, moved[h, row : row + BZ, :], c, x, h, (even_rest, odd_rest))
                out[h, row : row + BZ, :] = tile
                for layer in range(2):
                    keep, start = ((low, E * layer) if h == 0 else (high, L - E - E * layer))
                    strip = rl(tile, at - start)
                    old = keep[layer][half]
                    keep[layer][half] = strip if old is None else jnp.where(here, strip, old)
        for layer in range(2):
            for h in range(2):
                at = plane_row(layer, h, c)
                near[at : at + BZ, :] = jnp.where(first, high[layer][h], low[layer][h])
                far[at : at + BZ, :] = jnp.where(first, low[layer][h], high[layer][h])


def ends(shape):
    gx, gy, _ = place_of(shape)
    x_first, y_first = gx % 2 == 0, gy % 2 == 0
    link_ok = jnp.where(x_first, gx > 0, gx < shape[0] - 1)
    far_ok = jnp.where(y_first, gy > 0, gy < shape[1] - 1)
    return x_first, y_first, link_ok, far_ok


def ysend_kernel(shape, link, core, rates, near, far, near_out, next_out, far_out):
    x_first, y_first, link_ok, _ = ends(shape)
    lane = lanes()
    near_out[: 2 * PLANE, :] = near[: 2 * PLANE, :]
    next_out[...] = near[2 * PLANE :, :]
    far_out[:FACE, :] = far[...]
    bottoms = [jnp.zeros((BZ, L), F32)] * 2
    tops = [jnp.zeros((BZ, L), F32)] * 2
    for c in range(NC):
        lines = []
        for h in range(2):
            at = plane_row(0, h, c)
            a = core[at : at + BZ, :]
            b = jnp.where(link_ok, link[at : at + BZ, :], 0.0)
            lines.append((jnp.where(x_first, b, a), jnp.where(x_first, a, b)))
        i, at = divmod(c, 4)
        at *= 2 * E
        low = (lane >= at) & (lane < at + E)
        high = (lane >= at + E) & (lane < at + 2 * E)
        bottoms[i] = jnp.where(low, rl(lines[0][0], at), jnp.where(high, rl(lines[0][1], at + E), bottoms[i]))
        tops[i] = jnp.where(low, rl(lines[1][0], at + E), jnp.where(high, rl(lines[1][1], at + 2 * E), tops[i]))
        rate = rates[c * BZ : c * BZ + BZ, :]
        bottoms[1] = jnp.where(lane == L // 2 + c, rate, bottoms[1])
        tops[1] = jnp.where(lane == L // 2 + c, rate, tops[1])
    for i in range(2):
        at = FACE + i * BZ
        near_out[at - 2 * PLANE : at - 2 * PLANE + BZ, :] = jnp.where(y_first, tops[i], bottoms[i])
        far_out[at : at + BZ, :] = jnp.where(y_first, bottoms[i], tops[i])


def extra_at(ref, c, start=FACE):
    i, at = divmod(c, 4)
    return rl(ref[start + i * BZ : start + i * BZ + BZ, :], -2 * E * at)


def y_rate(ref, c):
    return spread(ref[ref.shape[0] - BZ :, :], L // 2 + c)


def z_parts(x, lane, sub, swap):
    z = lane % E
    down = jnp.where(sub == 0, 0.0, rs(x, 1))
    up = jnp.where(sub == BZ - 1, 0.0, rs(x, -1))
    ends_ = pick_lanes(jnp.where(z == E - 1, down, up), swap)
    return jnp.where(z == 0, ends_, rl(x, 1)) + jnp.where(z == E - 1, ends_, rl(x, -1))


def swap_index(lane):
    z = lane % E
    return jnp.where(z == 0, lane + E - 1, jnp.where(z == E - 1, lane - E + 1, lane))


def inner(pair, lane, sub, swap):
    a, b = pair
    a1, b1, a2, b2 = rl(a, E), rl(b, E), rl(a, -E), rl(b, -E)
    low, high = lane < E, lane >= L - E
    first = jnp.where(low, 0.0, a1) + jnp.where(high, b2, a2) + z_parts(a, lane, sub, swap)
    second = jnp.where(low, a1, b1) + jnp.where(high, 0.0, b2) + z_parts(b, lane, sub, swap)
    return first, second


def pair_at(ref, layer, c):
    return tuple(ref[plane_row(layer, h, c) : plane_row(layer, h, c) + BZ, :] for h in range(2))


def tile_at(ref, c, x):
    row = (c * E + x) * BZ
    return tuple(ref[h, row : row + BZ, :] for h in range(2))


def z_differences(tiles, sub, upper):
    down = [jnp.where(sub == 0, 0.0, t) for t in [rs(t, 1) for t in tiles]]
    up = [jnp.where(sub == BZ - 1, 0.0, t) for t in [rs(t, -1) for t in tiles]]
    high = [rl(t, 1 - E) for t in [jnp.where(upper, t, d) for t, d in zip(tiles, down)]]
    return [jnp.where(upper, u - g, g - t) for g, u, t in zip(high, up, tiles)]


def sweep_kernel(shape, moved, rates, link, core, core_sent, link_sent, out, core_first, link_first, tops):
    x_first, _, link_ok, _ = ends(shape)
    _, gy, _ = place_of(shape)
    lane, sub = lanes(), subs()
    swap = swap_index(lane)
    upper = sub % 2 == 1
    z = lane % E
    for c in range(NC):
        rate = rates[c * BZ : c * BZ + BZ, :]
        scale = 1.0 / (1.0 + 6.0 * rate)
        ghost = []
        for got, sent, kept, ok in ((core, core_sent, core_first, None), (link, link_sent, link_first, link_ok)):
            g0, g1, own = pair_at(got, 0, c), pair_at(got, 1, c), pair_at(sent, 0, c)
            g_rate = spread(got[FACE:, :], c)
            if ok is not None:
                g0, g1 = (tuple(jnp.where(ok, t, 0.0) for t in g) for g in (g0, g1))
                g_rate = jnp.where(ok, g_rate, 0.0)
            kept[2 * PLANE + c * BZ : 2 * PLANE + c * BZ + BZ, :] = g_rate
            ghost.append(g0)
            g_scale = 1.0 / (1.0 + 6.0 * g_rate)
            sums = inner(g0, lane, sub, swap)
            for h in range(2):
                value = (g0[h] + g_rate * (sums[h] + g1[h] + own[h])) * g_scale
                if ok is not None:
                    value = jnp.where(ok, value, 0.0)
                row = (h * NC + c) * BZ
                kept[row : row + BZ, :] = value
        low = [jnp.where(x_first, b, a) for a, b in zip(*ghost)]
        high = [jnp.where(x_first, a, b) for a, b in zip(*ghost)]
        for x in range(E):
            here = tile_at(moved, c, x)
            before = low if x == 0 else tile_at(moved, c, x - 1)
            after = high if x == E - 1 else tile_at(moved, c, x + 1)
            sums = inner(here, lane, sub, swap)
            row = (c * E + x) * BZ
            for h in range(2):
                out[h, row : row + BZ, :] = (here[h] + rate * (sums[h] + before[h] + after[h])) * scale
    every = [(h, c, k) for c in range(NC) for h in range(2) for k in range(E // 2)]
    d = []
    for h, c, k in every:
        row = (c * E + 2 * k) * BZ
        d.append(out[h, row : row + BZ, :] + out[h, row + BZ : row + 2 * BZ, :])
    d = z_differences(d, sub, upper)
    d = [t + r for t, r in zip(d, [rl(t, -E) for t in d])]
    d = [rl(t, k) for t, (_, _, k) in zip(d, every)]
    faces = {}
    for t, (h, c, k) in zip(d, every):
        faces[h, c] = t if k == 0 else jnp.where(z == k, t, faces[h, c])
    y8 = lane % 8
    source = (y8 % 4) * (2 * E) + lane // E
    picked = {key: pick_lanes(t, source) for key, t in faces.items()}
    for c in range(NC):
        top = jnp.where(y8 < 4, picked[0, c], picked[1, c])
        tops[c * BZ : c * BZ + BZ, :] = jnp.where(z // 8 == gy % 2, top, 0.0)


def coarse_plane(pair, parity, lane, sub):
    sums = []
    for t in pair:
        t = t + rl(t, -1)
        sums.append(t + rl(t, -E))
    source = (lane // E % 4) * (2 * E) + 2 * (lane % 8)
    out = jnp.where(lane < L // 2, pick_lanes(sums[0], source), pick_lanes(sums[1], source))
    return jnp.where(lane % E // 8 == sub % 2, 0.25 * out, 0.0)


def strips(low, high, x, low_lane, high_lane):
    shift = E * (x % 8)
    return (
        jnp.where(low_lane, rl(low[x // 8], -shift), 0.0),
        jnp.where(high_lane, rl(high[x // 8], L - E - shift), 0.0),
    )


def corner(extra, low_lane, high_lane):
    return jnp.where(low_lane, extra, 0.0), jnp.where(high_lane, rl(extra, L - 2 * E), 0.0)


def y_ghosts(got, ok, c):
    g0, g1, extra = pair_at(got, 0, c), pair_at(got, 1, c), extra_at(got, c)
    if ok is not None:
        g0, g1 = (tuple(jnp.where(ok, t, 0.0) for t in g) for g in (g0, g1))
        extra = jnp.where(ok, extra, 0.0)
    return g0, g1, extra


def near_ghosts(got, following, c):
    second = None if following is None else pair_at(following, 0, c)
    return pair_at(got, 0, c), second, extra_at(got, c, 2 * PLANE)


def y_first_sweep(got, sent, ok, ghost, c, lane, sub, swap):
    g0, g1, extra = ghost
    own = pair_at(sent, 0, c)
    g_rate = y_rate(got, c)
    if ok is not None:
        g_rate = jnp.where(ok, g_rate, 0.0)
    g_scale = 1.0 / (1.0 + 6.0 * g_rate)
    sums, line = inner(g0, lane, sub, swap), corner(extra, lane < E, lane >= L - E)
    values = [(g0[h] + g_rate * (sums[h] + line[h] + g1[h] + own[h])) * g_scale for h in range(2)]
    return values if ok is None else [jnp.where(ok, t, 0.0) for t in values]


def x_first_sweep(part, ok, at_low, low_line, high_line, c, low_lane, high_lane):
    g_rate = part[2 * PLANE + c * BZ : 2 * PLANE + c * BZ + BZ, :]
    g_weight = g_rate / (1.0 + 6.0 * g_rate)
    bottom = jnp.where(at_low, low_line, rl(low_line, -E))
    top = jnp.where(at_low, rl(high_line, L - E), rl(high_line, L - 2 * E))
    values = []
    for h, (line, there) in enumerate(((bottom, low_lane), (top, high_lane))):
        row = (h * NC + c) * BZ
        values.append(part[row : row + BZ, :] + g_weight * jnp.where(there, line, 0.0))
    return values if ok is None else [jnp.where(ok, t, 0.0) for t in values]


def flux_kernel(
    shape, partial, moved_rates, masks, tops, link_first, far, near, far_sent, own_far, y_far, kept, to_row, to_column, to_both
):
    x_first, y_first, link_ok, far_ok = ends(shape)
    gx, gy, _ = place_of(shape)
    par_x, par_y = gx % 2, gy % 2
    lane, sub = lanes(), subs()
    swap = swap_index(lane)
    upper = sub % 2 == 1
    z = lane % E
    low_lane, high_lane = lane < E, lane >= L - E
    each = range(NC)
    rate = [moved_rates[c * BZ : c * BZ + BZ, :] for c in each]
    scale = [1.0 / (1.0 + 6.0 * r) for r in rate]
    weight = [r * q for r, q in zip(rate, scale)]
    near_g = [near_ghosts(near, None, c) for c in each]
    far_g = [y_ghosts(far, far_ok, c) for c in each]
    far_f = []
    for c in each:
        values = y_first_sweep(far, far_sent, far_ok, far_g[c], c, lane, sub, swap)
        for h in range(2):
            row = (h * NC + c) * BZ
            y_far[row : row + BZ, :] = values[h]
        far_f.append(values)
    far_r = [g[0] for g in far_g]

    def by_side(which, c):
        a, b = near_g[c][which], far_g[c][which]
        if which == 2:
            return jnp.where(y_first, b, a), jnp.where(y_first, a, b)
        return [jnp.where(y_first, q, p) for p, q in zip(a, b)], [jnp.where(y_first, p, q) for p, q in zip(a, b)]

    faces_y = []
    for c in each:
        own = pair_at(own_far, 0, c)
        flux = [far_f[c][h] - own[h] - weight[c] * far_r[c][h] for h in range(2)]
        face = coarse_plane(flux, par_x, lane, sub) * (rate[c] * masks[BZ : 2 * BZ, :])
        faces_y.append(face + rs(face, 1))
    faces_x = []
    for c in each:
        ghost = x_first_sweep(link_first, link_ok, x_first, *by_side(2, c), c, low_lane, high_lane)
        low_r, high_r = by_side(0, c)
        at_0, at_15 = (strips(low_r, high_r, x, low_lane, high_lane) for x in (0, E - 1))
        cells_0, cells_15 = tile_at(partial, c, 0), tile_at(partial, c, E - 1)
        flux = []
        for h in range(2):
            cell = jnp.where(x_first, cells_0[h], cells_15[h])
            cell = cell + weight[c] * jnp.where(x_first, at_0[h], at_15[h])
            flux.append(ghost[h] - cell)
        face = coarse_plane(flux, par_y, lane, sub) * (rate[c] * masks[0:BZ, :])
        faces_x.append(face + rs(face, -1))
    faces_z = []
    source = (lane // E % 4) * (2 * E) + jnp.where(lane % 8 == 7, 7, 0)
    d = []
    for c in each:
        for side in by_side(0, c):
            d += [weight[c] * t for t in side]
    d = [t + r for t, r in zip(d, [rl(t, -E) for t in d])]
    d = z_differences(d, sub, upper)
    halves = []
    for c in each:
        for h in range(2):
            halves.append(jnp.where(z == 7, rl(d[4 * c + 2 + h], 7), d[4 * c + h]))
    halves = [pick_lanes(t, source) for t in halves]
    for c in each:
        add = jnp.where(lane < L // 2, halves[2 * c], halves[2 * c + 1])
        add = jnp.where((z == 8 * par_y) | (z == 8 * par_y + 7), add, 0.0)
        faces_z.append((tops[c * BZ : c * BZ + BZ, :] + add) * (0.25 * rate[c] * masks[2 * BZ :, :]))
    left = sub % 4 < 2
    top = sub < 4
    own_tiles, other_tiles = [], []
    for c in each:
        outer = jnp.where(upper, faces_y[c], faces_x[c])
        columns = (jnp.where(left, outer, rs(faces_z[c], 2)), jnp.where(left, rs(outer, -2), faces_z[c]))
        own_tiles.append(jnp.where(y_first, columns[0], columns[1]))
        other_tiles.append(jnp.where(y_first, columns[1], columns[0]))
    for tiles, same, other in ((own_tiles, kept, to_row), (other_tiles, to_column, to_both)):
        turned = [rs(t, 4) for t in tiles]
        for i in range(0, NC, 2):
            j = min(i + 1, NC - 1)
            low, high = jnp.where(top, tiles[i], turned[j]), jnp.where(top, turned[i], tiles[j])
            row = i // 2 * BZ
            same[row : row + BZ, :] = jnp.where(x_first, low, high)
            other[row : row + BZ, :] = jnp.where(x_first, high, low)


def register_kernel(shape, kept, by_both, by_column, by_row, _, out):
    x_first, y_first, _, _ = ends(shape)
    sub = subs()
    for c in range(NC):
        at = c // 2 * BZ
        m, m4, g, g4 = (rs(ref[at : at + BZ, :], 4 * (c % 2)) for ref in (kept, by_column, by_row, by_both))
        for h in range(2):
            same_y, same_x = (y_first, x_first) if h == 0 else (~y_first, ~x_first)
            a, b = jnp.where(same_y, m, m4), jnp.where(same_y, g, g4)
            x0, x1 = jnp.where(x_first, a, b), jnp.where(x_first, b, a)
            t, t4 = jnp.where(same_x, m, g), jnp.where(same_x, m4, g4)
            y0, y1 = jnp.where(y_first, rs(t, 1), rs(t4, 1)), jnp.where(y_first, rs(t4, 2), rs(t, 2))
            rows = jnp.where(sub == 0, x0, jnp.where(sub == 1, rs(x1, 1), rs(t + t4, 2)))
            rows = jnp.where(sub == 2, y0, jnp.where(sub == 3, y1, rows))
            out[0, 0, c, :, h * L : h * L + L] = rows[:6]


def second_kernel(shape, moved, rates, partial, core_first, link_first, far_sent, out, own_far):
    x_first, _, _, _ = ends(shape)
    lane, sub = lanes(), subs()
    swap = swap_index(lane)
    for c in range(NC):
        rate = rates[c * BZ : c * BZ + BZ, :]
        scale = 1.0 / (1.0 + 6.0 * rate)
        own, own1 = pair_at(far_sent, 0, c), pair_at(far_sent, 1, c)
        sums, line = inner(own, lane, sub, swap), corner(extra_at(far_sent, c), lane < E, lane >= L - E)
        for h in range(2):
            row = (h * NC + c) * BZ
            own_far[row : row + BZ, :] = (own[h] + rate * (sums[h] + line[h] + own1[h])) * scale
        core, link = pair_at(core_first, 0, c), pair_at(link_first, 0, c)
        low = [jnp.where(x_first, b, a) for a, b in zip(core, link)]
        high = [jnp.where(x_first, a, b) for a, b in zip(core, link)]
        for x in range(E):
            here = tile_at(partial, c, x)
            before = low if x == 0 else tile_at(partial, c, x - 1)
            after = high if x == E - 1 else tile_at(partial, c, x + 1)
            sums = inner(here, lane, sub, swap)
            start = tile_at(moved, c, x)
            row = (c * E + x) * BZ
            for h in range(2):
                out[h, row : row + BZ, :] = start[h] + rate * (sums[h] + before[h] + after[h])


def smooth_kernel(
    shape, rates, partial, core_first, link_first, far, near, following, near_sent, y_far, out, done, planes, held, boxes, sem
):
    done[...] = jnp.zeros((BZ, L), F32)
    x_first, y_first, _, far_ok = ends(shape)
    lane, sub = lanes(), subs()
    swap = swap_index(lane)
    low_lane, high_lane = lane < E, lane >= L - E

    def by_side(a, b, a_first):
        low = [jnp.where(a_first, q, p) for p, q in zip(a, b)]
        high = [jnp.where(a_first, p, q) for p, q in zip(a, b)]
        return low, high

    for c in range(NC):
        rate = rates[c * BZ : c * BZ + BZ, :]
        weight = rate / (1.0 + 6.0 * rate)
        near_g, far_g = near_ghosts(near, following, c), y_ghosts(far, far_ok, c)
        near_f = y_first_sweep(near, near_sent, None, near_g, c, lane, sub, swap)
        ghosts_f = by_side(near_f, pair_at(y_far, 0, c), y_first)
        ghosts_r = by_side(near_g[0], far_g[0], y_first)
        lines = by_side(near_g[2:], far_g[2:], y_first)
        x_rates = [ref[2 * PLANE + c * BZ : 2 * PLANE + c * BZ + BZ, :] for ref in (core_first, link_first)]
        x_weights = [t / (1.0 + 6.0 * t) for t in x_rates]
        (low_w,), (high_w,) = by_side(x_weights[:1], x_weights[1:], x_first)
        for side in range(2):
            added = [weight * t for t in ghosts_r[side]]
            (line,) = lines[side]
            sums = inner(added, lane, sub, swap)
            ends_ = (jnp.where(low_lane, low_w * line, 0.0), jnp.where(high_lane, high_w * rl(line, L - 2 * E), 0.0))
            for h in range(2):
                row = ((side * 2 + h) * NC + c) * BZ
                planes[0, row : row + BZ, :] = rate * (sums[h] + ends_[h] + ghosts_f[side][h])
                planes[1, row : row + BZ, :] = rate * added[h]
    next_low = (lane >= E) & (lane < 2 * E)
    next_high = (lane >= L - 2 * E) & (lane < L - E)
    copies = []
    for c in range(NC):
        rate = rates[c * BZ : c * BZ + BZ, :]
        scale = 1.0 / (1.0 + 6.0 * rate)
        for x in range(E):
            row = (c * E + x) * BZ
            shift = E * (x % 8)
            for h, (here, there, at) in enumerate(((low_lane, next_low, 0), (high_lane, next_high, L - E))):
                plane = ((h * 2 + x // 8) * NC + c) * BZ
                first = rl(planes[0, plane : plane + BZ, :], at - shift)
                second = rl(planes[1, plane : plane + BZ, :], (at - E if h else E) - shift)
                add = jnp.where(here, first, jnp.where(there, second, 0.0))
                held[h, row : row + BZ, :] = (partial[h, row : row + BZ, :] + add) * scale
        for s in range(BZ):
            for h in range(2):
                boxes[c, s, :, h * L : h * L + L] = held[h, pl.ds(c * E * BZ + s, E, stride=BZ), :]
        copies.append(pltpu.make_async_copy(boxes.at[c], out.at[0, 0, :, c], sem.at[c]))
        copies[-1].start()
    for copy in copies:
        copy.wait()


def body(shape, fields_old, coeff_old, new_place, cf_mask):
    rows, columns = shape
    count = rows * columns
    both = ("gx", "gy")

    def swap(array, pairs):
        return lax.ppermute(array, both, pairs)

    even_pairs = [(i, i ^ 1) for i in range(count)]
    odd_pairs = [(i, (i + 1) % count if i % 2 else (i - 1) % count) for i in range(count)]
    at = lambda a, b: a * columns + b
    core_pairs = [(at(a, b), at(a ^ 1, b)) for a in range(rows) for b in range(columns)]
    both_pairs = [(at(a, b), at(a ^ 1, b ^ 1)) for a in range(rows) for b in range(columns)]
    link_pairs = [
        (at(a, b), at(a, b ^ 2) if a in (0, rows - 1) else at(a + 1 if a % 2 else a - 1, b))
        for a in range(rows)
        for b in range(columns)
    ]
    far_pairs = [
        (at(a, b), at(a ^ 1, b) if b in (0, columns - 1) else at(a, b + 1 if b % 2 else b - 1))
        for a in range(rows)
        for b in range(columns)
    ]
    k = lambda f: functools.partial(f, shape)
    coeff_old = coeff_old.transpose(0, 3, 1, 2)
    cf_mask = cf_mask.transpose(0, 2, 1, 3)
    big = (2, NC * E * BZ, L)

    plane = ((2 * PLANE, L), "vmem")
    even, odd, even_rest, odd_rest, boxes, slots, rates, masks = call(
        k(pack_kernel),
        [(a, "hbm") for a in (new_place, coeff_old, cf_mask, fields_old)],
        [
            ((PARCEL, 2 * L), "vmem"),
            ((PARCEL, 2 * L), "vmem"),
            ((REST, 2 * L), "vmem"),
            ((REST, 2 * L), "vmem"),
            ((BZ, NC, E, 2 * L), "vmem"),
            ((BZ, L), "vmem"),
            ((PLANE, L), "vmem"),
            ((3 * BZ, L), "vmem"),
        ],
        [
            SM((1, 1, BZ), I32),
            SM((1, NC, 1, BZ), F32),
            SM((1, 3, 1, BZ), I32),
            pltpu.SemaphoreType.DMA((4,)),
        ],
    )
    even_got = swap(even, even_pairs)
    odd_got = swap(odd, odd_pairs)
    even_rest_got = swap(even_rest, even_pairs)
    odd_rest_got = swap(odd_rest, odd_pairs)
    core, link, rates = call(
        k(xsend_kernel),
        [(a, "vmem") for a in (even_got, odd_got, boxes, slots, rates)],
        [((XFACE, L), "vmem"), ((XFACE, L), "vmem"), ((PLANE, L), "vmem")],
    )
    (stayed,) = call(k(stay_kernel), [(boxes, "vmem"), (slots, "vmem")], [(big, "vmem")])
    core_got = swap(core, core_pairs)
    link_got = swap(link, link_pairs)
    moved, near, far = call(
        k(merge_kernel),
        [(a, "vmem") for a in (even_got, odd_got, even_rest_got, odd_rest_got, stayed)],
        [(big, "vmem"), ((FACE, L), "vmem"), ((FACE, L), "vmem")],
    )
    near, following, far = call(
        k(ysend_kernel),
        [(a, "vmem") for a in (link_got, core_got, rates, near, far)],
        [((YNEAR, L), "vmem"), ((2 * PLANE, L), "vmem"), ((YFACE, L), "vmem")],
    )
    near_got = swap(near, even_pairs)
    far_got = swap(far, far_pairs)
    next_got = swap(following, even_pairs)
    part, core_first, link_first, tops = call(
        k(sweep_kernel),
        [(a, "vmem") for a in (moved, rates, link_got, core_got, core, link)],
        [(big, "vmem"), ((3 * PLANE, L), "vmem"), ((3 * PLANE, L), "vmem"), ((PLANE, L), "vmem")],
    )
    second, own_far = call(
        k(second_kernel),
        [(a, "vmem") for a in (moved, rates, part, core_first, link_first, far)],
        [(big, "vmem"), plane],
    )
    y_far, kept, to_row, to_column, to_both = call(
        k(flux_kernel),
        [(a, "vmem") for a in (part, rates, masks, tops, link_first, far_got, near_got, far, own_far)],
        [plane] + [(((NC + 1) // 2 * BZ, L), "vmem")] * 4,
    )
    by_both = swap(to_both, both_pairs)
    by_column = swap(to_column, even_pairs)
    by_row = swap(to_row, core_pairs)
    smoothed, done = call(
        k(smooth_kernel),
        [(a, "vmem") for a in (rates, second, core_first, link_first, far_got, near_got, next_got, near, y_far)],
        [((1, 1, BZ, NC, E, 2 * L), "hbm"), ((BZ, L), "vmem")],
        [
            VM((2, 4 * PLANE, L), F32),
            VM(big, F32),
            VM((NC, BZ, E, 2 * L), F32),
            pltpu.SemaphoreType.DMA((NC,)),
        ],
    )
    (registers,) = call(
        k(register_kernel),
        [(a, "vmem") for a in (kept, by_both, by_column, by_row, done)],
        [((1, 1, NC, 6, 2 * L), "out")],
    )
    return smoothed, registers


def solution(mesh):
    shape = (mesh.shape["gx"], mesh.shape["gy"])
    return jax.shard_map(
        functools.partial(body, shape),
        mesh=mesh,
        in_specs=(
            P("gx", "gy", None, None, None, None),
            P("gx", "gy", None, None),
            P("gx", "gy", None),
            P("gx", "gy", None, None),
        ),
        out_specs=(P("gx", "gy", None, None, None, None), P("gx", "gy", None, None, None)),
        check_vma=False,
    )
```

```python
import functools

import jax
import jax.numpy as jnp
from jax import lax
from jax.experimental import pallas as pl
from jax.experimental.pallas import tpu as pltpu
from jax.sharding import PartitionSpec as P

NC = 5
E = 16
BZ = 8
MOVE = 2
L = 128
F32 = jnp.float32
I32 = jnp.int32

PLANE = NC * BZ
FACE = 4 * PLANE
EDGES = (0, 1, E - 2, E - 1)
AHEAD = MOVE * NC * 4
PARCEL = 48
REST = MOVE * NC * 12
XFACE = FACE + BZ
YFACE = FACE + 2 * BZ
YNEAR = 2 * PLANE + 2 * BZ

VM = pltpu.VMEM
SM = pltpu.SMEM


def call(kernel, ins, outs, scratch=(), aliases=None, flops=1000, **kw):
    given, in_specs = [], []
    for array, space in ins:
        if space == "vmem":
            given.append(pltpu.with_memory_space_constraint(array, VM))
            in_specs.append(pl.BlockSpec(memory_space=VM))
        else:
            given.append(pltpu.with_memory_space_constraint(array, pltpu.HBM))
            in_specs.append(pl.BlockSpec(memory_space=pltpu.HBM))
    shapes, out_specs = [], []
    for shape, space in outs:
        if space == "vmem":
            shapes.append(VM(shape, F32))
            out_specs.append(pl.BlockSpec(memory_space=VM))
        else:
            shapes.append(jax.ShapeDtypeStruct(shape, F32))
            out_specs.append(pl.BlockSpec(memory_space=pltpu.HBM if space == "hbm" else VM))
    return pl.pallas_call(
        kernel,
        out_shape=shapes,
        in_specs=in_specs,
        out_specs=out_specs,
        scratch_shapes=list(scratch),
        input_output_aliases=aliases or {},
        cost_estimate=pl.CostEstimate(flops=flops, bytes_accessed=0, transcendentals=0),
        compiler_params=pltpu.CompilerParams(vmem_limit_bytes=24 * 1024 * 1024),
        **kw,
    )(*given)


def lanes():
    return lax.broadcasted_iota(I32, (BZ, L), 1)


def subs():
    return lax.broadcasted_iota(I32, (BZ, L), 0)


def rl(x, shift):
    shift %= L
    return x if shift == 0 else pltpu.roll(x, shift, 1)


def rs(x, shift):
    shift %= BZ
    return x if shift == 0 else pltpu.roll(x, shift, 0)


def pick_lanes(x, index):
    return jnp.take_along_axis(x, index, axis=1)


def place_of(mesh_shape):
    gx = lax.axis_index("gx")
    gy = lax.axis_index("gy")
    return gx, gy, gx * mesh_shape[1] + gy


def sources_of(place, owner):
    count = jnp.int32(0)
    sources = [jnp.int32(0)] * MOVE
    labels = [jnp.int32(0)] * MOVE
    for s in range(BZ):
        value = place[s]
        hit = value // BZ == owner
        for k in range(MOVE):
            taken = hit & (count == k)
            sources[k] = jnp.where(taken, s, sources[k])
            labels[k] = jnp.where(taken, value % BZ + 1, labels[k])
        count = count + hit.astype(I32)
    return sources, labels


def fill_rest(rest, boxes, sources):
    for k in range(MOVE):
        for c in range(NC):
            box = k * NC + c
            rest[12 * box : 12 * box + 12, :] = boxes[sources[k], c, 2 : E - 2]


def pack_kernel(
    shape, place_hbm, coeff_hbm, mask_hbm, fields_hbm, even, odd, even_rest, odd_rest, boxes, slots, rates, masks,
    place_s, coeff, mask, sem,
):
    pairs = ((fields_hbm.at[0, 0], boxes), (place_hbm, place_s), (coeff_hbm, coeff), (mask_hbm, mask))
    copies = [pltpu.make_async_copy(a, b, sem.at[i]) for i, (a, b) in enumerate(pairs)]
    for copy in copies:
        copy.start()
    _, _, me = place_of(shape)
    ahead = 1 - 2 * (me % 2)
    lane = lax.broadcasted_iota(I32, (1, L), 1)
    for copy in copies[1:]:
        copy.wait()
    place = [place_s[0, 0, s] for s in range(BZ)]
    chosen = [sources_of(place, me + ahead), sources_of(place, me - ahead)]
    for out, (sources, labels) in zip((even, odd), chosen):
        out[AHEAD:PARCEL, :] = jnp.zeros((PARCEL - AHEAD, 2 * L), F32)
        for k in range(MOVE):
            out[AHEAD + k : AHEAD + k + 1, L:] = jnp.full((1, L), labels[k].astype(F32), F32)
            line = jnp.zeros((1, L), F32)
            for c in range(NC):
                line = jnp.where(lane == c, coeff[0, c, 0, sources[k]], line)
            out[AHEAD + k : AHEAD + k + 1, :L] = line
    for s in range(BZ):
        label = jnp.where(place[s] // BZ == me, place[s] % BZ + 1, 0)
        slots[s : s + 1, :] = jnp.full((1, L), label.astype(F32), F32)
        for c in range(NC):
            rates[s * NC + c : s * NC + c + 1, :] = jnp.full((1, L), coeff[0, c, 0, s], F32)
        for d in range(3):
            masks[d * BZ + s : d * BZ + s + 1, :] = jnp.full((1, L), mask[0, d, 0, s].astype(F32), F32)
    copies[0].wait()
    for out, rest, (sources, _) in zip((even, odd), (even_rest, odd_rest), chosen):
        for k in range(MOVE):
            for c in range(NC):
                box = k * NC + c
                out[4 * box : 4 * box + 2, :] = boxes[sources[k], c, :2]
                out[4 * box + 2 : 4 * box + 4, :] = boxes[sources[k], c, E - 2 :]
                rest[12 * box : 12 * box + 12, :] = boxes[sources[k], c, 2 : E - 2]


def stays(slots):
    label = (subs() + 1).astype(F32)
    return [slots[s : s + 1, :] == label for s in range(BZ)]


def stayed_tile(found, boxes, c, x, h):
    tile = jnp.zeros((BZ, L), F32)
    for s in range(BZ):
        tile = jnp.where(found[s], boxes[s, c, x : x + 1, h * L : h * L + L], tile)
    return tile


def stay_kernel(shape, boxes, slots, moved):
    found = stays(slots)
    for c in range(NC):
        for x in range(E):
            row = (c * E + x) * BZ
            for h in range(2):
                moved[h, row : row + BZ, :] = stayed_tile(found, boxes, c, x, h)


def arrivals(even, odd):
    sub = subs()
    found = []
    for parcel in (even, odd):
        for k in range(MOVE):
            label = parcel[AHEAD + k : AHEAD + k + 1, L:]
            found.append((parcel, k, label == (sub + 1).astype(F32)))
    return found


def merged(found, tile, c, x, h, rests=None):
    for i, (parcel, k, hit) in enumerate(found):
        if x in EDGES:
            source, at = parcel, (k * NC + c) * 4 + EDGES.index(x)
        else:
            source, at = rests[i // MOVE], (k * NC + c) * 12 + x - 2
        tile = jnp.where(hit, source[at : at + 1, h * L : h * L + L], tile)
    return tile


def spread(tile, lane):
    return pick_lanes(tile, jnp.full((BZ, L), lane, I32))


def plane_row(layer, h, c):
    return ((layer * 2 + h) * NC + c) * BZ


def xsend_kernel(shape, even, odd, boxes, slots, old_rates, core, link, rates):
    gx, _, _ = place_of(shape)
    first = gx % 2 == 0
    kept, found = stays(slots), arrivals(even, odd)
    lane = lanes()
    together = jnp.zeros((BZ, L), F32)
    for c in range(NC):
        tile = jnp.zeros((BZ, L), F32)
        for s in range(BZ):
            tile = jnp.where(kept[s], old_rates[s * NC + c : s * NC + c + 1, :], tile)
        for parcel, k, hit in found:
            line = jnp.broadcast_to(parcel[AHEAD + k : AHEAD + k + 1, :L], (BZ, L))
            tile = jnp.where(hit, spread(line, c), tile)
        rates[c * BZ : c * BZ + BZ, :] = tile
        together = jnp.where(lane == c, tile, together)
        for layer in range(2):
            for h in range(2):
                sides = [merged(found, stayed_tile(kept, boxes, c, x, h), c, x, h) for x in (layer, E - 1 - layer)]
                at = plane_row(layer, h, c)
                core[at : at + BZ, :] = jnp.where(first, sides[1], sides[0])
                link[at : at + BZ, :] = jnp.where(first, sides[0], sides[1])
    core[FACE:, :] = together
    link[FACE:, :] = together


def merge_kernel(shape, even, odd, even_rest, odd_rest, moved, out, near, far):
    _, gy, _ = place_of(shape)
    first = gy % 2 == 0
    found = arrivals(even, odd)
    lane = lanes()
    for c in range(NC):
        low = [[None, None], [None, None]]
        high = [[None, None], [None, None]]
        for x in range(E):
            row = (c * E + x) * BZ
            at = L // 8 * (x % 8)
            here = lane // E == x % 8
            half = x // 8
            for h in range(2):
                tile = merged(found, moved[h, row : row + BZ, :], c, x, h, (even_rest, odd_rest))
                out[h, row : row + BZ, :] = tile
                for layer in range(2):
                    keep, start = ((low, E * layer) if h == 0 else (high, L - E - E * layer))
                    strip = rl(tile, at - start)
                    old = keep[layer][half]
                    keep[layer][half] = strip if old is None else jnp.where(here, strip, old)
        for layer in range(2):
            for h in range(2):
                at = plane_row(layer, h, c)
                near[at : at + BZ, :] = jnp.where(first, high[layer][h], low[layer][h])
                far[at : at + BZ, :] = jnp.where(first, low[layer][h], high[layer][h])


def ends(shape):
    gx, gy, _ = place_of(shape)
    x_first, y_first = gx % 2 == 0, gy % 2 == 0
    link_ok = jnp.where(x_first, gx > 0, gx < shape[0] - 1)
    far_ok = jnp.where(y_first, gy > 0, gy < shape[1] - 1)
    return x_first, y_first, link_ok, far_ok


def ysend_kernel(shape, link, core, rates, near, far, near_out, next_out, far_out):
    x_first, y_first, link_ok, _ = ends(shape)
    lane = lanes()
    near_out[: 2 * PLANE, :] = near[: 2 * PLANE, :]
    next_out[...] = near[2 * PLANE :, :]
    far_out[:FACE, :] = far[...]
    bottoms = [jnp.zeros((BZ, L), F32)] * 2
    tops = [jnp.zeros((BZ, L), F32)] * 2
    for c in range(NC):
        lines = []
        for h in range(2):
            at = plane_row(0, h, c)
            a = core[at : at + BZ, :]
            b = jnp.where(link_ok, link[at : at + BZ, :], 0.0)
            lines.append((jnp.where(x_first, b, a), jnp.where(x_first, a, b)))
        i, at = divmod(c, 4)
        at *= 2 * E
        low = (lane >= at) & (lane < at + E)
        high = (lane >= at + E) & (lane < at + 2 * E)
        bottoms[i] = jnp.where(low, rl(lines[0][0], at), jnp.where(high, rl(lines[0][1], at + E), bottoms[i]))
        tops[i] = jnp.where(low, rl(lines[1][0], at + E), jnp.where(high, rl(lines[1][1], at + 2 * E), tops[i]))
        rate = rates[c * BZ : c * BZ + BZ, :]
        bottoms[1] = jnp.where(lane == L // 2 + c, rate, bottoms[1])
        tops[1] = jnp.where(lane == L // 2 + c, rate, tops[1])
    for i in range(2):
        at = FACE + i * BZ
        near_out[at - 2 * PLANE : at - 2 * PLANE + BZ, :] = jnp.where(y_first, tops[i], bottoms[i])
        far_out[at : at + BZ, :] = jnp.where(y_first, bottoms[i], tops[i])


def extra_at(ref, c, start=FACE):
    i, at = divmod(c, 4)
    return rl(ref[start + i * BZ : start + i * BZ + BZ, :], -2 * E * at)


def y_rate(ref, c):
    return spread(ref[ref.shape[0] - BZ :, :], L // 2 + c)


def z_parts(x, lane, sub, swap):
    z = lane % E
    down = jnp.where(sub == 0, 0.0, rs(x, 1))
    up = jnp.where(sub == BZ - 1, 0.0, rs(x, -1))
    ends_ = pick_lanes(jnp.where(z == E - 1, down, up), swap)
    return jnp.where(z == 0, ends_, rl(x, 1)) + jnp.where(z == E - 1, ends_, rl(x, -1))


def swap_index(lane):
    z = lane % E
    return jnp.where(z == 0, lane + E - 1, jnp.where(z == E - 1, lane - E + 1, lane))


def inner(pair, lane, sub, swap):
    a, b = pair
    a1, b1, a2, b2 = rl(a, E), rl(b, E), rl(a, -E), rl(b, -E)
    low, high = lane < E, lane >= L - E
    first = jnp.where(low, 0.0, a1) + jnp.where(high, b2, a2) + z_parts(a, lane, sub, swap)
    second = jnp.where(low, a1, b1) + jnp.where(high, 0.0, b2) + z_parts(b, lane, sub, swap)
    return first, second


def pair_at(ref, layer, c):
    return tuple(ref[plane_row(layer, h, c) : plane_row(layer, h, c) + BZ, :] for h in range(2))


def tile_at(ref, c, x):
    row = (c * E + x) * BZ
    return tuple(ref[h, row : row + BZ, :] for h in range(2))


def z_differences(tiles, sub, upper):
    down = [jnp.where(sub == 0, 0.0, t) for t in [rs(t, 1) for t in tiles]]
    up = [jnp.where(sub == BZ - 1, 0.0, t) for t in [rs(t, -1) for t in tiles]]
    high = [rl(t, 1 - E) for t in [jnp.where(upper, t, d) for t, d in zip(tiles, down)]]
    return [jnp.where(upper, u - g, g - t) for g, u, t in zip(high, up, tiles)]


def sweep_kernel(shape, moved, rates, link, core, core_sent, link_sent, out, core_first, link_first, tops):
    x_first, _, link_ok, _ = ends(shape)
    _, gy, _ = place_of(shape)
    lane, sub = lanes(), subs()
    swap = swap_index(lane)
    upper = sub % 2 == 1
    z = lane % E
    for c in range(NC):
        rate = rates[c * BZ : c * BZ + BZ, :]
        scale = 1.0 / (1.0 + 6.0 * rate)
        ghost = []
        for got, sent, kept, ok in ((core, core_sent, core_first, None), (link, link_sent, link_first, link_ok)):
            g0, g1, own = pair_at(got, 0, c), pair_at(got, 1, c), pair_at(sent, 0, c)
            g_rate = spread(got[FACE:, :], c)
            if ok is not None:
                g0, g1 = (tuple(jnp.where(ok, t, 0.0) for t in g) for g in (g0, g1))
                g_rate = jnp.where(ok, g_rate, 0.0)
            kept[2 * PLANE + c * BZ : 2 * PLANE + c * BZ + BZ, :] = g_rate
            ghost.append(g0)
            g_scale = 1.0 / (1.0 + 6.0 * g_rate)
            sums = inner(g0, lane, sub, swap)
            for h in range(2):
                value = (g0[h] + g_rate * (sums[h] + g1[h] + own[h])) * g_scale
                if ok is not None:
                    value = jnp.where(ok, value, 0.0)
                row = (h * NC + c) * BZ
                kept[row : row + BZ, :] = value
        low = [jnp.where(x_first, b, a) for a, b in zip(*ghost)]
        high = [jnp.where(x_first, a, b) for a, b in zip(*ghost)]
        for x in range(E):
            here = tile_at(moved, c, x)
            before = low if x == 0 else tile_at(moved, c, x - 1)
            after = high if x == E - 1 else tile_at(moved, c, x + 1)
            sums = inner(here, lane, sub, swap)
            row = (c * E + x) * BZ
            for h in range(2):
                out[h, row : row + BZ, :] = (here[h] + rate * (sums[h] + before[h] + after[h])) * scale
    every = [(h, c, k) for c in range(NC) for h in range(2) for k in range(E // 2)]
    d = []
    for h, c, k in every:
        row = (c * E + 2 * k) * BZ
        d.append(out[h, row : row + BZ, :] + out[h, row + BZ : row + 2 * BZ, :])
    d = z_differences(d, sub, upper)
    d = [t + r for t, r in zip(d, [rl(t, -E) for t in d])]
    d = [rl(t, k) for t, (_, _, k) in zip(d, every)]
    faces = {}
    for t, (h, c, k) in zip(d, every):
        faces[h, c] = t if k == 0 else jnp.where(z == k, t, faces[h, c])
    y8 = lane % 8
    source = (y8 % 4) * (2 * E) + lane // E
    picked = {key: pick_lanes(t, source) for key, t in faces.items()}
    for c in range(NC):
        top = jnp.where(y8 < 4, picked[0, c], picked[1, c])
        tops[c * BZ : c * BZ + BZ, :] = jnp.where(z // 8 == gy % 2, top, 0.0)


def coarse_plane(pair, parity, lane, sub):
    sums = []
    for t in pair:
        t = t + rl(t, -1)
        sums.append(t + rl(t, -E))
    source = (lane // E % 4) * (2 * E) + 2 * (lane % 8)
    out = jnp.where(lane < L // 2, pick_lanes(sums[0], source), pick_lanes(sums[1], source))
    return jnp.where(lane % E // 8 == sub % 2, 0.25 * out, 0.0)


def strips(low, high, x, low_lane, high_lane):
    shift = E * (x % 8)
    return (
        jnp.where(low_lane, rl(low[x // 8], -shift), 0.0),
        jnp.where(high_lane, rl(high[x // 8], L - E - shift), 0.0),
    )


def corner(extra, low_lane, high_lane):
    return jnp.where(low_lane, extra, 0.0), jnp.where(high_lane, rl(extra, L - 2 * E), 0.0)


def y_ghosts(got, ok, c):
    g0, g1, extra = pair_at(got, 0, c), pair_at(got, 1, c), extra_at(got, c)
    if ok is not None:
        g0, g1 = (tuple(jnp.where(ok, t, 0.0) for t in g) for g in (g0, g1))
        extra = jnp.where(ok, extra, 0.0)
    return g0, g1, extra


def near_ghosts(got, following, c):
    second = None if following is None else pair_at(following, 0, c)
    return pair_at(got, 0, c), second, extra_at(got, c, 2 * PLANE)


def y_first_sweep(got, sent, ok, ghost, c, lane, sub, swap):
    g0, g1, extra = ghost
    own = pair_at(sent, 0, c)
    g_rate = y_rate(got, c)
    if ok is not None:
        g_rate = jnp.where(ok, g_rate, 0.0)
    g_scale = 1.0 / (1.0 + 6.0 * g_rate)
    sums, line = inner(g0, lane, sub, swap), corner(extra, lane < E, lane >= L - E)
    values = [(g0[h] + g_rate * (sums[h] + line[h] + g1[h] + own[h])) * g_scale for h in range(2)]
    return values if ok is None else [jnp.where(ok, t, 0.0) for t in values]


def x_first_sweep(part, ok, at_low, low_line, high_line, c, low_lane, high_lane):
    g_rate = part[2 * PLANE + c * BZ : 2 * PLANE + c * BZ + BZ, :]
    g_weight = g_rate / (1.0 + 6.0 * g_rate)
    bottom = jnp.where(at_low, low_line, rl(low_line, -E))
    top = jnp.where(at_low, rl(high_line, L - E), rl(high_line, L - 2 * E))
    values = []
    for h, (line, there) in enumerate(((bottom, low_lane), (top, high_lane))):
        row = (h * NC + c) * BZ
        values.append(part[row : row + BZ, :] + g_weight * jnp.where(there, line, 0.0))
    return values if ok is None else [jnp.where(ok, t, 0.0) for t in values]


def flux_kernel(
    shape, partial, moved_rates, masks, tops, link_first, far, near, far_sent, own_far, y_far, kept, to_row, to_column, to_both
):
    x_first, y_first, link_ok, far_ok = ends(shape)
    gx, gy, _ = place_of(shape)
    par_x, par_y = gx % 2, gy % 2
    lane, sub = lanes(), subs()
    swap = swap_index(lane)
    upper = sub % 2 == 1
    z = lane % E
    low_lane, high_lane = lane < E, lane >= L - E
    each = range(NC)
    rate = [moved_rates[c * BZ : c * BZ + BZ, :] for c in each]
    scale = [1.0 / (1.0 + 6.0 * r) for r in rate]
    weight = [r * q for r, q in zip(rate, scale)]
    near_g = [near_ghosts(near, None, c) for c in each]
    far_g = [y_ghosts(far, far_ok, c) for c in each]
    far_f = []
    for c in each:
        values = y_first_sweep(far, far_sent, far_ok, far_g[c], c, lane, sub, swap)
        for h in range(2):
            row = (h * NC + c) * BZ
            y_far[row : row + BZ, :] = values[h]
        far_f.append(values)
    far_r = [g[0] for g in far_g]

    def by_side(which, c):
        a, b = near_g[c][which], far_g[c][which]
        if which == 2:
            return jnp.where(y_first, b, a), jnp.where(y_first, a, b)
        return [jnp.where(y_first, q, p) for p, q in zip(a, b)], [jnp.where(y_first, p, q) for p, q in zip(a, b)]

    faces_y = []
    for c in each:
        own = pair_at(own_far, 0, c)
        flux = [far_f[c][h] - own[h] - weight[c] * far_r[c][h] for h in range(2)]
        face = coarse_plane(flux, par_x, lane, sub) * (rate[c] * masks[BZ : 2 * BZ, :])
        faces_y.append(face + rs(face, 1))
    faces_x = []
    for c in each:
        ghost = x_first_sweep(link_first, link_ok, x_first, *by_side(2, c), c, low_lane, high_lane)
        low_r, high_r = by_side(0, c)
        at_0, at_15 = (strips(low_r, high_r, x, low_lane, high_lane) for x in (0, E - 1))
        cells_0, cells_15 = tile_at(partial, c, 0), tile_at(partial, c, E - 1)
        flux = []
        for h in range(2):
            cell = jnp.where(x_first, cells_0[h], cells_15[h])
            cell = cell + weight[c] * jnp.where(x_first, at_0[h], at_15[h])
            flux.append(ghost[h] - cell)
        face = coarse_plane(flux, par_y, lane, sub) * (rate[c] * masks[0:BZ, :])
        faces_x.append(face + rs(face, -1))
    faces_z = []
    source = (lane // E % 4) * (2 * E) + jnp.where(lane % 8 == 7, 7, 0)
    d = []
    for c in each:
        for side in by_side(0, c):
            d += [weight[c] * t for t in side]
    d = [t + r for t, r in zip(d, [rl(t, -E) for t in d])]
    d = z_differences(d, sub, upper)
    halves = []
    for c in each:
        for h in range(2):
            halves.append(jnp.where(z == 7, rl(d[4 * c + 2 + h], 7), d[4 * c + h]))
    halves = [pick_lanes(t, source) for t in halves]
    for c in each:
        add = jnp.where(lane < L // 2, halves[2 * c], halves[2 * c + 1])
        add = jnp.where((z == 8 * par_y) | (z == 8 * par_y + 7), add, 0.0)
        faces_z.append((tops[c * BZ : c * BZ + BZ, :] + add) * (0.25 * rate[c] * masks[2 * BZ :, :]))
    left = sub % 4 < 2
    top = sub < 4
    own_tiles, other_tiles = [], []
    for c in each:
        outer = jnp.where(upper, faces_y[c], faces_x[c])
        columns = (jnp.where(left, outer, rs(faces_z[c], 2)), jnp.where(left, rs(outer, -2), faces_z[c]))
        own_tiles.append(jnp.where(y_first, columns[0], columns[1]))
        other_tiles.append(jnp.where(y_first, columns[1], columns[0]))
    for tiles, same, other in ((own_tiles, kept, to_row), (other_tiles, to_column, to_both)):
        turned = [rs(t, 4) for t in tiles]
        for i in range(0, NC, 2):
            j = min(i + 1, NC - 1)
            low, high = jnp.where(top, tiles[i], turned[j]), jnp.where(top, turned[i], tiles[j])
            row = i // 2 * BZ
            same[row : row + BZ, :] = jnp.where(x_first, low, high)
            other[row : row + BZ, :] = jnp.where(x_first, high, low)


def register_kernel(shape, kept, by_both, by_column, by_row, _, out):
    x_first, y_first, _, _ = ends(shape)
    sub = subs()
    for c in range(NC):
        at = c // 2 * BZ
        m, m4, g, g4 = (rs(ref[at : at + BZ, :], 4 * (c % 2)) for ref in (kept, by_column, by_row, by_both))
        for h in range(2):
            same_y, same_x = (y_first, x_first) if h == 0 else (~y_first, ~x_first)
            a, b = jnp.where(same_y, m, m4), jnp.where(same_y, g, g4)
            x0, x1 = jnp.where(x_first, a, b), jnp.where(x_first, b, a)
            t, t4 = jnp.where(same_x, m, g), jnp.where(same_x, m4, g4)
            y0, y1 = jnp.where(y_first, rs(t, 1), rs(t4, 1)), jnp.where(y_first, rs(t4, 2), rs(t, 2))
            rows = jnp.where(sub == 0, x0, jnp.where(sub == 1, rs(x1, 1), rs(t + t4, 2)))
            rows = jnp.where(sub == 2, y0, jnp.where(sub == 3, y1, rows))
            out[0, 0, c, :, h * L : h * L + L] = rows[:6]


def second_kernel(shape, moved, rates, partial, core_first, link_first, far_sent, out, own_far):
    x_first, _, _, _ = ends(shape)
    lane, sub = lanes(), subs()
    swap = swap_index(lane)
    for c in range(NC):
        rate = rates[c * BZ : c * BZ + BZ, :]
        scale = 1.0 / (1.0 + 6.0 * rate)
        own, own1 = pair_at(far_sent, 0, c), pair_at(far_sent, 1, c)
        sums, line = inner(own, lane, sub, swap), corner(extra_at(far_sent, c), lane < E, lane >= L - E)
        for h in range(2):
            row = (h * NC + c) * BZ
            own_far[row : row + BZ, :] = (own[h] + rate * (sums[h] + line[h] + own1[h])) * scale
        core, link = pair_at(core_first, 0, c), pair_at(link_first, 0, c)
        low = [jnp.where(x_first, b, a) for a, b in zip(core, link)]
        high = [jnp.where(x_first, a, b) for a, b in zip(core, link)]
        for x in range(E):
            here = tile_at(partial, c, x)
            before = low if x == 0 else tile_at(partial, c, x - 1)
            after = high if x == E - 1 else tile_at(partial, c, x + 1)
            sums = inner(here, lane, sub, swap)
            start = tile_at(moved, c, x)
            row = (c * E + x) * BZ
            for h in range(2):
                out[h, row : row + BZ, :] = start[h] + rate * (sums[h] + before[h] + after[h])


def smooth_kernel(
    shape, rates, partial, core_first, link_first, far, near, following, near_sent, y_far, out, done, planes, held, boxes, sem
):
    done[...] = jnp.zeros((BZ, L), F32)
    x_first, y_first, _, far_ok = ends(shape)
    lane, sub = lanes(), subs()
    swap = swap_index(lane)
    low_lane, high_lane = lane < E, lane >= L - E

    def by_side(a, b, a_first):
        low = [jnp.where(a_first, q, p) for p, q in zip(a, b)]
        high = [jnp.where(a_first, p, q) for p, q in zip(a, b)]
        return low, high

    for c in range(NC):
        rate = rates[c * BZ : c * BZ + BZ, :]
        weight = rate / (1.0 + 6.0 * rate)
        near_g, far_g = near_ghosts(near, following, c), y_ghosts(far, far_ok, c)
        near_f = y_first_sweep(near, near_sent, None, near_g, c, lane, sub, swap)
        ghosts_f = by_side(near_f, pair_at(y_far, 0, c), y_first)
        ghosts_r = by_side(near_g[0], far_g[0], y_first)
        lines = by_side(near_g[2:], far_g[2:], y_first)
        x_rates = [ref[2 * PLANE + c * BZ : 2 * PLANE + c * BZ + BZ, :] for ref in (core_first, link_first)]
        x_weights = [t / (1.0 + 6.0 * t) for t in x_rates]
        (low_w,), (high_w,) = by_side(x_weights[:1], x_weights[1:], x_first)
        for side in range(2):
            added = [weight * t for t in ghosts_r[side]]
            (line,) = lines[side]
            sums = inner(added, lane, sub, swap)
            ends_ = (jnp.where(low_lane, low_w * line, 0.0), jnp.where(high_lane, high_w * rl(line, L - 2 * E), 0.0))
            for h in range(2):
                row = ((side * 2 + h) * NC + c) * BZ
                planes[0, row : row + BZ, :] = rate * (sums[h] + ends_[h] + ghosts_f[side][h])
                planes[1, row : row + BZ, :] = rate * added[h]
    next_low = (lane >= E) & (lane < 2 * E)
    next_high = (lane >= L - 2 * E) & (lane < L - E)
    copies = []
    for c in range(NC):
        rate = rates[c * BZ : c * BZ + BZ, :]
        scale = 1.0 / (1.0 + 6.0 * rate)
        for x in range(E):
            row = (c * E + x) * BZ
            shift = E * (x % 8)
            for h, (here, there, at) in enumerate(((low_lane, next_low, 0), (high_lane, next_high, L - E))):
                plane = ((h * 2 + x // 8) * NC + c) * BZ
                first = rl(planes[0, plane : plane + BZ, :], at - shift)
                second = rl(planes[1, plane : plane + BZ, :], (at - E if h else E) - shift)
                add = jnp.where(here, first, jnp.where(there, second, 0.0))
                held[h, row : row + BZ, :] = (partial[h, row : row + BZ, :] + add) * scale
        for s in range(BZ):
            for h in range(2):
                boxes[c, s, :, h * L : h * L + L] = held[h, pl.ds(c * E * BZ + s, E, stride=BZ), :]
        copies.append(pltpu.make_async_copy(boxes.at[c], out.at[0, 0, :, c], sem.at[c]))
        copies[-1].start()
    for copy in copies:
        copy.wait()


def body(shape, fields_old, coeff_old, new_place, cf_mask):
    rows, columns = shape
    count = rows * columns
    both = ("gx", "gy")

    def swap(array, pairs):
        return lax.ppermute(array, both, pairs)

    even_pairs = [(i, i ^ 1) for i in range(count)]
    odd_pairs = [(i, (i + 1) % count if i % 2 else (i - 1) % count) for i in range(count)]
    at = lambda a, b: a * columns + b
    core_pairs = [(at(a, b), at(a ^ 1, b)) for a in range(rows) for b in range(columns)]
    both_pairs = [(at(a, b), at(a ^ 1, b ^ 1)) for a in range(rows) for b in range(columns)]
    link_pairs = [
        (at(a, b), at(a, b ^ 2) if a in (0, rows - 1) else at(a + 1 if a % 2 else a - 1, b))
        for a in range(rows)
        for b in range(columns)
    ]
    far_pairs = [
        (at(a, b), at(a ^ 1, b) if b in (0, columns - 1) else at(a, b + 1 if b % 2 else b - 1))
        for a in range(rows)
        for b in range(columns)
    ]
    k = lambda f: functools.partial(f, shape)
    coeff_old = coeff_old.transpose(0, 3, 1, 2)
    cf_mask = cf_mask.transpose(0, 2, 1, 3)
    big = (2, NC * E * BZ, L)

    plane = ((2 * PLANE, L), "vmem")
    even, odd, even_rest, odd_rest, boxes, slots, rates, masks = call(
        k(pack_kernel),
        [(a, "hbm") for a in (new_place, coeff_old, cf_mask, fields_old)],
        [
            ((PARCEL, 2 * L), "vmem"),
            ((PARCEL, 2 * L), "vmem"),
            ((REST, 2 * L), "vmem"),
            ((REST, 2 * L), "vmem"),
            ((BZ, NC, E, 2 * L), "vmem"),
            ((BZ, L), "vmem"),
            ((PLANE, L), "vmem"),
            ((3 * BZ, L), "vmem"),
        ],
        [
            SM((1, 1, BZ), I32),
            SM((1, NC, 1, BZ), F32),
            SM((1, 3, 1, BZ), I32),
            pltpu.SemaphoreType.DMA((4,)),
        ],
    )
    even_got = swap(even, even_pairs)
    odd_got = swap(odd, odd_pairs)
    even_rest_got = swap(even_rest, even_pairs)
    odd_rest_got = swap(odd_rest, odd_pairs)
    core, link, rates = call(
        k(xsend_kernel),
        [(a, "vmem") for a in (even_got, odd_got, boxes, slots, rates)],
        [((XFACE, L), "vmem"), ((XFACE, L), "vmem"), ((PLANE, L), "vmem")],
    )
    (stayed,) = call(k(stay_kernel), [(boxes, "vmem"), (slots, "vmem")], [(big, "vmem")])
    core_got = swap(core, core_pairs)
    link_got = swap(link, link_pairs)
    moved, near, far = call(
        k(merge_kernel),
        [(a, "vmem") for a in (even_got, odd_got, even_rest_got, odd_rest_got, stayed)],
        [(big, "vmem"), ((FACE, L), "vmem"), ((FACE, L), "vmem")],
    )
    near, following, far = call(
        k(ysend_kernel),
        [(a, "vmem") for a in (link_got, core_got, rates, near, far)],
        [((YNEAR, L), "vmem"), ((2 * PLANE, L), "vmem"), ((YFACE, L), "vmem")],
    )
    near_got = swap(near, even_pairs)
    far_got = swap(far, far_pairs)
    next_got = swap(following, even_pairs)
    part, core_first, link_first, tops = call(
        k(sweep_kernel),
        [(a, "vmem") for a in (moved, rates, link_got, core_got, core, link)],
        [(big, "vmem"), ((3 * PLANE, L), "vmem"), ((3 * PLANE, L), "vmem"), ((PLANE, L), "vmem")],
    )
    second, own_far = call(
        k(second_kernel),
        [(a, "vmem") for a in (moved, rates, part, core_first, link_first, far)],
        [(big, "vmem"), plane],
    )
    y_far, kept, to_row, to_column, to_both = call(
        k(flux_kernel),
        [(a, "vmem") for a in (part, rates, masks, tops, link_first, far_got, near_got, far, own_far)],
        [plane] + [(((NC + 1) // 2 * BZ, L), "vmem")] * 4,
    )
    by_both = swap(to_both, both_pairs)
    by_column = swap(to_column, even_pairs)
    by_row = swap(to_row, core_pairs)
    smoothed, done = call(
        k(smooth_kernel),
        [(a, "vmem") for a in (rates, second, core_first, link_first, far_got, near_got, next_got, near, y_far)],
        [((1, 1, BZ, NC, E, 2 * L), "hbm"), ((BZ, L), "vmem")],
        [
            VM((2, 4 * PLANE, L), F32),
            VM((2, NC * E * BZ + BZ, L), F32),
            VM((NC, BZ, E, 2 * L), F32),
            pltpu.SemaphoreType.DMA((NC,)),
        ],
    )
    (registers,) = call(
        k(register_kernel),
        [(a, "vmem") for a in (kept, by_both, by_column, by_row, done)],
        [((1, 1, NC, 6, 2 * L), "out")],
    )
    return smoothed, registers


def solution(mesh):
    shape = (mesh.shape["gx"], mesh.shape["gy"])
    return jax.shard_map(
        functools.partial(body, shape),
        mesh=mesh,
        in_specs=(
            P("gx", "gy", None, None, None, None),
            P("gx", "gy", None, None),
            P("gx", "gy", None),
            P("gx", "gy", None, None),
        ),
        out_specs=(P("gx", "gy", None, None, None, None), P("gx", "gy", None, None, None)),
        check_vma=False,
    )
```
